512 devices in a mesh: seq: 16 (over x_hi, z), head: 8 (over y), cand: 4 (over x_lo, core).
Axes of the slice: x: 4 (x_hi: 2, x_lo: 2; x = x_hi * 2 + x_lo), y: 8, z: 8, core: 2. Of those that a mesh axis runs over, the one named last changes fastest.
Arguments:
- hidden: bfloat16 [256, 16384], P('cand', 'seq'), may hold values from -6 to 6
- query_weight: bfloat16 [16384, 2048], P('seq', 'head'), may hold values from -0.046875 to 0.046875
- key_weight: bfloat16 [16384, 128], P('seq'), may hold values from -0.375 to 0.375
- value_weight: bfloat16 [16384, 128], P('seq'), may hold values from -0.046875 to 0.046875
- out_weight: bfloat16 [2048, 16384], P('head', 'seq'), may hold values from -0.125 to 0.125
- key_cache: bfloat16 [131072, 128], P(('seq', 'cand')), may hold values from -60 to 60
- value_cache: bfloat16 [131072, 128], P(('seq', 'cand')), may hold values from -6 to 6
- cand_group: int32 [32], replicated, may hold values from 0 to 7
Outputs:
- attn_out: bfloat16 [256, 16384], P('cand', ('seq', 'head'))
The draws below stay inside these ranges and needn't reach their ends.
Inputs may be any that keep to these rules, and one draw needn't show every extreme that they name: `cand_group`: each candidate's question.
All inputs are finite; a program needn't handle non-finite values.
Results may differ from the reference program's by a relative error of at most 0.02.
Values may be sent and summed in bfloat16 or wider, within the bound.
No kernel may reach another device: no remote copies, remote signals or barrier semaphores. Data moves between devices by JAX's collectives and lax.ppermute only.
A program may use at most 64 MiB of HBM per device.

```python
import math
import jax
import jax.numpy as jnp
from jax import lax

D = 16384
HD = 128
HEADS = 16
GROUPS = 8
ANS_LEN = 8
CANDS = 32
TOKENS = 256
PREFIX = 131072


def draw_key_cache(key, part):
    key = jax.random.fold_in(key, 11)
    first = jax.random.fold_in(key, 0)
    return (3.0 * jax.random.truncated_normal(first, -5.0, 5.0, (PREFIX, HD), jnp.float32)).astype(jnp.bfloat16)


def with_ends(drawn, key, low, high):
    shape = drawn.shape
    place = [jax.random.randint(jax.random.fold_in(key, axis), (), 0, shape[axis]) for axis in range(len(shape))]
    drawn = drawn.at[tuple(place)].set(low)
    longest = shape.index(max(shape))
    place[longest] = (place[longest] + 1) % shape[longest]
    return drawn.at[tuple(place)].set(high)


def block_levels(own_key, shape, cuts, smallest, largest):
    gain, own = 1.0, jax.random.fold_in(own_key, 6)
    for axis_at, shards_of in cuts:
        draws = jnp.exp(jax.random.uniform(jax.random.fold_in(own, axis_at), (shards_of,), jnp.float32, smallest / len(cuts), largest / len(cuts)))
        gain = gain * jnp.repeat(draws, shape[axis_at] // shards_of).reshape([-1 if axis == axis_at else 1 for axis in range(len(shape))])
    return gain


def centred(key, extent, scale, limit, cuts=(), kind=jnp.bfloat16):
    values = jax.random.normal(key, extent, jnp.float32) * scale
    if len(cuts) > 0:
        values = block_levels(key, extent, cuts, -0.22, 0.18) * values
    return jnp.clip(values, min=-limit, max=limit).astype(kind)


def setup_inputs(seed: int = 0) -> dict:
    key_of = jax.random.split(jax.random.key(seed), 9)
    hidden = centred(key_of[0], (TOKENS, D), 1.0, 6.0, ((0, 4), (1, 16)))
    query_weight = centred(key_of[1], (D, HEADS * HD), D ** -0.5, 0.046875, ((0, 16), (1, 8)))
    key_weight = centred(key_of[2], (D, HD), (8.0 * D ** -0.5), 0.375, ((0, 16),))
    value_weight = centred(key_of[3], (D, HD), D ** -0.5, 0.046875, ((0, 16),))
    out_weight = centred(key_of[4], (HEADS * HD, D), (HEADS * HD) ** -0.5, 0.125, ((0, 8), (1, 16)))
    key_cache = draw_key_cache(jax.random.fold_in(key_of[8], 71), 0)
    value_cache = centred(key_of[6], (PREFIX, HD), 1.0, 6.0, ((0, 64),))
    cand_group = with_ends(jax.random.randint(key_of[7], (CANDS,), 0, GROUPS), jax.random.fold_in(key_of[7], 1), 0, GROUPS - 1).astype(jnp.int32)
    return dict(hidden=hidden, query_weight=query_weight, key_weight=key_weight, value_weight=value_weight, out_weight=out_weight, key_cache=key_cache, value_cache=value_cache, cand_group=cand_group)


NEGATIVE = -1.0e30


def rounded_float(weights):
    return lax.optimization_barrier(weights.astype(jnp.bfloat16)).astype(jnp.float32)


def reference(hidden, query_weight, key_weight, value_weight, out_weight, key_cache, value_cache, cand_group):
    scale = HD ** -0.5
    queries = jnp.dot(hidden, query_weight, preferred_element_type=jnp.float32).astype(jnp.bfloat16)
    keys = jnp.dot(hidden, key_weight, preferred_element_type=jnp.float32).astype(jnp.bfloat16)
    values = jnp.dot(hidden, value_weight, preferred_element_type=jnp.float32).astype(jnp.bfloat16)
    query_three = queries.reshape(TOKENS, HEADS, HD).astype(jnp.float32)
    limits = (jnp.repeat(cand_group, ANS_LEN) + 1) * (PREFIX // GROUPS)
    width = math.gcd(PREFIX, 4096)
    count = PREFIX // width
    key_blocks = key_cache.reshape(count, width, HD)
    value_blocks = value_cache.reshape(count, width, HD)
    starts = jnp.arange(count, dtype=jnp.int32) * width

    def update(carry, block):
        top, total, acc = carry
        key_block, value_block, start = block
        scores = jnp.einsum("thd,kd->thk", query_three, key_block.astype(jnp.float32)) * scale
        places = start + jnp.arange(width, dtype=jnp.int32)
        visible = (places[None, :] < limits[:, None])[:, None, :]
        scores = jnp.where(visible, scores, NEGATIVE)
        new_top = jnp.maximum(top, jnp.max(scores, axis=2))
        weights = jnp.where(visible, jnp.exp(scores - new_top[..., None]), 0.0)
        shrink = jnp.exp(top - new_top)
        total = total * shrink + jnp.sum(weights, axis=2)
        acc = acc * shrink[..., None] + jnp.einsum("thk,kd->thd", rounded_float(weights), value_block.astype(jnp.float32))
        return (new_top, total, acc), None

    start_state = (jnp.full((TOKENS, HEADS), NEGATIVE, jnp.float32), jnp.zeros((TOKENS, HEADS), jnp.float32), jnp.zeros((TOKENS, HEADS, HD), jnp.float32))
    (top, total, acc), _ = lax.scan(update, start_state, (key_blocks, value_blocks, starts))

    query_four = query_three.reshape(CANDS, ANS_LEN, HEADS, HD)
    key_four = keys.reshape(CANDS, ANS_LEN, HD).astype(jnp.float32)
    value_four = values.reshape(CANDS, ANS_LEN, HD).astype(jnp.float32)
    own = jnp.einsum("cthd,cud->cthu", query_four, key_four) * scale
    causal = (jnp.arange(ANS_LEN)[None, :] <= jnp.arange(ANS_LEN)[:, None])[None, :, None, :]
    own = jnp.where(causal, own, NEGATIVE)
    own_top = jnp.max(own, axis=3)
    own_weights = jnp.where(causal, jnp.exp(own - own_top[..., None]), 0.0)
    own_total = jnp.sum(own_weights, axis=3).reshape(TOKENS, HEADS)
    own_acc = jnp.einsum("cthu,cud->cthd", rounded_float(own_weights), value_four).reshape(TOKENS, HEADS, HD)
    own_top = own_top.reshape(TOKENS, HEADS)
    best = jnp.maximum(top, own_top)
    first = jnp.exp(top - best)
    second = jnp.exp(own_top - best)
    denominator = total * first + own_total * second
    numerator = acc * first[..., None] + own_acc * second[..., None]
    attention = (numerator / denominator[..., None]).astype(jnp.bfloat16).reshape(TOKENS, HEADS * HD)
    return jnp.dot(attention, out_weight, preferred_element_type=jnp.float32).astype(jnp.bfloat16)
```

```python
import math

import jax
import jax.numpy as jnp
from jax import lax
from jax.experimental import pallas as pl
from jax.experimental.pallas import tpu as pltpu
from jax.sharding import PartitionSpec as P

HD = 128
GROUPS = 8
ANS_LEN = 8
ROW_BLOCK = 128

NEGATIVE = -1e30
LOG2E = math.log2(math.e)
SMALL_SCALE = 16.0
KEY_SCALE = 2.0

VMEM = pl.BlockSpec(memory_space=pltpu.VMEM)
HBM = pl.BlockSpec(memory_space=pltpu.HBM)

SEQ = ("far", "pair", "side")
CAND = ("lo", "core")


def call(kernel, out_shape, in_specs, **cost):
    return pl.pallas_call(
        kernel,
        out_shape=out_shape,
        in_specs=in_specs,
        out_specs=jax.tree.map(lambda _: VMEM, out_shape),
        compiler_params=pltpu.CompilerParams(vmem_limit_bytes=40 * 1024 * 1024),
        cost_estimate=pl.CostEstimate(**cost),
    )


def dot(a, b):
    return jnp.dot(a, b, preferred_element_type=jnp.float32)


def dot_transposed(a, b):
    return lax.dot_general(a, b, (((1,), (1,)), ((), ())), preferred_element_type=jnp.float32)


def project_kernel(
    hidden_hbm, query_hbm, key_hbm, value_hbm, group_hbm, key_cache, value_cache,
    out_ref, bias_ref, cache_hbm, hidden_ref, weight_ref, group_smem, sems,
):
    far, pairs, side = (lax.axis_size(name) for name in SEQ)
    features = hidden_ref.shape[1]
    width = query_hbm.shape[1]
    halves = [pl.ds(i * (features // 2), features // 2) for i in range(2)]
    copies = []

    def start(source, target):
        copies.append(pltpu.make_async_copy(source, target, sems.at[len(copies)]))
        copies[-1].start()

    for half in halves:
        start(query_hbm.at[half, :], weight_ref.at[half, pl.ds(0, width)])
        start(hidden_hbm.at[:, half], hidden_ref.at[:, half])
        start(key_hbm.at[half, :], weight_ref.at[half, pl.ds(width, HD)])
        start(value_hbm.at[half, :], weight_ref.at[half, pl.ds(width + HD, HD)])
    start(group_hbm, group_smem)
    start(key_cache, cache_hbm.at[0])
    start(value_cache, cache_hbm.at[1])
    total = None
    for i, half in enumerate(halves):
        for copy in copies[4 * i : 4 * i + 4]:
            copy.wait()
        part = dot(hidden_ref[:, half], weight_ref[half, :])
        total = part if total is None else total + part
    ring = SMALL_SCALE * lax.axis_size("pair") * side
    tokens = total.shape[0]
    for h in range(side):
        for p in range(pairs):
            out_ref[p * side + h, :tokens] = total[:, h * HD : (h + 1) * HD] * ring
    for s, scale in ((0, ring * KEY_SCALE / SMALL_SCALE), (1, ring)):
        part = total[:, width + s * HD : width + (s + 1) * HD] * scale
        for p in range(pairs):
            for f in range(far):
                place = slice((f * pairs + p) * ANS_LEN, (f * pairs + p + 1) * ANS_LEN)
                out_ref[p * side + s, tokens + f * ANS_LEN : tokens + (f + 1) * ANS_LEN] = part[place]
    copies[-3].wait()
    chunk = lax.axis_index(SEQ) // (lax.axis_size(SEQ) // GROUPS)
    lane = lax.broadcasted_iota(jnp.int32, bias_ref.shape, 1)
    bias = jnp.zeros(bias_ref.shape, jnp.float32)
    for c in range(group_smem.shape[0]):
        hidden_by = jnp.where(group_smem[c] >= chunk, 0.0, NEGATIVE)
        bias = jnp.where(lane == c, hidden_by, bias)
    bias_ref[...] = bias
    copies[-2].wait()
    copies[-1].wait()


def reduce_kernel(part_ref, out_ref):
    total = jnp.sum(part_ref[...], axis=0) * (1 / part_ref.shape[0])
    out_ref[...] = jnp.broadcast_to(total[None], out_ref.shape)


def packed(mean, level):
    high = level.astype(jnp.bfloat16).astype(jnp.float32)
    middle = (level - high).astype(jnp.bfloat16).astype(jnp.float32)
    row = lax.broadcasted_iota(jnp.int32, mean.shape, 0)
    lane = lax.broadcasted_iota(jnp.int32, mean.shape, 1)
    line = lax.broadcasted_iota(jnp.int32, (ANS_LEN, HD), 0)
    lines = jnp.zeros((ANS_LEN, HD), jnp.float32)
    for place, term in enumerate((high, middle, level - high - middle)):
        spread = jnp.sum(jnp.where(lane == row, term, 0.0), axis=0, keepdims=True)
        lines = jnp.where(line == place, spread, lines)
    return jnp.concatenate([mean, lines], axis=0).astype(jnp.bfloat16)


def unpacked(state):
    state = state.astype(jnp.float32)
    rows = state.shape[-2] - ANS_LEN
    mean = state[..., :rows, :]
    line = jnp.sum(state[..., rows:, :], axis=-2, keepdims=True)
    row = lax.broadcasted_iota(jnp.int32, mean.shape, mean.ndim - 2)
    lane = lax.broadcasted_iota(jnp.int32, mean.shape, mean.ndim - 1)
    return mean, jnp.sum(jnp.where(lane == row, line, 0.0), axis=-1, keepdims=True)


def merged(mean, level):
    best = jnp.max(level, axis=0)
    factor = jnp.exp(level - best[None])
    total = jnp.sum(factor, axis=0)
    return jnp.sum(mean * factor, axis=0) / total, best + jnp.log(total)


def attend_kernel(query_ref, cache_ref, other_ref, bias_ref, out_ref):
    scale = HD ** (-0.5)
    far, side, lo, rows, _ = out_ref.shape
    rows -= ANS_LEN
    halves = far
    sources = ROW_BLOCK // rows * halves
    cores = lax.axis_size("core")
    cands = rows // ANS_LEN
    row = lax.broadcasted_iota(jnp.int32, (ROW_BLOCK, HD), 0)
    lane = lax.broadcasted_iota(jnp.int32, (ROW_BLOCK, HD), 1)
    caches = (cache_ref, other_ref)
    steps = [(r, cache) for r in range(query_ref.shape[0] // sources) for cache in caches]

    def scored(step):
        r, cache = step
        parts = query_ref[r * sources : (r + 1) * sources, :rows]
        query = jnp.sum(parts.reshape(-1, halves, rows, HD), axis=1).reshape(ROW_BLOCK, HD)
        query = (query * (1 / SMALL_SCALE)).astype(jnp.bfloat16)
        return dot_transposed(query, cache[0])

    ahead = scored(steps[0])
    held = []
    for i, (r, cache) in enumerate(steps):
        scores = ahead
        if i + 1 < len(steps):
            ahead = scored(steps[i + 1])
        top = jnp.max(scores, axis=1, keepdims=True)
        weights = jnp.exp2((scores - top) * (scale * LOG2E))
        total = jnp.sum(weights, axis=1, keepdims=True)
        held.append((top * scale, total, dot(weights.astype(jnp.bfloat16), cache[1])))
        if len(held) < len(caches):
            continue
        top = jnp.maximum(held[0][0], held[1][0])
        factors = [jnp.exp(part[0] - top) for part in held]
        total = held[0][1] * factors[0] + held[1][1] * factors[1]
        mean = (held[0][2] * factors[0] + held[1][2] * factors[1]) / total
        held = []
        place = (row + r * ROW_BLOCK) // ANS_LEN
        cand = place // cands % lo * cores + lax.axis_index("core")
        candidate = cand * cands + place % cands
        bias = jnp.sum(jnp.where(lane == candidate, bias_ref[0:1, :], 0.0), axis=1, keepdims=True)
        level = top + jnp.log(total) + bias
        for j in range(ROW_BLOCK // rows):
            part = slice(j * rows, (j + 1) * rows)
            state = packed(mean[part], level[part])
            block = r * (ROW_BLOCK // rows) + j
            for f in range(far):
                out_ref[f, block // lo, block % lo] = state


def merge_kernel(state_ref, own_ref, out_ref):
    mean, level = merged(*unpacked(state_ref[...]))
    halves, pairs, _ = (lax.axis_size(name) for name in SEQ)
    rows = pairs * ANS_LEN
    tokens = mean.shape[0]

    def own(s, part, scale):
        place = (s * lax.axis_size("lo") + lax.axis_index("lo")) * halves
        total = own_ref[place, part]
        for half in range(1, halves):
            total = total + own_ref[place + half, part]
        return (total * (1 / scale)).astype(jnp.bfloat16)

    query = own(lax.axis_index("side"), slice(0, tokens), SMALL_SCALE)
    key = own(0, slice(tokens, None), KEY_SCALE)
    value = own(1, slice(tokens, None), SMALL_SCALE)
    scores = dot_transposed(query, key) * HD ** (-0.5)
    row = lax.broadcasted_iota(jnp.int32, scores.shape, 0)
    column = lax.broadcasted_iota(jnp.int32, scores.shape, 1)
    shown = (row // rows == column // ANS_LEN) & (column % ANS_LEN <= row % ANS_LEN)
    scores = jnp.where(shown, scores, NEGATIVE)
    top = jnp.max(scores, axis=1, keepdims=True)
    weights = jnp.where(shown, jnp.exp(scores - top), 0.0)
    total = jnp.sum(weights, axis=1, keepdims=True)
    own_mean = dot(weights.astype(jnp.bfloat16), value) / total
    own_level = top + jnp.log(total)
    row = lax.broadcasted_iota(jnp.int32, level.shape, 0)
    mine = row // ANS_LEN % pairs == lax.axis_index("pair")
    own_level = jnp.where(mine, own_level, NEGATIVE)
    mean, level = merged(jnp.stack([mean, own_mean]), jnp.stack([level, own_level]))
    out_ref[...] = jnp.broadcast_to(packed(mean, level)[None], out_ref.shape)


def output_kernel(state_ref, weight_ref, out_ref):
    blocks, _, width = out_ref.shape
    columns = [merged(*unpacked(state_ref[s]))[0] for s in range(state_ref.shape[0])]
    attention = jnp.concatenate(columns, axis=1).astype(jnp.bfloat16)
    out = dot(attention, weight_ref[...])
    for block in range(blocks):
        out_ref[block] = out[:, block * width : (block + 1) * width].astype(jnp.bfloat16)


def sum_kernel(part_ref, out_ref):
    out_ref[...] = jnp.sum(part_ref[...].astype(jnp.float32), axis=0).astype(out_ref.dtype)


def body(
    hidden, query_weight, key_weight, value_weight, out_weight, key_cache, value_cache, cand_group
):
    tok_dev, feat_dev = hidden.shape
    heads_dev = query_weight.shape[1] // HD
    head, lo = lax.axis_size("head"), lax.axis_size("lo")
    far, pairs, side = (lax.axis_size(name) for name in SEQ)
    shard_len = key_cache.shape[0]
    bf16, f32 = jnp.bfloat16, jnp.float32
    rows = tok_dev * heads_dev * lo
    columns = out_weight.shape[1] // head

    inputs = (hidden, query_weight, key_weight, value_weight, cand_group, key_cache, value_cache)
    inputs = [pltpu.with_memory_space_constraint(x, pltpu.HBM) for x in inputs]
    partial, bias, cache = pl.pallas_call(
        project_kernel,
        out_shape=(
            jax.ShapeDtypeStruct((pairs * side, tok_dev + far * ANS_LEN, HD), f32),
            jax.ShapeDtypeStruct((ANS_LEN, HD), f32),
            jax.ShapeDtypeStruct((2, *key_cache.shape), bf16),
        ),
        in_specs=[HBM] * 7,
        out_specs=(VMEM, VMEM, HBM),
        scratch_shapes=[
            pltpu.VMEM(hidden.shape, bf16),
            pltpu.VMEM((feat_dev, (heads_dev + 2) * HD), bf16),
            pltpu.SMEM(cand_group.shape, jnp.int32),
            pltpu.SemaphoreType.DMA((11,)),
        ],
        compiler_params=pltpu.CompilerParams(vmem_limit_bytes=40 * 1024 * 1024),
        cost_estimate=pl.CostEstimate(
            flops=2 * tok_dev * feat_dev * (heads_dev + 2) * HD,
            bytes_accessed=2 * feat_dev * (tok_dev + (heads_dev + 2) * HD),
            transcendentals=0,
        ),
    )(*inputs)
    other = lax.ppermute(cache, "core", [(0, 1), (1, 0)])
    partial = lax.all_to_all(partial.astype(jnp.float16), ("pair", "side"), 0, 0, tiled=True)
    near = far * side * lo
    queries = call(
        reduce_kernel,
        jax.ShapeDtypeStruct((near, *partial.shape[1:]), f32),
        [VMEM],
        flops=partial.size,
        bytes_accessed=partial.size * 4,
        transcendentals=0,
    )(partial.astype(f32))
    queries = queries.astype(jnp.float16)
    queries = lax.all_to_all(queries, ("side", "lo", "far"), 0, 0, tiled=True).astype(f32)
    state = call(
        attend_kernel,
        jax.ShapeDtypeStruct((far, side, lo, tok_dev + ANS_LEN, HD), bf16),
        [VMEM] * 4,
        flops=8 * rows * shard_len * HD,
        bytes_accessed=8 * shard_len * HD,
        transcendentals=2 * rows * shard_len,
    )(queries, cache, other, bias)
    state = state.reshape(near, tok_dev + ANS_LEN, HD)
    state = lax.all_to_all(state, ("far", "side", "lo"), 0, 0, tiled=True)
    state = call(
        merge_kernel,
        jax.ShapeDtypeStruct((side * pairs, tok_dev + ANS_LEN, HD), bf16),
        [VMEM] * 2,
        flops=4 * state.size,
        bytes_accessed=2 * state.size,
        transcendentals=0,
    )(state, queries)
    state = lax.all_to_all(state, ("side", "pair"), 0, 0, tiled=True)
    projected = call(
        output_kernel,
        jax.ShapeDtypeStruct((head, tok_dev, columns), bf16),
        [VMEM] * 2,
        flops=2 * tok_dev * out_weight.size,
        bytes_accessed=2 * out_weight.size,
        transcendentals=0,
    )(state.reshape(side, pairs, tok_dev + ANS_LEN, HD), out_weight)
    projected = lax.all_to_all(projected, "head", 0, 0, tiled=True)
    return call(
        sum_kernel,
        jax.ShapeDtypeStruct((tok_dev, columns), bf16),
        [VMEM],
        flops=projected.size,
        bytes_accessed=2 * projected.size,
        transcendentals=0,
    )(projected)


def solution(mesh):
    seq, head, cand = (mesh.shape[name] for name in ("seq", "head", "cand"))
    parts = jax.sharding.Mesh(
        mesh.devices.reshape(2, seq // 4, 2, head, cand // 2, 2), (*SEQ, "head", *CAND)
    )
    in_specs = (
        P(CAND, SEQ),
        P(SEQ, "head"),
        P(SEQ, None),
        P(SEQ, None),
        P("head", SEQ),
        P((*SEQ, *CAND), None),
        P((*SEQ, *CAND), None),
        P(),
    )
    out_specs = P(CAND, (*SEQ, "head"))
    return jax.shard_map(body, mesh=parts, in_specs=in_specs, out_specs=out_specs, check_vma=False)
```

```python
import math

import jax
import jax.numpy as jnp
from jax import lax
from jax.experimental import pallas as pl
from jax.experimental.pallas import tpu as pltpu
from jax.sharding import PartitionSpec as P

HD = 128
GROUPS = 8
ANS_LEN = 8
KEY_BLOCK = 1024

NEGATIVE = -1e30
LOG2E = math.log2(math.e)
SMALL_SCALE = 16.0
KEY_SCALE = 2.0

VMEM = pl.BlockSpec(memory_space=pltpu.VMEM)
HBM = pl.BlockSpec(memory_space=pltpu.HBM)

SEQ = ("far", "pair", "side")
CAND = ("lo", "core")


def call(kernel, out_shape, in_specs, **cost):
    return pl.pallas_call(
        kernel,
        out_shape=out_shape,
        in_specs=in_specs,
        out_specs=jax.tree.map(lambda _: VMEM, out_shape),
        compiler_params=pltpu.CompilerParams(vmem_limit_bytes=40 * 1024 * 1024),
        cost_estimate=pl.CostEstimate(**cost),
    )


def dot(a, b):
    return jnp.dot(a, b, preferred_element_type=jnp.float32)


def dot_transposed(a, b):
    return lax.dot_general(a, b, (((1,), (1,)), ((), ())), preferred_element_type=jnp.float32)


def project_kernel(
    hidden_hbm, query_hbm, key_hbm, value_hbm, group_hbm, key_cache, value_cache,
    out_ref, bias_ref, cache_hbm, hidden_ref, weight_ref, group_smem, sems,
):
    far, pairs, side = (lax.axis_size(name) for name in SEQ)
    features = hidden_ref.shape[1]
    width = query_hbm.shape[1]
    halves = [pl.ds(i * (features // 2), features // 2) for i in range(2)]
    copies = []

    def start(source, target):
        copies.append(pltpu.make_async_copy(source, target, sems.at[len(copies)]))
        copies[-1].start()

    for half in halves:
        start(query_hbm.at[half, :], weight_ref.at[half, pl.ds(0, width)])
        start(hidden_hbm.at[:, half], hidden_ref.at[:, half])
        start(key_hbm.at[half, :], weight_ref.at[half, pl.ds(width, HD)])
        start(value_hbm.at[half, :], weight_ref.at[half, pl.ds(width + HD, HD)])
    start(group_hbm, group_smem)
    start(key_cache, cache_hbm.at[0])
    start(value_cache, cache_hbm.at[1])
    total = None
    for i, half in enumerate(halves):
        for copy in copies[4 * i : 4 * i + 4]:
            copy.wait()
        part = dot(hidden_ref[:, half], weight_ref[half, :])
        total = part if total is None else total + part
    ring = SMALL_SCALE * lax.axis_size("pair") * side
    tokens = total.shape[0]
    for h in range(side):
        for p in range(pairs):
            out_ref[p * side + h, :tokens] = total[:, h * HD : (h + 1) * HD] * ring
    for s, scale in ((0, ring * KEY_SCALE / SMALL_SCALE), (1, ring)):
        part = total[:, width + s * HD : width + (s + 1) * HD] * scale
        for p in range(pairs):
            for f in range(far):
                place = slice((f * pairs + p) * ANS_LEN, (f * pairs + p + 1) * ANS_LEN)
                out_ref[p * side + s, tokens + f * ANS_LEN : tokens + (f + 1) * ANS_LEN] = part[place]
    copies[-3].wait()
    chunk = lax.axis_index(SEQ) // (lax.axis_size(SEQ) // GROUPS)
    lane = lax.broadcasted_iota(jnp.int32, bias_ref.shape, 1)
    bias = jnp.zeros(bias_ref.shape, jnp.float32)
    for c in range(group_smem.shape[0]):
        hidden_by = jnp.where(group_smem[c] >= chunk, 0.0, NEGATIVE)
        bias = jnp.where(lane == c, hidden_by, bias)
    bias_ref[...] = bias
    copies[-2].wait()
    copies[-1].wait()


def reduce_kernel(part_ref, out_ref):
    total = jnp.sum(part_ref[...], axis=0) * (1 / part_ref.shape[0])
    out_ref[...] = jnp.broadcast_to(total[None], out_ref.shape)


def packed(mean, level):
    high = level.astype(jnp.bfloat16).astype(jnp.float32)
    middle = (level - high).astype(jnp.bfloat16).astype(jnp.float32)
    row = lax.broadcasted_iota(jnp.int32, mean.shape, 0)
    lane = lax.broadcasted_iota(jnp.int32, mean.shape, 1)
    line = lax.broadcasted_iota(jnp.int32, (ANS_LEN, HD), 0)
    lines = jnp.zeros((ANS_LEN, HD), jnp.float32)
    for place, term in enumerate((high, middle, level - high - middle)):
        spread = jnp.sum(jnp.where(lane == row, term, 0.0), axis=0, keepdims=True)
        lines = jnp.where(line == place, spread, lines)
    return jnp.concatenate([mean, lines], axis=0).astype(jnp.bfloat16)


def unpacked(state):
    state = state.astype(jnp.float32)
    rows = state.shape[-2] - ANS_LEN
    mean = state[..., :rows, :]
    line = jnp.sum(state[..., rows:, :], axis=-2, keepdims=True)
    row = lax.broadcasted_iota(jnp.int32, mean.shape, mean.ndim - 2)
    lane = lax.broadcasted_iota(jnp.int32, mean.shape, mean.ndim - 1)
    return mean, jnp.sum(jnp.where(lane == row, line, 0.0), axis=-1, keepdims=True)


def merged(mean, level):
    best = jnp.max(level, axis=0)
    factor = jnp.exp(level - best[None])
    total = jnp.sum(factor, axis=0)
    return jnp.sum(mean * factor, axis=0) / total, best + jnp.log(total)


def attend_kernel(query_ref, cache_ref, other_ref, bias_ref, out_ref):
    scale = HD ** (-0.5)
    far, side, lo, rows, _ = out_ref.shape
    rows -= ANS_LEN
    halves = far
    cores = lax.axis_size("core")
    cands = rows // ANS_LEN
    query = query_ref[:, :rows].reshape(side * lo, halves, rows, HD)
    query = jnp.sum(query, axis=1).reshape(side * lo * rows, HD)
    query = (query * (1 / SMALL_SCALE)).astype(jnp.bfloat16)
    shard = cache_ref.shape[1]
    steps = [
        (cache, slice(start, start + KEY_BLOCK))
        for cache in (cache_ref, other_ref)
        for start in range(0, shard, KEY_BLOCK)
    ]

    def scored(step):
        cache, part = step
        return dot_transposed(query, cache[0, part])

    ahead = scored(steps[0])
    held = []
    for i, (cache, part) in enumerate(steps):
        scores = ahead
        if i + 1 < len(steps):
            ahead = scored(steps[i + 1])
        top = jnp.max(scores, axis=1, keepdims=True)
        weights = jnp.exp2((scores - top) * (scale * LOG2E))
        total = jnp.sum(weights, axis=1, keepdims=True)
        held.append((top * scale, total, dot(weights.astype(jnp.bfloat16), cache[1, part])))
    top = held[0][0]
    for part in held[1:]:
        top = jnp.maximum(top, part[0])
    factors = [jnp.exp(part[0] - top) for part in held]
    total = sum(part[1] * factor for part, factor in zip(held, factors))
    mean = sum(part[2] * factor for part, factor in zip(held, factors)) / total
    place = lax.broadcasted_iota(jnp.int32, mean.shape, 0) // ANS_LEN
    lane = lax.broadcasted_iota(jnp.int32, mean.shape, 1)
    cand = place // cands % lo * cores + lax.axis_index("core")
    candidate = cand * cands + place % cands
    bias = jnp.sum(jnp.where(lane == candidate, bias_ref[0:1, :], 0.0), axis=1, keepdims=True)
    level = top + jnp.log(total) + bias
    for block in range(side * lo):
        part = slice(block * rows, (block + 1) * rows)
        state = packed(mean[part], level[part])
        for f in range(far):
            out_ref[f, block // lo, block % lo] = state


def merge_kernel(state_ref, own_ref, out_ref):
    mean, level = merged(*unpacked(state_ref[...]))
    halves, pairs, _ = (lax.axis_size(name) for name in SEQ)
    rows = pairs * ANS_LEN
    tokens = mean.shape[0]

    def own(s, part, scale):
        place = (s * lax.axis_size("lo") + lax.axis_index("lo")) * halves
        total = own_ref[place, part]
        for half in range(1, halves):
            total = total + own_ref[place + half, part]
        return (total * (1 / scale)).astype(jnp.bfloat16)

    query = own(lax.axis_index("side"), slice(0, tokens), SMALL_SCALE)
    key = own(0, slice(tokens, None), KEY_SCALE)
    value = own(1, slice(tokens, None), SMALL_SCALE)
    scores = dot_transposed(query, key) * HD ** (-0.5)
    row = lax.broadcasted_iota(jnp.int32, scores.shape, 0)
    column = lax.broadcasted_iota(jnp.int32, scores.shape, 1)
    shown = (row // rows == column // ANS_LEN) & (column % ANS_LEN <= row % ANS_LEN)
    scores = jnp.where(shown, scores, NEGATIVE)
    top = jnp.max(scores, axis=1, keepdims=True)
    weights = jnp.where(shown, jnp.exp(scores - top), 0.0)
    total = jnp.sum(weights, axis=1, keepdims=True)
    own_mean = dot(weights.astype(jnp.bfloat16), value) / total
    own_level = top + jnp.log(total)
    row = lax.broadcasted_iota(jnp.int32, level.shape, 0)
    mine = row // ANS_LEN % pairs == lax.axis_index("pair")
    own_level = jnp.where(mine, own_level, NEGATIVE)
    mean, level = merged(jnp.stack([mean, own_mean]), jnp.stack([level, own_level]))
    out_ref[...] = jnp.broadcast_to(packed(mean, level)[None], out_ref.shape)


def output_kernel(state_ref, weight_ref, out_ref):
    blocks, _, width = out_ref.shape
    columns = [merged(*unpacked(state_ref[s]))[0] for s in range(state_ref.shape[0])]
    attention = jnp.concatenate(columns, axis=1).astype(jnp.bfloat16)
    out = dot(attention, weight_ref[...])
    for block in range(blocks):
        out_ref[block] = out[:, block * width : (block + 1) * width].astype(jnp.bfloat16)


def body(
    hidden, query_weight, key_weight, value_weight, out_weight, key_cache, value_cache, cand_group
):
    tok_dev, feat_dev = hidden.shape
    heads_dev = query_weight.shape[1] // HD
    head, lo = lax.axis_size("head"), lax.axis_size("lo")
    far, pairs, side = (lax.axis_size(name) for name in SEQ)
    shard_len = key_cache.shape[0]
    bf16, f32 = jnp.bfloat16, jnp.float32
    rows = tok_dev * heads_dev * lo
    columns = out_weight.shape[1] // head

    inputs = (hidden, query_weight, key_weight, value_weight, cand_group, key_cache, value_cache)
    inputs = [pltpu.with_memory_space_constraint(x, pltpu.HBM) for x in inputs]
    partial, bias, cache = pl.pallas_call(
        project_kernel,
        out_shape=(
            jax.ShapeDtypeStruct((pairs * side, tok_dev + far * ANS_LEN, HD), f32),
            jax.ShapeDtypeStruct((ANS_LEN, HD), f32),
            jax.ShapeDtypeStruct((2, *key_cache.shape), bf16),
        ),
        in_specs=[HBM] * 7,
        out_specs=(VMEM, VMEM, HBM),
        scratch_shapes=[
            pltpu.VMEM(hidden.shape, bf16),
            pltpu.VMEM((feat_dev, (heads_dev + 2) * HD), bf16),
            pltpu.SMEM(cand_group.shape, jnp.int32),
            pltpu.SemaphoreType.DMA((11,)),
        ],
        compiler_params=pltpu.CompilerParams(vmem_limit_bytes=40 * 1024 * 1024),
        cost_estimate=pl.CostEstimate(
            flops=2 * tok_dev * feat_dev * (heads_dev + 2) * HD,
            bytes_accessed=2 * feat_dev * (tok_dev + (heads_dev + 2) * HD),
            transcendentals=0,
        ),
    )(*inputs)
    other = lax.ppermute(cache, "core", [(0, 1), (1, 0)])
    partial = lax.all_to_all(partial.astype(jnp.float16), ("pair", "side"), 0, 0, tiled=True)
    near = far * side * lo
    queries = call(
        reduce_kernel,
        jax.ShapeDtypeStruct((near, *partial.shape[1:]), f32),
        [VMEM],
        flops=partial.size,
        bytes_accessed=partial.size * 4,
        transcendentals=0,
    )(partial.astype(f32))
    queries = queries.astype(jnp.float16)
    queries = lax.all_to_all(queries, ("side", "lo", "far"), 0, 0, tiled=True).astype(f32)
    state = call(
        attend_kernel,
        jax.ShapeDtypeStruct((far, side, lo, tok_dev + ANS_LEN, HD), bf16),
        [VMEM] * 4,
        flops=8 * rows * shard_len * HD,
        bytes_accessed=8 * shard_len * HD,
        transcendentals=2 * rows * shard_len,
    )(queries, cache, other, bias)
    state = state.reshape(near, tok_dev + ANS_LEN, HD)
    state = lax.all_to_all(state, ("far", "side", "lo"), 0, 0, tiled=True)
    state = call(
        merge_kernel,
        jax.ShapeDtypeStruct((side * pairs, tok_dev + ANS_LEN, HD), bf16),
        [VMEM] * 2,
        flops=4 * state.size,
        bytes_accessed=2 * state.size,
        transcendentals=0,
    )(state, queries)
    state = lax.all_to_all(state, ("side", "pair"), 0, 0, tiled=True)
    projected = call(
        output_kernel,
        jax.ShapeDtypeStruct((head, tok_dev, columns), bf16),
        [VMEM] * 2,
        flops=2 * tok_dev * out_weight.size,
        bytes_accessed=2 * out_weight.size,
        transcendentals=0,
    )(state.reshape(side, pairs, tok_dev + ANS_LEN, HD), out_weight)
    projected = lax.all_to_all(projected, "head", 0, 0, tiled=True)
    return jnp.sum(projected.astype(f32), axis=0).astype(bf16)


def solution(mesh):
    seq, head, cand = (mesh.shape[name] for name in ("seq", "head", "cand"))
    parts = jax.sharding.Mesh(
        mesh.devices.reshape(2, seq // 4, 2, head, cand // 2, 2), (*SEQ, "head", *CAND)
    )
    in_specs = (
        P(CAND, SEQ),
        P(SEQ, "head"),
        P(SEQ, None),
        P(SEQ, None),
        P("head", SEQ),
        P((*SEQ, *CAND), None),
        P((*SEQ, *CAND), None),
        P(),
    )
    out_specs = P(CAND, (*SEQ, "head"))
    return jax.shard_map(body, mesh=parts, in_specs=in_specs, out_specs=out_specs, check_vma=False)
```

```python
import math

import jax
import jax.numpy as jnp
from jax import lax
from jax.experimental import pallas as pl
from jax.experimental.pallas import tpu as pltpu
from jax.sharding import PartitionSpec as P

HD = 128
GROUPS = 8
ANS_LEN = 8
KEY_BLOCK = 1024

NEGATIVE = -1e30
LOG2E = math.log2(math.e)
SMALL_SCALE = 16.0
KEY_SCALE = 2.0

VMEM = pl.BlockSpec(memory_space=pltpu.VMEM)
HBM = pl.BlockSpec(memory_space=pltpu.HBM)

SEQ = ("far", "pair", "side")
CAND = ("lo", "core")


def call(kernel, out_shape, in_specs, scratch=(), **cost):
    return pl.pallas_call(
        kernel,
        out_shape=out_shape,
        in_specs=in_specs,
        scratch_shapes=scratch,
        out_specs=jax.tree.map(lambda _: VMEM, out_shape),
        compiler_params=pltpu.CompilerParams(vmem_limit_bytes=40 * 1024 * 1024),
        cost_estimate=pl.CostEstimate(**cost),
    )


def dot(a, b):
    return jnp.dot(a, b, preferred_element_type=jnp.float32)


def dot_transposed(a, b):
    return lax.dot_general(a, b, (((1,), (1,)), ((), ())), preferred_element_type=jnp.float32)


def project_kernel(
    hidden_hbm, query_hbm, key_hbm, value_hbm, group_hbm, key_cache, value_cache,
    out_ref, bias_ref, cache_hbm, hidden_ref, weight_ref, group_smem, sems,
):
    far, pairs, side = (lax.axis_size(name) for name in SEQ)
    features = hidden_ref.shape[1]
    width = query_hbm.shape[1]
    halves = [pl.ds(i * (features // 2), features // 2) for i in range(2)]
    copies = []

    def start(source, target):
        copies.append(pltpu.make_async_copy(source, target, sems.at[len(copies)]))
        copies[-1].start()

    start(group_hbm, group_smem)
    for half in halves:
        start(query_hbm.at[half, :], weight_ref.at[half, pl.ds(0, width)])
        start(hidden_hbm.at[:, half], hidden_ref.at[:, half])
        start(key_hbm.at[half, :], weight_ref.at[half, pl.ds(width, HD)])
        start(value_hbm.at[half, :], weight_ref.at[half, pl.ds(width + HD, HD)])
    start(key_cache, cache_hbm.at[0])
    start(value_cache, cache_hbm.at[1])
    copies[0].wait()
    chunk = lax.axis_index(SEQ) // (lax.axis_size(SEQ) // GROUPS)
    lane = lax.broadcasted_iota(jnp.int32, bias_ref.shape, 1)
    bias = jnp.zeros(bias_ref.shape, jnp.float32)
    for c in range(group_smem.shape[0]):
        hidden_by = jnp.where(group_smem[c] >= chunk, 0.0, NEGATIVE)
        bias = jnp.where(lane == c, hidden_by, bias)
    bias_ref[...] = bias
    total = None
    for i, half in enumerate(halves):
        for copy in copies[4 * i + 1 : 4 * i + 5]:
            copy.wait()
        part = dot(hidden_ref[:, half], weight_ref[half, :])
        total = part if total is None else total + part
    ring = SMALL_SCALE * lax.axis_size("pair") * side
    tokens = total.shape[0]
    for h in range(side):
        for p in range(pairs):
            out_ref[p * side + h, :tokens] = total[:, h * HD : (h + 1) * HD] * ring
    for s, scale in ((0, ring * KEY_SCALE / SMALL_SCALE), (1, ring)):
        part = total[:, width + s * HD : width + (s + 1) * HD] * scale
        for p in range(pairs):
            for f in range(far):
                place = slice((f * pairs + p) * ANS_LEN, (f * pairs + p + 1) * ANS_LEN)
                out_ref[p * side + s, tokens + f * ANS_LEN : tokens + (f + 1) * ANS_LEN] = part[place]
    copies[-2].wait()
    copies[-1].wait()


def reduce_kernel(part_ref, out_ref):
    total = jnp.sum(part_ref[...], axis=0) * (1 / part_ref.shape[0])
    out_ref[...] = jnp.broadcast_to(total[None], out_ref.shape)


def packed(mean, level):
    high = level.astype(jnp.bfloat16).astype(jnp.float32)
    middle = (level - high).astype(jnp.bfloat16).astype(jnp.float32)
    row = lax.broadcasted_iota(jnp.int32, mean.shape, 0)
    lane = lax.broadcasted_iota(jnp.int32, mean.shape, 1)
    line = lax.broadcasted_iota(jnp.int32, (ANS_LEN, HD), 0)
    lines = jnp.zeros((ANS_LEN, HD), jnp.float32)
    for place, term in enumerate((high, middle, level - high - middle)):
        spread = jnp.sum(jnp.where(lane == row, term, 0.0), axis=0, keepdims=True)
        lines = jnp.where(line == place, spread, lines)
    return jnp.concatenate([mean, lines], axis=0).astype(jnp.bfloat16)


def unpacked(state):
    state = state.astype(jnp.float32)
    rows = state.shape[-2] - ANS_LEN
    mean = state[..., :rows, :]
    line = jnp.sum(state[..., rows:, :], axis=-2, keepdims=True)
    row = lax.broadcasted_iota(jnp.int32, mean.shape, mean.ndim - 2)
    lane = lax.broadcasted_iota(jnp.int32, mean.shape, mean.ndim - 1)
    return mean, jnp.sum(jnp.where(lane == row, line, 0.0), axis=-1, keepdims=True)


def merged(mean, level):
    best = jnp.max(level, axis=0)
    factor = jnp.exp(level - best[None])
    total = jnp.sum(factor, axis=0)
    return jnp.sum(mean * factor, axis=0) / total, best + jnp.log(total)


def attend_kernel(query_ref, cache_ref, other_ref, bias_ref, out_ref, held_ref):
    scale = HD ** (-0.5)
    far, side, lo, rows, _ = out_ref.shape
    rows -= ANS_LEN
    halves = far
    cores = lax.axis_size("core")
    cands = rows // ANS_LEN
    query = query_ref[:, :rows].reshape(side * lo, halves, rows, HD)
    query = jnp.sum(query, axis=1).reshape(side * lo * rows, HD)
    query = (query * (1 / SMALL_SCALE)).astype(jnp.bfloat16)
    shard = cache_ref.shape[1]
    steps = [
        (cache, slice(start, start + KEY_BLOCK))
        for cache in (cache_ref, other_ref)
        for start in range(0, shard, KEY_BLOCK)
    ]

    top = None
    for i, (cache, part) in enumerate(steps):
        scores = dot_transposed(query, cache[0, part])
        held_ref[i] = scores
        for lanes in range(0, KEY_BLOCK, HD):
            piece = scores[:, lanes : lanes + HD]
            top = piece if top is None else jnp.maximum(top, piece)
    top = jnp.max(top, axis=1, keepdims=True)
    total, mean = 0.0, 0.0
    for i, (cache, part) in enumerate(steps):
        weights = jnp.exp2((held_ref[i] - top) * (scale * LOG2E))
        for lanes in range(0, KEY_BLOCK, HD):
            total = total + weights[:, lanes : lanes + HD]
        mean = mean + dot(weights.astype(jnp.bfloat16), cache[1, part])
    total = jnp.sum(total, axis=1, keepdims=True)
    mean = mean / total
    place = lax.broadcasted_iota(jnp.int32, mean.shape, 0) // ANS_LEN
    lane = lax.broadcasted_iota(jnp.int32, mean.shape, 1)
    cand = place // cands % lo * cores + lax.axis_index("core")
    candidate = cand * cands + place % cands
    bias = jnp.sum(jnp.where(lane == candidate, bias_ref[0:1, :], 0.0), axis=1, keepdims=True)
    level = top * scale + jnp.log(total) + bias
    for block in range(side * lo):
        part = slice(block * rows, (block + 1) * rows)
        state = packed(mean[part], level[part])
        for f in range(far):
            out_ref[f, block // lo, block % lo] = state


def merge_kernel(state_ref, own_ref, out_ref):
    mean, level = merged(*unpacked(state_ref[...]))
    halves, pairs, _ = (lax.axis_size(name) for name in SEQ)
    rows = pairs * ANS_LEN
    tokens = mean.shape[0]

    def own(s, part, scale):
        place = (s * lax.axis_size("lo") + lax.axis_index("lo")) * halves
        total = own_ref[place, part]
        for half in range(1, halves):
            total = total + own_ref[place + half, part]
        return (total * (1 / scale)).astype(jnp.bfloat16)

    query = own(lax.axis_index("side"), slice(0, tokens), SMALL_SCALE)
    key = own(0, slice(tokens, None), KEY_SCALE)
    value = own(1, slice(tokens, None), SMALL_SCALE)
    scores = dot_transposed(query, key) * HD ** (-0.5)
    row = lax.broadcasted_iota(jnp.int32, scores.shape, 0)
    column = lax.broadcasted_iota(jnp.int32, scores.shape, 1)
    shown = (row // rows == column // ANS_LEN) & (column % ANS_LEN <= row % ANS_LEN)
    scores = jnp.where(shown, scores, NEGATIVE)
    top = jnp.max(scores, axis=1, keepdims=True)
    weights = jnp.where(shown, jnp.exp(scores - top), 0.0)
    total = jnp.sum(weights, axis=1, keepdims=True)
    own_mean = dot(weights.astype(jnp.bfloat16), value) / total
    own_level = top + jnp.log(total)
    row = lax.broadcasted_iota(jnp.int32, level.shape, 0)
    mine = row // ANS_LEN % pairs == lax.axis_index("pair")
    own_level = jnp.where(mine, own_level, NEGATIVE)
    mean, level = merged(jnp.stack([mean, own_mean]), jnp.stack([level, own_level]))
    out_ref[...] = jnp.broadcast_to(packed(mean, level)[None], out_ref.shape)


def output_kernel(state_ref, weight_ref, out_ref):
    blocks, _, width = out_ref.shape
    columns = [merged(*unpacked(state_ref[s]))[0] for s in range(state_ref.shape[0])]
    attention = jnp.concatenate(columns, axis=1).astype(jnp.bfloat16)
    out = dot(attention, weight_ref[...])
    for block in range(blocks):
        out_ref[block] = out[:, block * width : (block + 1) * width].astype(jnp.bfloat16)


def body(
    hidden, query_weight, key_weight, value_weight, out_weight, key_cache, value_cache, cand_group
):
    tok_dev, feat_dev = hidden.shape
    heads_dev = query_weight.shape[1] // HD
    head, lo = lax.axis_size("head"), lax.axis_size("lo")
    far, pairs, side = (lax.axis_size(name) for name in SEQ)
    shard_len = key_cache.shape[0]
    bf16, f32 = jnp.bfloat16, jnp.float32
    rows = tok_dev * heads_dev * lo
    columns = out_weight.shape[1] // head

    inputs = (hidden, query_weight, key_weight, value_weight, cand_group, key_cache, value_cache)
    inputs = [pltpu.with_memory_space_constraint(x, pltpu.HBM) for x in inputs]
    partial, bias, cache = pl.pallas_call(
        project_kernel,
        out_shape=(
            jax.ShapeDtypeStruct((pairs * side, tok_dev + far * ANS_LEN, HD), f32),
            jax.ShapeDtypeStruct((ANS_LEN, HD), f32),
            jax.ShapeDtypeStruct((2, *key_cache.shape), bf16),
        ),
        in_specs=[HBM] * 7,
        out_specs=(VMEM, VMEM, HBM),
        scratch_shapes=[
            pltpu.VMEM(hidden.shape, bf16),
            pltpu.VMEM((feat_dev, (heads_dev + 2) * HD), bf16),
            pltpu.SMEM(cand_group.shape, jnp.int32),
            pltpu.SemaphoreType.DMA((11,)),
        ],
        compiler_params=pltpu.CompilerParams(vmem_limit_bytes=40 * 1024 * 1024),
        cost_estimate=pl.CostEstimate(
            flops=2 * tok_dev * feat_dev * (heads_dev + 2) * HD,
            bytes_accessed=2 * feat_dev * (tok_dev + (heads_dev + 2) * HD),
            transcendentals=0,
        ),
    )(*inputs)
    other = lax.ppermute(cache, "core", [(0, 1), (1, 0)])
    partial = lax.all_to_all(partial.astype(jnp.float16), ("pair", "side"), 0, 0, tiled=True)
    near = far * side * lo
    queries = call(
        reduce_kernel,
        jax.ShapeDtypeStruct((near, *partial.shape[1:]), f32),
        [VMEM],
        flops=partial.size,
        bytes_accessed=partial.size * 4,
        transcendentals=0,
    )(partial.astype(f32))
    queries = queries.astype(jnp.float16)
    queries = lax.all_to_all(queries, ("side", "lo", "far"), 0, 0, tiled=True).astype(f32)
    state = call(
        attend_kernel,
        jax.ShapeDtypeStruct((far, side, lo, tok_dev + ANS_LEN, HD), bf16),
        [VMEM] * 4,
        [pltpu.VMEM((2 * shard_len // KEY_BLOCK, rows, KEY_BLOCK), f32)],
        flops=8 * rows * shard_len * HD,
        bytes_accessed=8 * shard_len * HD,
        transcendentals=2 * rows * shard_len,
    )(queries, cache, other, bias)
    state = state.reshape(near, tok_dev + ANS_LEN, HD)
    state = lax.all_to_all(state, ("far", "side", "lo"), 0, 0, tiled=True)
    state = call(
        merge_kernel,
        jax.ShapeDtypeStruct((side * pairs, tok_dev + ANS_LEN, HD), bf16),
        [VMEM] * 2,
        flops=4 * state.size,
        bytes_accessed=2 * state.size,
        transcendentals=0,
    )(state, queries)
    state = lax.all_to_all(state, ("side", "pair"), 0, 0, tiled=True)
    projected = call(
        output_kernel,
        jax.ShapeDtypeStruct((head, tok_dev, columns), bf16),
        [VMEM] * 2,
        flops=2 * tok_dev * out_weight.size,
        bytes_accessed=2 * out_weight.size,
        transcendentals=0,
    )(state.reshape(side, pairs, tok_dev + ANS_LEN, HD), out_weight)
    projected = lax.all_to_all(projected, "head", 0, 0, tiled=True)
    return jnp.sum(projected.astype(f32), axis=0).astype(bf16)


def solution(mesh):
    seq, head, cand = (mesh.shape[name] for name in ("seq", "head", "cand"))
    parts = jax.sharding.Mesh(
        mesh.devices.reshape(2, seq // 4, 2, head, cand // 2, 2), (*SEQ, "head", *CAND)
    )
    in_specs = (
        P(CAND, SEQ),
        P(SEQ, "head"),
        P(SEQ, None),
        P(SEQ, None),
        P("head", SEQ),
        P((*SEQ, *CAND), None),
        P((*SEQ, *CAND), None),
        P(),
    )
    out_specs = P(CAND, (*SEQ, "head"))
    return jax.shard_map(body, mesh=parts, in_specs=in_specs, out_specs=out_specs, check_vma=False)
```

```python
import math

import jax
import jax.numpy as jnp
from jax import lax
from jax.experimental import pallas as pl
from jax.experimental.pallas import tpu as pltpu
from jax.sharding import PartitionSpec as P

HD = 128
GROUPS = 8
ANS_LEN = 8
ROW_BLOCK = 128

NEGATIVE = -1e30
LOG2E = math.log2(math.e)
SMALL_SCALE = 16.0
KEY_SCALE = 2.0

VMEM = pl.BlockSpec(memory_space=pltpu.VMEM)
HBM = pl.BlockSpec(memory_space=pltpu.HBM)

SEQ = ("far", "pair", "side")
CAND = ("lo", "core")


def call(kernel, out_shape, in_specs, **cost):
    return pl.pallas_call(
        kernel,
        out_shape=out_shape,
        in_specs=in_specs,
        out_specs=jax.tree.map(lambda _: VMEM, out_shape),
        compiler_params=pltpu.CompilerParams(vmem_limit_bytes=40 * 1024 * 1024),
        cost_estimate=pl.CostEstimate(**cost),
    )


def dot(a, b):
    return jnp.dot(a, b, preferred_element_type=jnp.float32)


def dot_transposed(a, b):
    return lax.dot_general(a, b, (((1,), (1,)), ((), ())), preferred_element_type=jnp.float32)


def project_kernel(
    hidden_hbm, query_hbm, key_hbm, value_hbm, group_hbm, key_cache, value_cache,
    out_ref, bias_ref, cache_hbm, hidden_ref, weight_ref, group_smem, sems,
):
    far, pairs, side = (lax.axis_size(name) for name in SEQ)
    features = hidden_ref.shape[1]
    width = query_hbm.shape[1]
    halves = [pl.ds(i * (features // 2), features // 2) for i in range(2)]
    copies = []

    def start(source, target):
        copies.append(pltpu.make_async_copy(source, target, sems.at[len(copies)]))
        copies[-1].start()

    start(group_hbm, group_smem)
    for half in halves:
        start(query_hbm.at[half, :], weight_ref.at[half, pl.ds(0, width)])
        start(hidden_hbm.at[:, half], hidden_ref.at[:, half])
        start(key_hbm.at[half, :], weight_ref.at[half, pl.ds(width, HD)])
        start(value_hbm.at[half, :], weight_ref.at[half, pl.ds(width + HD, HD)])
    start(key_cache, cache_hbm.at[0])
    start(value_cache, cache_hbm.at[1])
    copies[0].wait()
    chunk = lax.axis_index(SEQ) // (lax.axis_size(SEQ) // GROUPS)
    lane = lax.broadcasted_iota(jnp.int32, bias_ref.shape, 1)
    bias = jnp.zeros(bias_ref.shape, jnp.float32)
    for c in range(group_smem.shape[0]):
        hidden_by = jnp.where(group_smem[c] >= chunk, 0.0, NEGATIVE)
        bias = jnp.where(lane == c, hidden_by, bias)
    bias_ref[...] = bias
    total = None
    for i, half in enumerate(halves):
        for copy in copies[4 * i + 1 : 4 * i + 5]:
            copy.wait()
        part = dot(hidden_ref[:, half], weight_ref[half, :])
        total = part if total is None else total + part
    ring = SMALL_SCALE * lax.axis_size("pair") * side
    tokens = total.shape[0]
    for h in range(side):
        for p in range(pairs):
            out_ref[p * side + h, :tokens] = total[:, h * HD : (h + 1) * HD] * ring
    for s, scale in ((0, ring * KEY_SCALE / SMALL_SCALE), (1, ring)):
        part = total[:, width + s * HD : width + (s + 1) * HD] * scale
        for p in range(pairs):
            for f in range(far):
                place = slice((f * pairs + p) * ANS_LEN, (f * pairs + p + 1) * ANS_LEN)
                out_ref[p * side + s, tokens + f * ANS_LEN : tokens + (f + 1) * ANS_LEN] = part[place]
    copies[-2].wait()
    copies[-1].wait()


def reduce_kernel(part_ref, out_ref):
    total = jnp.sum(part_ref[...], axis=0) * (1 / part_ref.shape[0])
    out_ref[...] = jnp.broadcast_to(total[None], out_ref.shape)


def packed(mean, level):
    high = level.astype(jnp.bfloat16).astype(jnp.float32)
    middle = (level - high).astype(jnp.bfloat16).astype(jnp.float32)
    row = lax.broadcasted_iota(jnp.int32, mean.shape, 0)
    lane = lax.broadcasted_iota(jnp.int32, mean.shape, 1)
    line = lax.broadcasted_iota(jnp.int32, (ANS_LEN, HD), 0)
    lines = jnp.zeros((ANS_LEN, HD), jnp.float32)
    for place, term in enumerate((high, middle, level - high - middle)):
        spread = jnp.sum(jnp.where(lane == row, term, 0.0), axis=0, keepdims=True)
        lines = jnp.where(line == place, spread, lines)
    return jnp.concatenate([mean, lines], axis=0).astype(jnp.bfloat16)


def unpacked(state):
    state = state.astype(jnp.float32)
    rows = state.shape[-2] - ANS_LEN
    mean = state[..., :rows, :]
    line = jnp.sum(state[..., rows:, :], axis=-2, keepdims=True)
    row = lax.broadcasted_iota(jnp.int32, mean.shape, mean.ndim - 2)
    lane = lax.broadcasted_iota(jnp.int32, mean.shape, mean.ndim - 1)
    return mean, jnp.sum(jnp.where(lane == row, line, 0.0), axis=-1, keepdims=True)


def merged(mean, level):
    best = jnp.max(level, axis=0)
    factor = jnp.exp(level - best[None])
    total = jnp.sum(factor, axis=0)
    return jnp.sum(mean * factor, axis=0) / total, best + jnp.log(total)


def own_state(own_ref, halves, pairs):
    tokens = own_ref.shape[1] - halves * ANS_LEN
    rows = tokens // halves

    def own(s, part, scale):
        place = (s * lax.axis_size("lo") + lax.axis_index("lo")) * halves
        total = own_ref[place, part]
        for half in range(1, halves):
            total = total + own_ref[place + half, part]
        return (total * (1 / scale)).astype(jnp.bfloat16)

    query = own(lax.axis_index("side"), slice(0, tokens), SMALL_SCALE)
    key = own(0, slice(tokens, None), KEY_SCALE)
    value = own(1, slice(tokens, None), SMALL_SCALE)
    scores = dot_transposed(query, key) * HD ** (-0.5)
    row = lax.broadcasted_iota(jnp.int32, scores.shape, 0)
    column = lax.broadcasted_iota(jnp.int32, scores.shape, 1)
    shown = (row // rows == column // ANS_LEN) & (column % ANS_LEN <= row % ANS_LEN)
    scores = jnp.where(shown, scores, NEGATIVE)
    top = jnp.max(scores, axis=1, keepdims=True)
    weights = jnp.where(shown, jnp.exp(scores - top), 0.0)
    total = jnp.sum(weights, axis=1, keepdims=True)
    mean = dot(weights.astype(jnp.bfloat16), value) / total
    row = lax.broadcasted_iota(jnp.int32, mean.shape, 0)
    mine = row // ANS_LEN % pairs == lax.axis_index("pair")
    return mean, jnp.where(mine, jnp.broadcast_to(top + jnp.log(total), mean.shape), NEGATIVE)


def attend_kernel(query_ref, cache_ref, other_ref, bias_ref, out_ref, own_ref):
    scale = HD ** (-0.5)
    far, side, lo, rows, _ = out_ref.shape
    rows -= ANS_LEN
    halves = far
    sources = ROW_BLOCK // rows * halves
    cores = lax.axis_size("core")
    cands = rows // ANS_LEN
    row = lax.broadcasted_iota(jnp.int32, (ROW_BLOCK, HD), 0)
    lane = lax.broadcasted_iota(jnp.int32, (ROW_BLOCK, HD), 1)
    caches = (cache_ref, other_ref)
    blocks = query_ref.shape[0] // sources

    def scored(r):
        parts = query_ref[r * sources : (r + 1) * sources, :rows]
        query = jnp.sum(parts.reshape(-1, halves, rows, HD), axis=1).reshape(ROW_BLOCK, HD)
        query = (query * (1 / SMALL_SCALE)).astype(jnp.bfloat16)
        return [dot_transposed(query, cache[0]) for cache in caches]

    ahead = scored(0)
    for r in range(blocks):
        scores = ahead
        if r + 1 < blocks:
            ahead = scored(r + 1)
        else:
            own_ref[0], own_ref[1] = own_state(query_ref, halves, cands // halves)
        top = jnp.maximum(*(jnp.max(part, axis=1, keepdims=True) for part in scores))
        total, mean = 0.0, 0.0
        for part, cache in zip(scores, caches):
            weights = jnp.exp2((part - top) * (scale * LOG2E))
            total = total + jnp.sum(weights, axis=1, keepdims=True)
            mean = mean + dot(weights.astype(jnp.bfloat16), cache[1])
        mean = mean / total
        place = (row + r * ROW_BLOCK) // ANS_LEN
        cand = place // cands % lo * cores + lax.axis_index("core")
        candidate = cand * cands + place % cands
        bias = jnp.sum(jnp.where(lane == candidate, bias_ref[0:1, :], 0.0), axis=1, keepdims=True)
        level = top * scale + jnp.log(total) + bias
        for j in range(ROW_BLOCK // rows):
            part = slice(j * rows, (j + 1) * rows)
            state = packed(mean[part], level[part])
            block = r * (ROW_BLOCK // rows) + j
            for f in range(far):
                out_ref[f, block // lo, block % lo] = state


def merge_kernel(state_ref, own_ref, out_ref):
    mean, level = unpacked(state_ref[...])
    mean = jnp.concatenate([mean, own_ref[0:1]], axis=0)
    level = jnp.concatenate([level, own_ref[1:2, :, 0:1]], axis=0)
    state = packed(*merged(mean, level))
    out_ref[...] = jnp.broadcast_to(state[None], out_ref.shape)


def output_kernel(state_ref, weight_ref, out_ref):
    blocks, _, width = out_ref.shape
    columns = [merged(*unpacked(state_ref[s]))[0] for s in range(state_ref.shape[0])]
    attention = jnp.concatenate(columns, axis=1).astype(jnp.bfloat16)
    out = dot(attention, weight_ref[...])
    for block in range(blocks):
        out_ref[block] = out[:, block * width : (block + 1) * width].astype(jnp.bfloat16)


def body(
    hidden, query_weight, key_weight, value_weight, out_weight, key_cache, value_cache, cand_group
):
    tok_dev, feat_dev = hidden.shape
    heads_dev = query_weight.shape[1] // HD
    head, lo = lax.axis_size("head"), lax.axis_size("lo")
    far, pairs, side = (lax.axis_size(name) for name in SEQ)
    shard_len = key_cache.shape[0]
    bf16, f32 = jnp.bfloat16, jnp.float32
    rows = tok_dev * heads_dev * lo
    columns = out_weight.shape[1] // head

    inputs = (hidden, query_weight, key_weight, value_weight, cand_group, key_cache, value_cache)
    inputs = [pltpu.with_memory_space_constraint(x, pltpu.HBM) for x in inputs]
    partial, bias, cache = pl.pallas_call(
        project_kernel,
        out_shape=(
            jax.ShapeDtypeStruct((pairs * side, tok_dev + far * ANS_LEN, HD), f32),
            jax.ShapeDtypeStruct((ANS_LEN, HD), f32),
            jax.ShapeDtypeStruct((2, *key_cache.shape), bf16),
        ),
        in_specs=[HBM] * 7,
        out_specs=(VMEM, VMEM, HBM),
        scratch_shapes=[
            pltpu.VMEM(hidden.shape, bf16),
            pltpu.VMEM((feat_dev, (heads_dev + 2) * HD), bf16),
            pltpu.SMEM(cand_group.shape, jnp.int32),
            pltpu.SemaphoreType.DMA((11,)),
        ],
        compiler_params=pltpu.CompilerParams(vmem_limit_bytes=40 * 1024 * 1024),
        cost_estimate=pl.CostEstimate(
            flops=2 * tok_dev * feat_dev * (heads_dev + 2) * HD,
            bytes_accessed=2 * feat_dev * (tok_dev + (heads_dev + 2) * HD),
            transcendentals=0,
        ),
    )(*inputs)
    other = lax.ppermute(cache, "core", [(0, 1), (1, 0)])
    partial = lax.all_to_all(partial.astype(jnp.float16), ("pair", "side"), 0, 0, tiled=True)
    near = far * side * lo
    queries = call(
        reduce_kernel,
        jax.ShapeDtypeStruct((near, *partial.shape[1:]), f32),
        [VMEM],
        flops=partial.size,
        bytes_accessed=partial.size * 4,
        transcendentals=0,
    )(partial.astype(f32))
    queries = queries.astype(jnp.float16)
    queries = lax.all_to_all(queries, ("side", "lo", "far"), 0, 0, tiled=True).astype(f32)
    state, own = call(
        attend_kernel,
        (
            jax.ShapeDtypeStruct((far, side, lo, tok_dev + ANS_LEN, HD), bf16),
            jax.ShapeDtypeStruct((2, tok_dev, HD), f32),
        ),
        [VMEM] * 4,
        flops=8 * rows * shard_len * HD,
        bytes_accessed=8 * shard_len * HD,
        transcendentals=2 * rows * shard_len,
    )(queries, cache, other, bias)
    state = state.reshape(near, tok_dev + ANS_LEN, HD)
    state = lax.all_to_all(state, ("far", "side", "lo"), 0, 0, tiled=True)
    state = call(
        merge_kernel,
        jax.ShapeDtypeStruct((side * pairs, tok_dev + ANS_LEN, HD), bf16),
        [VMEM] * 2,
        flops=4 * state.size,
        bytes_accessed=2 * state.size,
        transcendentals=0,
    )(state, own)
    state = lax.all_to_all(state, ("side", "pair"), 0, 0, tiled=True)
    projected = call(
        output_kernel,
        jax.ShapeDtypeStruct((head, tok_dev, columns), bf16),
        [VMEM] * 2,
        flops=2 * tok_dev * out_weight.size,
        bytes_accessed=2 * out_weight.size,
        transcendentals=0,
    )(state.reshape(side, pairs, tok_dev + ANS_LEN, HD), out_weight)
    projected = lax.all_to_all(projected, "head", 0, 0, tiled=True)
    return jnp.sum(projected.astype(f32), axis=0).astype(bf16)


def solution(mesh):
    seq, head, cand = (mesh.shape[name] for name in ("seq", "head", "cand"))
    parts = jax.sharding.Mesh(
        mesh.devices.reshape(2, seq // 4, 2, head, cand // 2, 2), (*SEQ, "head", *CAND)
    )
    in_specs = (
        P(CAND, SEQ),
        P(SEQ, "head"),
        P(SEQ, None),
        P(SEQ, None),
        P("head", SEQ),
        P((*SEQ, *CAND), None),
        P((*SEQ, *CAND), None),
        P(),
    )
    out_specs = P(CAND, (*SEQ, "head"))
    return jax.shard_map(body, mesh=parts, in_specs=in_specs, out_specs=out_specs, check_vma=False)
```

```python
import math

import jax
import jax.numpy as jnp
from jax import lax
from jax.experimental import pallas as pl
from jax.experimental.pallas import tpu as pltpu
from jax.sharding import PartitionSpec as P

HD = 128
GROUPS = 8
ANS_LEN = 8
ROW_BLOCK = 128

NEGATIVE = -1e30
LOG2E = math.log2(math.e)
SMALL_SCALE = 16.0
KEY_SCALE = 2.0

VMEM = pl.BlockSpec(memory_space=pltpu.VMEM)
HBM = pl.BlockSpec(memory_space=pltpu.HBM)

SEQ = ("far", "pair", "side")
CAND = ("lo", "core")


def call(kernel, out_shape, in_specs, **cost):
    return pl.pallas_call(
        kernel,
        out_shape=out_shape,
        in_specs=in_specs,
        out_specs=jax.tree.map(lambda _: VMEM, out_shape),
        compiler_params=pltpu.CompilerParams(vmem_limit_bytes=40 * 1024 * 1024),
        cost_estimate=pl.CostEstimate(**cost),
    )


def dot(a, b):
    return jnp.dot(a, b, preferred_element_type=jnp.float32)


def dot_transposed(a, b):
    return lax.dot_general(a, b, (((1,), (1,)), ((), ())), preferred_element_type=jnp.float32)


def project_kernel(
    hidden_hbm, query_hbm, key_hbm, value_hbm, group_hbm, key_cache, value_cache,
    out_ref, bias_ref, cache_hbm, hidden_ref, weight_ref, group_smem, sems,
):
    far, pairs, side = (lax.axis_size(name) for name in SEQ)
    features = hidden_ref.shape[1]
    width = query_hbm.shape[1]
    halves = [pl.ds(i * (features // 2), features // 2) for i in range(2)]
    copies = []

    def start(source, target):
        copies.append(pltpu.make_async_copy(source, target, sems.at[len(copies)]))
        copies[-1].start()

    for half in halves:
        start(query_hbm.at[half, :], weight_ref.at[half, pl.ds(0, width)])
        start(hidden_hbm.at[:, half], hidden_ref.at[:, half])
        start(key_hbm.at[half, :], weight_ref.at[half, pl.ds(width, HD)])
        start(value_hbm.at[half, :], weight_ref.at[half, pl.ds(width + HD, HD)])
    start(group_hbm, group_smem)
    start(key_cache, cache_hbm.at[0])
    start(value_cache, cache_hbm.at[1])
    total = None
    for i, half in enumerate(halves):
        for copy in copies[4 * i : 4 * i + 4]:
            copy.wait()
        part = dot(hidden_ref[:, half], weight_ref[half, :])
        total = part if total is None else total + part
    ring = SMALL_SCALE * lax.axis_size("pair") * side
    tokens = total.shape[0]
    for h in range(side):
        for p in range(pairs):
            out_ref[p * side + h, :tokens] = total[:, h * HD : (h + 1) * HD] * ring
    for s, scale in ((0, ring * KEY_SCALE / SMALL_SCALE), (1, ring)):
        part = total[:, width + s * HD : width + (s + 1) * HD] * scale
        for p in range(pairs):
            for f in range(far):
                place = slice((f * pairs + p) * ANS_LEN, (f * pairs + p + 1) * ANS_LEN)
                out_ref[p * side + s, tokens + f * ANS_LEN : tokens + (f + 1) * ANS_LEN] = part[place]
    copies[-3].wait()
    chunk = lax.axis_index(SEQ) // (lax.axis_size(SEQ) // GROUPS)
    lane = lax.broadcasted_iota(jnp.int32, bias_ref.shape, 1)
    bias = jnp.zeros(bias_ref.shape, jnp.float32)
    for c in range(group_smem.shape[0]):
        hidden_by = jnp.where(group_smem[c] >= chunk, 0.0, NEGATIVE)
        bias = jnp.where(lane == c, hidden_by, bias)
    bias_ref[...] = bias
    copies[-2].wait()
    copies[-1].wait()


def reduce_kernel(part_ref, out_ref):
    total = jnp.sum(part_ref[...], axis=0) * (1 / part_ref.shape[0])
    out_ref[...] = jnp.broadcast_to(total[None], out_ref.shape)


def packed(mean, level):
    high = level.astype(jnp.bfloat16).astype(jnp.float32)
    middle = (level - high).astype(jnp.bfloat16).astype(jnp.float32)
    row = lax.broadcasted_iota(jnp.int32, mean.shape, 0)
    lane = lax.broadcasted_iota(jnp.int32, mean.shape, 1)
    line = lax.broadcasted_iota(jnp.int32, (ANS_LEN, HD), 0)
    lines = jnp.zeros((ANS_LEN, HD), jnp.float32)
    for place, term in enumerate((high, middle, level - high - middle)):
        spread = jnp.sum(jnp.where(lane == row, term, 0.0), axis=0, keepdims=True)
        lines = jnp.where(line == place, spread, lines)
    return jnp.concatenate([mean, lines], axis=0).astype(jnp.bfloat16)


def unpacked(state):
    state = state.astype(jnp.float32)
    rows = state.shape[-2] - ANS_LEN
    mean = state[..., :rows, :]
    line = jnp.sum(state[..., rows:, :], axis=-2, keepdims=True)
    row = lax.broadcasted_iota(jnp.int32, mean.shape, mean.ndim - 2)
    lane = lax.broadcasted_iota(jnp.int32, mean.shape, mean.ndim - 1)
    return mean, jnp.sum(jnp.where(lane == row, line, 0.0), axis=-1, keepdims=True)


def merged(mean, level):
    best = jnp.max(level, axis=0)
    factor = jnp.exp(level - best[None])
    total = jnp.sum(factor, axis=0)
    return jnp.sum(mean * factor, axis=0) / total, best + jnp.log(total)


def attend_kernel(query_ref, cache_ref, other_ref, bias_ref, out_ref):
    scale = HD ** (-0.5)
    side, far, lo, rows, _ = out_ref.shape
    rows -= ANS_LEN
    halves = far
    assert ROW_BLOCK == lo * rows
    cores = lax.axis_size("core")
    cands = rows // ANS_LEN
    row = lax.broadcasted_iota(jnp.int32, (ROW_BLOCK, HD), 0)
    lane = lax.broadcasted_iota(jnp.int32, (ROW_BLOCK, HD), 1)
    caches = (cache_ref, other_ref)
    steps = [(r, cache) for r in range(side) for cache in caches]

    def scored(step):
        r, cache = step
        parts = query_ref[r * halves * lo : (r + 1) * halves * lo, :rows]
        query = jnp.sum(parts.reshape(halves, lo, rows, HD), axis=0).reshape(ROW_BLOCK, HD)
        query = (query * (1 / SMALL_SCALE)).astype(jnp.bfloat16)
        return dot_transposed(query, cache[0])

    ahead = scored(steps[0])
    held = []
    for i, (r, cache) in enumerate(steps):
        scores = ahead
        if i + 1 < len(steps):
            ahead = scored(steps[i + 1])
        top = jnp.max(scores, axis=1, keepdims=True)
        weights = jnp.exp2((scores - top) * (scale * LOG2E))
        total = jnp.sum(weights, axis=1, keepdims=True)
        held.append((top * scale, total, dot(weights.astype(jnp.bfloat16), cache[1])))
        if len(held) < len(caches):
            continue
        top = jnp.maximum(held[0][0], held[1][0])
        factors = [jnp.exp(part[0] - top) for part in held]
        total = held[0][1] * factors[0] + held[1][1] * factors[1]
        mean = (held[0][2] * factors[0] + held[1][2] * factors[1]) / total
        held = []
        place = (row + r * ROW_BLOCK) // ANS_LEN
        cand = place // cands % lo * cores + lax.axis_index("core")
        candidate = cand * cands + place % cands
        bias = jnp.sum(jnp.where(lane == candidate, bias_ref[0:1, :], 0.0), axis=1, keepdims=True)
        level = top + jnp.log(total) + bias
        for j in range(lo):
            part = slice(j * rows, (j + 1) * rows)
            state = packed(mean[part], level[part])
            for f in range(far):
                out_ref[r, f, j] = state


def merge_kernel(state_ref, own_ref, out_ref):
    mean, level = merged(*unpacked(state_ref[...]))
    halves, pairs, _ = (lax.axis_size(name) for name in SEQ)
    rows = pairs * ANS_LEN
    tokens = mean.shape[0]

    def own(s, part, scale):
        lo = lax.axis_size("lo")
        place = s * halves * lo + lax.axis_index("lo")
        total = own_ref[place, part]
        for half in range(1, halves):
            total = total + own_ref[place + half * lo, part]
        return (total * (1 / scale)).astype(jnp.bfloat16)

    query = own(lax.axis_index("side"), slice(0, tokens), SMALL_SCALE)
    key = own(0, slice(tokens, None), KEY_SCALE)
    value = own(1, slice(tokens, None), SMALL_SCALE)
    scores = dot_transposed(query, key) * HD ** (-0.5)
    row = lax.broadcasted_iota(jnp.int32, scores.shape, 0)
    column = lax.broadcasted_iota(jnp.int32, scores.shape, 1)
    shown = (row // rows == column // ANS_LEN) & (column % ANS_LEN <= row % ANS_LEN)
    scores = jnp.where(shown, scores, NEGATIVE)
    top = jnp.max(scores, axis=1, keepdims=True)
    weights = jnp.where(shown, jnp.exp(scores - top), 0.0)
    total = jnp.sum(weights, axis=1, keepdims=True)
    own_mean = dot(weights.astype(jnp.bfloat16), value) / total
    own_level = top + jnp.log(total)
    row = lax.broadcasted_iota(jnp.int32, level.shape, 0)
    mine = row // ANS_LEN % pairs == lax.axis_index("pair")
    own_level = jnp.where(mine, own_level, NEGATIVE)
    mean, level = merged(jnp.stack([mean, own_mean]), jnp.stack([level, own_level]))
    out_ref[...] = jnp.broadcast_to(packed(mean, level)[None], out_ref.shape)


def output_kernel(state_ref, weight_ref, out_ref):
    blocks, _, width = out_ref.shape
    columns = [merged(*unpacked(state_ref[:, s]))[0] for s in range(state_ref.shape[1])]
    attention = jnp.concatenate(columns, axis=1).astype(jnp.bfloat16)
    out = dot(attention, weight_ref[...])
    for block in range(blocks):
        out_ref[block] = out[:, block * width : (block + 1) * width].astype(jnp.bfloat16)


def sum_kernel(part_ref, out_ref):
    out_ref[...] = jnp.sum(part_ref[...].astype(jnp.float32), axis=0).astype(out_ref.dtype)


def body(
    hidden, query_weight, key_weight, value_weight, out_weight, key_cache, value_cache, cand_group
):
    tok_dev, feat_dev = hidden.shape
    heads_dev = query_weight.shape[1] // HD
    head, lo = lax.axis_size("head"), lax.axis_size("lo")
    far, pairs, side = (lax.axis_size(name) for name in SEQ)
    shard_len = key_cache.shape[0]
    bf16, f32 = jnp.bfloat16, jnp.float32
    rows = tok_dev * heads_dev * lo
    columns = out_weight.shape[1] // head

    inputs = (hidden, query_weight, key_weight, value_weight, cand_group, key_cache, value_cache)
    inputs = [pltpu.with_memory_space_constraint(x, pltpu.HBM) for x in inputs]
    partial, bias, cache = pl.pallas_call(
        project_kernel,
        out_shape=(
            jax.ShapeDtypeStruct((pairs * side, tok_dev + far * ANS_LEN, HD), f32),
            jax.ShapeDtypeStruct((ANS_LEN, HD), f32),
            jax.ShapeDtypeStruct((2, *key_cache.shape), bf16),
        ),
        in_specs=[HBM] * 7,
        out_specs=(VMEM, VMEM, HBM),
        scratch_shapes=[
            pltpu.VMEM(hidden.shape, bf16),
            pltpu.VMEM((feat_dev, (heads_dev + 2) * HD), bf16),
            pltpu.SMEM(cand_group.shape, jnp.int32),
            pltpu.SemaphoreType.DMA((11,)),
        ],
        compiler_params=pltpu.CompilerParams(vmem_limit_bytes=40 * 1024 * 1024),
        cost_estimate=pl.CostEstimate(
            flops=2 * tok_dev * feat_dev * (heads_dev + 2) * HD,
            bytes_accessed=2 * feat_dev * (tok_dev + (heads_dev + 2) * HD),
            transcendentals=0,
        ),
    )(*inputs)
    other = lax.ppermute(cache, "core", [(0, 1), (1, 0)])
    partial = lax.all_to_all(partial.astype(jnp.float16), ("pair", "side"), 0, 0, tiled=True)
    near = far * side * lo
    queries = call(
        reduce_kernel,
        jax.ShapeDtypeStruct((near, *partial.shape[1:]), f32),
        [VMEM],
        flops=partial.size,
        bytes_accessed=partial.size * 4,
        transcendentals=0,
    )(partial.astype(f32))
    queries = queries.astype(jnp.float16)
    queries = lax.all_to_all(queries, ("side", "far", "lo"), 0, 0, tiled=True).astype(f32)
    state = call(
        attend_kernel,
        jax.ShapeDtypeStruct((side, far, lo, tok_dev + ANS_LEN, HD), bf16),
        [VMEM] * 4,
        flops=8 * rows * shard_len * HD,
        bytes_accessed=8 * shard_len * HD,
        transcendentals=2 * rows * shard_len,
    )(queries, cache, other, bias)
    state = state.reshape(near, tok_dev + ANS_LEN, HD)
    state = lax.all_to_all(state, ("side", "far", "lo"), 0, 0, tiled=True)
    state = call(
        merge_kernel,
        jax.ShapeDtypeStruct((side * pairs, tok_dev + ANS_LEN, HD), bf16),
        [VMEM] * 2,
        flops=4 * state.size,
        bytes_accessed=2 * state.size,
        transcendentals=0,
    )(state, queries)
    state = lax.all_to_all(state, ("pair", "side"), 0, 0, tiled=True)
    projected = call(
        output_kernel,
        jax.ShapeDtypeStruct((head, tok_dev, columns), bf16),
        [VMEM] * 2,
        flops=2 * tok_dev * out_weight.size,
        bytes_accessed=2 * out_weight.size,
        transcendentals=0,
    )(state.reshape(pairs, side, tok_dev + ANS_LEN, HD), out_weight)
    projected = lax.all_to_all(projected, "head", 0, 0, tiled=True)
    return call(
        sum_kernel,
        jax.ShapeDtypeStruct((tok_dev, columns), bf16),
        [VMEM],
        flops=projected.size,
        bytes_accessed=2 * projected.size,
        transcendentals=0,
    )(projected)


def solution(mesh):
    seq, head, cand = (mesh.shape[name] for name in ("seq", "head", "cand"))
    parts = jax.sharding.Mesh(
        mesh.devices.reshape(2, seq // 4, 2, head, cand // 2, 2), (*SEQ, "head", *CAND)
    )
    in_specs = (
        P(CAND, SEQ),
        P(SEQ, "head"),
        P(SEQ, None),
        P(SEQ, None),
        P("head", SEQ),
        P((*SEQ, *CAND), None),
        P((*SEQ, *CAND), None),
        P(),
    )
    out_specs = P(CAND, (*SEQ, "head"))
    return jax.shard_map(body, mesh=parts, in_specs=in_specs, out_specs=out_specs, check_vma=False)
```

```python
import math

import jax
import jax.numpy as jnp
from jax import lax
from jax.experimental import pallas as pl
from jax.experimental.pallas import tpu as pltpu
from jax.sharding import PartitionSpec as P

HD = 128
GROUPS = 8
ANS_LEN = 8
ROW_BLOCK = 128

NEGATIVE = -1e30
LOG2E = math.log2(math.e)
SMALL_SCALE = 16.0
KEY_SCALE = 2.0

VMEM = pl.BlockSpec(memory_space=pltpu.VMEM)
HBM = pl.BlockSpec(memory_space=pltpu.HBM)

PAIR = ("high", "low")
SEQ = ("far", *PAIR, "side")
RING = ("side", *PAIR[::-1])
HEAD = ("head2", "head1", "head0")
CAND = ("lo", "core")


def call(kernel, out_shape, in_specs, **cost):
    return pl.pallas_call(
        kernel,
        out_shape=out_shape,
        in_specs=in_specs,
        out_specs=jax.tree.map(lambda _: VMEM, out_shape),
        compiler_params=pltpu.CompilerParams(vmem_limit_bytes=40 * 1024 * 1024),
        cost_estimate=pl.CostEstimate(**cost),
    )


def reverse(place, count):
    out = 0
    while count > 1:
        out, place, count = 2 * out + place % 2, place // 2, count // 2
    return out


def dot(a, b):
    return jnp.dot(a, b, preferred_element_type=jnp.float32)


def dot_transposed(a, b):
    return lax.dot_general(a, b, (((1,), (1,)), ((), ())), preferred_element_type=jnp.float32)


def project_kernel(
    hidden_hbm, query_hbm, key_hbm, value_hbm, group_hbm, key_cache, value_cache,
    out_ref, bias_ref, cache_hbm, hidden_ref, weight_ref, group_smem, sems,
):
    far, pairs, side = (lax.axis_size(name) for name in ("far", PAIR, "side"))
    features = hidden_ref.shape[1]
    width = query_hbm.shape[1]
    halves = [pl.ds(i * (features // 2), features // 2) for i in range(2)]
    copies = []

    def start(source, target):
        copies.append(pltpu.make_async_copy(source, target, sems.at[len(copies)]))
        copies[-1].start()

    for half in halves:
        start(query_hbm.at[half, :], weight_ref.at[half, pl.ds(0, width)])
        start(hidden_hbm.at[:, half], hidden_ref.at[:, half])
        start(key_hbm.at[half, :], weight_ref.at[half, pl.ds(width, HD)])
        start(value_hbm.at[half, :], weight_ref.at[half, pl.ds(width + HD, HD)])
    start(group_hbm, group_smem)
    start(key_cache, cache_hbm.at[0])
    start(value_cache, cache_hbm.at[1])
    total = None
    for i, half in enumerate(halves):
        for copy in copies[4 * i : 4 * i + 4]:
            copy.wait()
        part = dot(hidden_ref[:, half], weight_ref[half, :])
        total = part if total is None else total + part
    ring = SMALL_SCALE * lax.axis_size(PAIR) * side
    tokens = total.shape[0]
    for h in range(side):
        for p in range(pairs):
            out_ref[h * pairs + p, :tokens] = total[:, h * HD : (h + 1) * HD] * ring
    for s, scale in ((0, ring * KEY_SCALE / SMALL_SCALE), (1, ring)):
        part = total[:, width + s * HD : width + (s + 1) * HD] * scale
        for p in range(pairs):
            for f in range(far):
                place = slice((f * pairs + p) * ANS_LEN, (f * pairs + p + 1) * ANS_LEN)
                target = s * pairs + reverse(p, pairs)
                out_ref[target, tokens + f * ANS_LEN : tokens + (f + 1) * ANS_LEN] = part[place]
    copies[-3].wait()
    chunk = lax.axis_index(SEQ) // (lax.axis_size(SEQ) // GROUPS)
    lane = lax.broadcasted_iota(jnp.int32, bias_ref.shape, 1)
    bias = jnp.zeros(bias_ref.shape, jnp.float32)
    for c in range(group_smem.shape[0]):
        hidden_by = jnp.where(group_smem[c] >= chunk, 0.0, NEGATIVE)
        bias = jnp.where(lane == c, hidden_by, bias)
    bias_ref[...] = bias
    copies[-2].wait()
    copies[-1].wait()


def reduce_kernel(part_ref, out_ref):
    total = jnp.sum(part_ref[...], axis=0) * (1 / part_ref.shape[0])
    out_ref[...] = jnp.broadcast_to(total[None], out_ref.shape)


def packed(mean, level):
    high = level.astype(jnp.bfloat16).astype(jnp.float32)
    middle = (level - high).astype(jnp.bfloat16).astype(jnp.float32)
    row = lax.broadcasted_iota(jnp.int32, mean.shape, 0)
    lane = lax.broadcasted_iota(jnp.int32, mean.shape, 1)
    line = lax.broadcasted_iota(jnp.int32, (ANS_LEN, HD), 0)
    lines = jnp.zeros((ANS_LEN, HD), jnp.float32)
    for place, term in enumerate((high, middle, level - high - middle)):
        spread = jnp.sum(jnp.where(lane == row, term, 0.0), axis=0, keepdims=True)
        lines = jnp.where(line == place, spread, lines)
    return jnp.concatenate([mean, lines], axis=0).astype(jnp.bfloat16)


def unpacked(state):
    state = state.astype(jnp.float32)
    rows = state.shape[-2] - ANS_LEN
    mean = state[..., :rows, :]
    line = jnp.sum(state[..., rows:, :], axis=-2, keepdims=True)
    row = lax.broadcasted_iota(jnp.int32, mean.shape, mean.ndim - 2)
    lane = lax.broadcasted_iota(jnp.int32, mean.shape, mean.ndim - 1)
    return mean, jnp.sum(jnp.where(lane == row, line, 0.0), axis=-1, keepdims=True)


def merged(mean, level):
    best = jnp.max(level, axis=0)
    factor = jnp.exp(level - best[None])
    total = jnp.sum(factor, axis=0)
    return jnp.sum(mean * factor, axis=0) / total, best + jnp.log(total)


def attend_kernel(query_ref, cache_ref, other_ref, bias_ref, out_ref):
    scale = HD ** (-0.5)
    side, far, lo, rows, _ = out_ref.shape
    rows -= ANS_LEN
    halves = far
    assert ROW_BLOCK == lo * rows
    cores = lax.axis_size("core")
    cands = rows // ANS_LEN
    row = lax.broadcasted_iota(jnp.int32, (ROW_BLOCK, HD), 0)
    lane = lax.broadcasted_iota(jnp.int32, (ROW_BLOCK, HD), 1)
    caches = (cache_ref, other_ref)
    steps = [(r, cache) for r in range(side) for cache in caches]

    def scored(step):
        r, cache = step
        parts = query_ref[r * halves * lo : (r + 1) * halves * lo, :rows]
        query = jnp.sum(parts.reshape(halves, lo, rows, HD), axis=0).reshape(ROW_BLOCK, HD)
        query = (query * (1 / SMALL_SCALE)).astype(jnp.bfloat16)
        return dot_transposed(query, cache[0])

    ahead = scored(steps[0])
    held = []
    for i, (r, cache) in enumerate(steps):
        scores = ahead
        if i + 1 < len(steps):
            ahead = scored(steps[i + 1])
        top = jnp.max(scores, axis=1, keepdims=True)
        weights = jnp.exp2((scores - top) * (scale * LOG2E))
        total = jnp.sum(weights, axis=1, keepdims=True)
        held.append((top * scale, total, dot(weights.astype(jnp.bfloat16), cache[1])))
        if len(held) < len(caches):
            continue
        top = jnp.maximum(held[0][0], held[1][0])
        factors = [jnp.exp(part[0] - top) for part in held]
        total = held[0][1] * factors[0] + held[1][1] * factors[1]
        mean = (held[0][2] * factors[0] + held[1][2] * factors[1]) / total
        held = []
        place = (row + r * ROW_BLOCK) // ANS_LEN
        cand = place // cands % lo * cores + lax.axis_index("core")
        candidate = cand * cands + place % cands
        bias = jnp.sum(jnp.where(lane == candidate, bias_ref[0:1, :], 0.0), axis=1, keepdims=True)
        level = top + jnp.log(total) + bias
        for j in range(lo):
            part = slice(j * rows, (j + 1) * rows)
            state = packed(mean[part], level[part])
            for f in range(far):
                out_ref[r, f, j] = state


def merge_kernel(state_ref, own_ref, out_ref):
    mean, level = merged(*unpacked(state_ref[...]))
    halves, pairs = lax.axis_size("far"), lax.axis_size(PAIR)
    rows = pairs * ANS_LEN
    tokens = mean.shape[0]

    def own(s, part, scale):
        lo = lax.axis_size("lo")
        place = s * halves * lo + lax.axis_index("lo")
        total = own_ref[place, part]
        for half in range(1, halves):
            total = total + own_ref[place + half * lo, part]
        return (total * (1 / scale)).astype(jnp.bfloat16)

    query = own(lax.axis_index("side"), slice(0, tokens), SMALL_SCALE)
    key = own(0, slice(tokens, None), KEY_SCALE)
    value = own(1, slice(tokens, None), SMALL_SCALE)
    scores = dot_transposed(query, key) * HD ** (-0.5)
    row = lax.broadcasted_iota(jnp.int32, scores.shape, 0)
    column = lax.broadcasted_iota(jnp.int32, scores.shape, 1)
    shown = (row // rows == column // ANS_LEN) & (column % ANS_LEN <= row % ANS_LEN)
    scores = jnp.where(shown, scores, NEGATIVE)
    top = jnp.max(scores, axis=1, keepdims=True)
    weights = jnp.where(shown, jnp.exp(scores - top), 0.0)
    total = jnp.sum(weights, axis=1, keepdims=True)
    own_mean = dot(weights.astype(jnp.bfloat16), value) / total
    own_level = top + jnp.log(total)
    row = lax.broadcasted_iota(jnp.int32, level.shape, 0)
    mine = row // ANS_LEN % pairs == lax.axis_index(PAIR)
    own_level = jnp.where(mine, own_level, NEGATIVE)
    mean, level = merged(jnp.stack([mean, own_mean]), jnp.stack([level, own_level]))
    out_ref[...] = jnp.broadcast_to(packed(mean, level)[None], out_ref.shape)


def output_kernel(state_ref, weight_ref, out_ref):
    blocks, _, width = out_ref.shape
    columns = [merged(*unpacked(state_ref[s]))[0] for s in range(state_ref.shape[0])]
    attention = jnp.concatenate(columns, axis=1).astype(jnp.bfloat16)
    out = dot(attention, weight_ref[...])
    for block in range(blocks):
        place = reverse(block, blocks)
        out_ref[block] = out[:, place * width : (place + 1) * width].astype(jnp.bfloat16)


def sum_kernel(part_ref, out_ref):
    out_ref[...] = jnp.sum(part_ref[...].astype(jnp.float32), axis=0).astype(out_ref.dtype)


def body(
    hidden, query_weight, key_weight, value_weight, out_weight, key_cache, value_cache, cand_group
):
    tok_dev, feat_dev = hidden.shape
    heads_dev = query_weight.shape[1] // HD
    head, lo = lax.axis_size(HEAD), lax.axis_size("lo")
    far, pairs, side = (lax.axis_size(name) for name in ("far", PAIR, "side"))
    shard_len = key_cache.shape[0]
    bf16, f32 = jnp.bfloat16, jnp.float32
    rows = tok_dev * heads_dev * lo
    columns = out_weight.shape[1] // head

    inputs = (hidden, query_weight, key_weight, value_weight, cand_group, key_cache, value_cache)
    inputs = [pltpu.with_memory_space_constraint(x, pltpu.HBM) for x in inputs]
    partial, bias, cache = pl.pallas_call(
        project_kernel,
        out_shape=(
            jax.ShapeDtypeStruct((pairs * side, tok_dev + far * ANS_LEN, HD), f32),
            jax.ShapeDtypeStruct((ANS_LEN, HD), f32),
            jax.ShapeDtypeStruct((2, *key_cache.shape), bf16),
        ),
        in_specs=[HBM] * 7,
        out_specs=(VMEM, VMEM, HBM),
        scratch_shapes=[
            pltpu.VMEM(hidden.shape, bf16),
            pltpu.VMEM((feat_dev, (heads_dev + 2) * HD), bf16),
            pltpu.SMEM(cand_group.shape, jnp.int32),
            pltpu.SemaphoreType.DMA((11,)),
        ],
        compiler_params=pltpu.CompilerParams(vmem_limit_bytes=40 * 1024 * 1024),
        cost_estimate=pl.CostEstimate(
            flops=2 * tok_dev * feat_dev * (heads_dev + 2) * HD,
            bytes_accessed=2 * feat_dev * (tok_dev + (heads_dev + 2) * HD),
            transcendentals=0,
        ),
    )(*inputs)
    other = lax.ppermute(cache, "core", [(0, 1), (1, 0)])
    partial = lax.all_to_all(partial.astype(jnp.float16), RING, 0, 0, tiled=True)
    near = far * side * lo
    queries = call(
        reduce_kernel,
        jax.ShapeDtypeStruct((near, *partial.shape[1:]), f32),
        [VMEM],
        flops=partial.size,
        bytes_accessed=partial.size * 4,
        transcendentals=0,
    )(partial.astype(f32))
    queries = queries.astype(jnp.float16)
    queries = lax.all_to_all(queries, ("side", "far", "lo"), 0, 0, tiled=True).astype(f32)
    state = call(
        attend_kernel,
        jax.ShapeDtypeStruct((side, far, lo, tok_dev + ANS_LEN, HD), bf16),
        [VMEM] * 4,
        flops=8 * rows * shard_len * HD,
        bytes_accessed=8 * shard_len * HD,
        transcendentals=2 * rows * shard_len,
    )(queries, cache, other, bias)
    state = state.reshape(near, tok_dev + ANS_LEN, HD)
    state = lax.all_to_all(state, ("side", "far", "lo"), 0, 0, tiled=True)
    state = call(
        merge_kernel,
        jax.ShapeDtypeStruct((side * pairs, tok_dev + ANS_LEN, HD), bf16),
        [VMEM] * 2,
        flops=4 * state.size,
        bytes_accessed=2 * state.size,
        transcendentals=0,
    )(state, queries)
    state = lax.all_to_all(state, RING, 0, 0, tiled=True)
    projected = call(
        output_kernel,
        jax.ShapeDtypeStruct((head, tok_dev, columns), bf16),
        [VMEM] * 2,
        flops=2 * tok_dev * out_weight.size,
        bytes_accessed=2 * out_weight.size,
        transcendentals=0,
    )(state.reshape(side, pairs, tok_dev + ANS_LEN, HD), out_weight)
    projected = lax.all_to_all(projected, HEAD[::-1], 0, 0, tiled=True)
    return call(
        sum_kernel,
        jax.ShapeDtypeStruct((tok_dev, columns), bf16),
        [VMEM],
        flops=projected.size,
        bytes_accessed=2 * projected.size,
        transcendentals=0,
    )(projected)


def solution(mesh):
    seq, head, cand = (mesh.shape[name] for name in ("seq", "head", "cand"))
    parts = jax.sharding.Mesh(
        mesh.devices.reshape(2, seq // 8, 2, 2, head // 4, 2, 2, cand // 2, 2),
        (*SEQ, *HEAD, *CAND),
    )
    in_specs = (
        P(CAND, SEQ),
        P(SEQ, HEAD),
        P(SEQ, None),
        P(SEQ, None),
        P(HEAD, SEQ),
        P((*SEQ, *CAND), None),
        P((*SEQ, *CAND), None),
        P(),
    )
    out_specs = P(CAND, (*SEQ, *HEAD))
    return jax.shard_map(body, mesh=parts, in_specs=in_specs, out_specs=out_specs, check_vma=False)
```

```python
import math

import jax
import jax.numpy as jnp
from jax import lax
from jax.experimental import pallas as pl
from jax.experimental.pallas import tpu as pltpu
from jax.sharding import PartitionSpec as P

HD = 128
GROUPS = 8
ANS_LEN = 8
ROW_BLOCK = 128

NEGATIVE = -1e30
LOG2E = math.log2(math.e)
SMALL_SCALE = 16.0
KEY_SCALE = 2.0

VMEM = pl.BlockSpec(memory_space=pltpu.VMEM)
HBM = pl.BlockSpec(memory_space=pltpu.HBM)

PAIR = ("high", "low")
SEQ = ("far", *PAIR, "side")
HEAD = ("head2", "head1", "head0")
CAND = ("lo", "core")
RING = ("low", "side", "high")
HEAD_RING = ("head1", "head0", "head2")
NEAR = ("lo", "side", "far")


def call(kernel, out_shape, in_specs, **cost):
    return pl.pallas_call(
        kernel,
        out_shape=out_shape,
        in_specs=in_specs,
        out_specs=jax.tree.map(lambda _: VMEM, out_shape),
        compiler_params=pltpu.CompilerParams(vmem_limit_bytes=40 * 1024 * 1024),
        cost_estimate=pl.CostEstimate(**cost),
    )


def counted(order, **at):
    place = 0
    for name in order:
        place = place * lax.axis_size(name) + at[name]
    return place


def coordinates(names, place):
    at = {}
    for name in reversed(names):
        at[name] = place % lax.axis_size(name)
        place //= lax.axis_size(name)
    return at


def dot(a, b):
    return jnp.dot(a, b, preferred_element_type=jnp.float32)


def dot_transposed(a, b):
    return lax.dot_general(a, b, (((1,), (1,)), ((), ())), preferred_element_type=jnp.float32)


def project_kernel(
    hidden_hbm, query_hbm, key_hbm, value_hbm, group_hbm, key_cache, value_cache,
    out_ref, bias_ref, cache_hbm, hidden_ref, weight_ref, group_smem, sems,
):
    far, pairs, side = (lax.axis_size(name) for name in ("far", PAIR, "side"))
    features = hidden_ref.shape[1]
    width = query_hbm.shape[1]
    halves = [pl.ds(i * (features // 2), features // 2) for i in range(2)]
    copies = []

    def start(source, target):
        copies.append(pltpu.make_async_copy(source, target, sems.at[len(copies)]))
        copies[-1].start()

    for half in halves:
        start(query_hbm.at[half, :], weight_ref.at[half, pl.ds(0, width)])
        start(hidden_hbm.at[:, half], hidden_ref.at[:, half])
        start(key_hbm.at[half, :], weight_ref.at[half, pl.ds(width, HD)])
        start(value_hbm.at[half, :], weight_ref.at[half, pl.ds(width + HD, HD)])
    start(group_hbm, group_smem)
    start(key_cache, cache_hbm.at[0])
    start(value_cache, cache_hbm.at[1])
    total = None
    for i, half in enumerate(halves):
        for copy in copies[4 * i : 4 * i + 4]:
            copy.wait()
        part = dot(hidden_ref[:, half], weight_ref[half, :])
        total = part if total is None else total + part
    ring = SMALL_SCALE * lax.axis_size(PAIR) * side
    tokens = total.shape[0]
    for h in range(side):
        for p in range(pairs):
            target = counted(RING, side=h, **coordinates(PAIR, p))
            out_ref[target, :tokens] = total[:, h * HD : (h + 1) * HD] * ring
    for s, scale in ((0, ring * KEY_SCALE / SMALL_SCALE), (1, ring)):
        part = total[:, width + s * HD : width + (s + 1) * HD] * scale
        for p in range(pairs):
            for f in range(far):
                place = slice((f * pairs + p) * ANS_LEN, (f * pairs + p + 1) * ANS_LEN)
                target = counted(RING, side=s, **coordinates(PAIR, p))
                out_ref[target, tokens + f * ANS_LEN : tokens + (f + 1) * ANS_LEN] = part[place]
    copies[-3].wait()
    chunk = lax.axis_index(SEQ) // (lax.axis_size(SEQ) // GROUPS)
    lane = lax.broadcasted_iota(jnp.int32, bias_ref.shape, 1)
    bias = jnp.zeros(bias_ref.shape, jnp.float32)
    for c in range(group_smem.shape[0]):
        hidden_by = jnp.where(group_smem[c] >= chunk, 0.0, NEGATIVE)
        bias = jnp.where(lane == c, hidden_by, bias)
    bias_ref[...] = bias
    copies[-2].wait()
    copies[-1].wait()


def reduce_kernel(part_ref, out_ref):
    total = jnp.sum(part_ref[...], axis=0) * (1 / part_ref.shape[0])
    out_ref[...] = jnp.broadcast_to(total[None], out_ref.shape)


def packed(mean, level):
    high = level.astype(jnp.bfloat16).astype(jnp.float32)
    middle = (level - high).astype(jnp.bfloat16).astype(jnp.float32)
    row = lax.broadcasted_iota(jnp.int32, mean.shape, 0)
    lane = lax.broadcasted_iota(jnp.int32, mean.shape, 1)
    line = lax.broadcasted_iota(jnp.int32, (ANS_LEN, HD), 0)
    lines = jnp.zeros((ANS_LEN, HD), jnp.float32)
    for place, term in enumerate((high, middle, level - high - middle)):
        spread = jnp.sum(jnp.where(lane == row, term, 0.0), axis=0, keepdims=True)
        lines = jnp.where(line == place, spread, lines)
    return jnp.concatenate([mean, lines], axis=0).astype(jnp.bfloat16)


def unpacked(state):
    state = state.astype(jnp.float32)
    rows = state.shape[-2] - ANS_LEN
    mean = state[..., :rows, :]
    line = jnp.sum(state[..., rows:, :], axis=-2, keepdims=True)
    row = lax.broadcasted_iota(jnp.int32, mean.shape, mean.ndim - 2)
    lane = lax.broadcasted_iota(jnp.int32, mean.shape, mean.ndim - 1)
    return mean, jnp.sum(jnp.where(lane == row, line, 0.0), axis=-1, keepdims=True)


def merged(mean, level):
    best = jnp.max(level, axis=0)
    factor = jnp.exp(level - best[None])
    total = jnp.sum(factor, axis=0)
    return jnp.sum(mean * factor, axis=0) / total, best + jnp.log(total)


def attend_kernel(query_ref, cache_ref, other_ref, bias_ref, out_ref):
    scale = HD ** (-0.5)
    rows = out_ref.shape[1] - ANS_LEN
    far, side, lo = (lax.axis_size(name) for name in ("far", "side", "lo"))
    assert ROW_BLOCK == lo * rows
    cores = lax.axis_size("core")
    cands = rows // ANS_LEN
    row = lax.broadcasted_iota(jnp.int32, (ROW_BLOCK, HD), 0)
    lane = lax.broadcasted_iota(jnp.int32, (ROW_BLOCK, HD), 1)
    caches = (cache_ref, other_ref)
    steps = [(r, cache) for r in range(side) for cache in caches]

    def scored(step):
        r, cache = step
        parts = [
            sum(query_ref[counted(NEAR, side=r, lo=j, far=half), :rows] for half in range(far))
            for j in range(lo)
        ]
        query = (jnp.concatenate(parts, axis=0) * (1 / SMALL_SCALE)).astype(jnp.bfloat16)
        return dot_transposed(query, cache[0])

    ahead = scored(steps[0])
    held = []
    for i, (r, cache) in enumerate(steps):
        scores = ahead
        if i + 1 < len(steps):
            ahead = scored(steps[i + 1])
        top = jnp.max(scores, axis=1, keepdims=True)
        weights = jnp.exp2((scores - top) * (scale * LOG2E))
        total = jnp.sum(weights, axis=1, keepdims=True)
        held.append((top * scale, total, dot(weights.astype(jnp.bfloat16), cache[1])))
        if len(held) < len(caches):
            continue
        top = jnp.maximum(held[0][0], held[1][0])
        factors = [jnp.exp(part[0] - top) for part in held]
        total = held[0][1] * factors[0] + held[1][1] * factors[1]
        mean = (held[0][2] * factors[0] + held[1][2] * factors[1]) / total
        held = []
        place = (row + r * ROW_BLOCK) // ANS_LEN
        cand = place // cands % lo * cores + lax.axis_index("core")
        candidate = cand * cands + place % cands
        bias = jnp.sum(jnp.where(lane == candidate, bias_ref[0:1, :], 0.0), axis=1, keepdims=True)
        level = top + jnp.log(total) + bias
        for j in range(lo):
            part = slice(j * rows, (j + 1) * rows)
            state = packed(mean[part], level[part])
            for f in range(far):
                out_ref[counted(NEAR, side=r, lo=j, far=f)] = state


def merge_kernel(state_ref, own_ref, out_ref):
    mean, level = merged(*unpacked(state_ref[...]))
    halves, pairs = lax.axis_size("far"), lax.axis_size(PAIR)
    rows = pairs * ANS_LEN
    tokens = mean.shape[0]

    def own(s, part, scale):
        lo = lax.axis_index("lo")
        total = sum(own_ref[counted(NEAR, side=s, lo=lo, far=half), part] for half in range(halves))
        return (total * (1 / scale)).astype(jnp.bfloat16)

    query = own(lax.axis_index("side"), slice(0, tokens), SMALL_SCALE)
    key = own(0, slice(tokens, None), KEY_SCALE)
    value = own(1, slice(tokens, None), SMALL_SCALE)
    scores = dot_transposed(query, key) * HD ** (-0.5)
    row = lax.broadcasted_iota(jnp.int32, scores.shape, 0)
    column = lax.broadcasted_iota(jnp.int32, scores.shape, 1)
    shown = (row // rows == column // ANS_LEN) & (column % ANS_LEN <= row % ANS_LEN)
    scores = jnp.where(shown, scores, NEGATIVE)
    top = jnp.max(scores, axis=1, keepdims=True)
    weights = jnp.where(shown, jnp.exp(scores - top), 0.0)
    total = jnp.sum(weights, axis=1, keepdims=True)
    own_mean = dot(weights.astype(jnp.bfloat16), value) / total
    own_level = top + jnp.log(total)
    row = lax.broadcasted_iota(jnp.int32, level.shape, 0)
    mine = row // ANS_LEN % pairs == lax.axis_index(PAIR)
    own_level = jnp.where(mine, own_level, NEGATIVE)
    mean, level = merged(jnp.stack([mean, own_mean]), jnp.stack([level, own_level]))
    out_ref[...] = jnp.broadcast_to(packed(mean, level)[None], out_ref.shape)


def output_kernel(state_ref, weight_ref, out_ref):
    blocks, _, width = out_ref.shape
    pairs, side = lax.axis_size(PAIR), lax.axis_size("side")
    columns = []
    for h in range(side):
        sources = [counted(RING, side=h, **coordinates(PAIR, p)) for p in range(pairs)]
        columns.append(merged(*unpacked(jnp.stack([state_ref[place] for place in sources])))[0])
    attention = jnp.concatenate(columns, axis=1).astype(jnp.bfloat16)
    out = dot(attention, weight_ref[...])
    for block in range(blocks):
        place = counted(HEAD_RING, **coordinates(HEAD, block))
        out_ref[place] = out[:, block * width : (block + 1) * width].astype(jnp.bfloat16)


def sum_kernel(part_ref, out_ref):
    out_ref[...] = jnp.sum(part_ref[...].astype(jnp.float32), axis=0).astype(out_ref.dtype)


def body(
    hidden, query_weight, key_weight, value_weight, out_weight, key_cache, value_cache, cand_group
):
    tok_dev, feat_dev = hidden.shape
    heads_dev = query_weight.shape[1] // HD
    head, lo = lax.axis_size(HEAD), lax.axis_size("lo")
    far, pairs, side = (lax.axis_size(name) for name in ("far", PAIR, "side"))
    shard_len = key_cache.shape[0]
    bf16, f32 = jnp.bfloat16, jnp.float32
    rows = tok_dev * heads_dev * lo
    columns = out_weight.shape[1] // head

    inputs = (hidden, query_weight, key_weight, value_weight, cand_group, key_cache, value_cache)
    inputs = [pltpu.with_memory_space_constraint(x, pltpu.HBM) for x in inputs]
    partial, bias, cache = pl.pallas_call(
        project_kernel,
        out_shape=(
            jax.ShapeDtypeStruct((pairs * side, tok_dev + far * ANS_LEN, HD), f32),
            jax.ShapeDtypeStruct((ANS_LEN, HD), f32),
            jax.ShapeDtypeStruct((2, *key_cache.shape), bf16),
        ),
        in_specs=[HBM] * 7,
        out_specs=(VMEM, VMEM, HBM),
        scratch_shapes=[
            pltpu.VMEM(hidden.shape, bf16),
            pltpu.VMEM((feat_dev, (heads_dev + 2) * HD), bf16),
            pltpu.SMEM(cand_group.shape, jnp.int32),
            pltpu.SemaphoreType.DMA((11,)),
        ],
        compiler_params=pltpu.CompilerParams(vmem_limit_bytes=40 * 1024 * 1024),
        cost_estimate=pl.CostEstimate(
            flops=2 * tok_dev * feat_dev * (heads_dev + 2) * HD,
            bytes_accessed=2 * feat_dev * (tok_dev + (heads_dev + 2) * HD),
            transcendentals=0,
        ),
    )(*inputs)
    other = lax.ppermute(cache, "core", [(0, 1), (1, 0)])
    partial = lax.all_to_all(partial.astype(jnp.float16), RING, 0, 0, tiled=True)
    near = far * side * lo
    queries = call(
        reduce_kernel,
        jax.ShapeDtypeStruct((near, *partial.shape[1:]), f32),
        [VMEM],
        flops=partial.size,
        bytes_accessed=partial.size * 4,
        transcendentals=0,
    )(partial.astype(f32))
    queries = queries.astype(jnp.float16)
    queries = lax.all_to_all(queries, NEAR, 0, 0, tiled=True).astype(f32)
    state = call(
        attend_kernel,
        jax.ShapeDtypeStruct((near, tok_dev + ANS_LEN, HD), bf16),
        [VMEM] * 4,
        flops=8 * rows * shard_len * HD,
        bytes_accessed=8 * shard_len * HD,
        transcendentals=2 * rows * shard_len,
    )(queries, cache, other, bias)
    state = lax.all_to_all(state, NEAR, 0, 0, tiled=True)
    state = call(
        merge_kernel,
        jax.ShapeDtypeStruct((side * pairs, tok_dev + ANS_LEN, HD), bf16),
        [VMEM] * 2,
        flops=4 * state.size,
        bytes_accessed=2 * state.size,
        transcendentals=0,
    )(state, queries)
    state = lax.all_to_all(state, RING, 0, 0, tiled=True)
    projected = call(
        output_kernel,
        jax.ShapeDtypeStruct((head, tok_dev, columns), bf16),
        [VMEM] * 2,
        flops=2 * tok_dev * out_weight.size,
        bytes_accessed=2 * out_weight.size,
        transcendentals=0,
    )(state, out_weight)
    projected = lax.all_to_all(projected, HEAD_RING, 0, 0, tiled=True)
    return call(
        sum_kernel,
        jax.ShapeDtypeStruct((tok_dev, columns), bf16),
        [VMEM],
        flops=projected.size,
        bytes_accessed=2 * projected.size,
        transcendentals=0,
    )(projected)


def solution(mesh):
    seq, head, cand = (mesh.shape[name] for name in ("seq", "head", "cand"))
    parts = jax.sharding.Mesh(
        mesh.devices.reshape(2, seq // 8, 2, 2, head // 4, 2, 2, cand // 2, 2),
        (*SEQ, *HEAD, *CAND),
    )
    in_specs = (
        P(CAND, SEQ),
        P(SEQ, HEAD),
        P(SEQ, None),
        P(SEQ, None),
        P(HEAD, SEQ),
        P((*SEQ, *CAND), None),
        P((*SEQ, *CAND), None),
        P(),
    )
    out_specs = P(CAND, (*SEQ, *HEAD))
    return jax.shard_map(body, mesh=parts, in_specs=in_specs, out_specs=out_specs, check_vma=False)
```

```python
import math

import jax
import jax.numpy as jnp
from jax import lax
from jax.experimental import pallas as pl
from jax.experimental.pallas import tpu as pltpu
from jax.sharding import PartitionSpec as P

HD = 128
GROUPS = 8
ANS_LEN = 8
ROW_BLOCK = 128

NEGATIVE = -1e30
LOG2E = math.log2(math.e)
SMALL_SCALE = 16.0
KEY_SCALE = 2.0

VMEM = pl.BlockSpec(memory_space=pltpu.VMEM)
HBM = pl.BlockSpec(memory_space=pltpu.HBM)

PAIR = ("high", "low")
SEQ = ("far", *PAIR, "side")
HEAD = ("head2", "head1", "head0")
CAND = ("lo", "core")
RING = ("side", "low", "high")
RING_OUT = ("low", "high", "side")
HEAD_RING = ("head1", "head2", "head0")
NEAR = ("far", "lo", "side")


def call(kernel, out_shape, in_specs, **cost):
    return pl.pallas_call(
        kernel,
        out_shape=out_shape,
        in_specs=in_specs,
        out_specs=jax.tree.map(lambda _: VMEM, out_shape),
        compiler_params=pltpu.CompilerParams(vmem_limit_bytes=40 * 1024 * 1024),
        cost_estimate=pl.CostEstimate(**cost),
    )


def counted(order, **at):
    place = 0
    for name in order:
        place = place * lax.axis_size(name) + at[name]
    return place


def coordinates(names, place):
    at = {}
    for name in reversed(names):
        at[name] = place % lax.axis_size(name)
        place //= lax.axis_size(name)
    return at


def dot(a, b):
    return jnp.dot(a, b, preferred_element_type=jnp.float32)


def dot_transposed(a, b):
    return lax.dot_general(a, b, (((1,), (1,)), ((), ())), preferred_element_type=jnp.float32)


def project_kernel(
    hidden_hbm, query_hbm, key_hbm, value_hbm, group_hbm, key_cache, value_cache,
    out_ref, bias_ref, cache_hbm, hidden_ref, weight_ref, group_smem, sems,
):
    far, pairs, side = (lax.axis_size(name) for name in ("far", PAIR, "side"))
    features = hidden_ref.shape[1]
    width = query_hbm.shape[1]
    halves = [pl.ds(i * (features // 2), features // 2) for i in range(2)]
    copies = []

    def start(source, target):
        copies.append(pltpu.make_async_copy(source, target, sems.at[len(copies)]))
        copies[-1].start()

    for half in halves:
        start(query_hbm.at[half, :], weight_ref.at[half, pl.ds(0, width)])
        start(hidden_hbm.at[:, half], hidden_ref.at[:, half])
        start(key_hbm.at[half, :], weight_ref.at[half, pl.ds(width, HD)])
        start(value_hbm.at[half, :], weight_ref.at[half, pl.ds(width + HD, HD)])
    start(group_hbm, group_smem)
    start(key_cache, cache_hbm.at[0])
    start(value_cache, cache_hbm.at[1])
    total = None
    for i, half in enumerate(halves):
        for copy in copies[4 * i : 4 * i + 4]:
            copy.wait()
        part = dot(hidden_ref[:, half], weight_ref[half, :])
        total = part if total is None else total + part
    ring = SMALL_SCALE * lax.axis_size(PAIR) * side
    tokens = total.shape[0]
    for h in range(side):
        for p in range(pairs):
            target = counted(RING, side=h, **coordinates(PAIR, p))
            out_ref[target, :tokens] = total[:, h * HD : (h + 1) * HD] * ring
    for s, scale in ((0, ring * KEY_SCALE / SMALL_SCALE), (1, ring)):
        part = total[:, width + s * HD : width + (s + 1) * HD] * scale
        for p in range(pairs):
            for f in range(far):
                place = slice((f * pairs + p) * ANS_LEN, (f * pairs + p + 1) * ANS_LEN)
                target = counted(RING, side=s, **coordinates(PAIR, p))
                out_ref[target, tokens + f * ANS_LEN : tokens + (f + 1) * ANS_LEN] = part[place]
    copies[-3].wait()
    chunk = lax.axis_index(SEQ) // (lax.axis_size(SEQ) // GROUPS)
    lane = lax.broadcasted_iota(jnp.int32, bias_ref.shape, 1)
    bias = jnp.zeros(bias_ref.shape, jnp.float32)
    for c in range(group_smem.shape[0]):
        hidden_by = jnp.where(group_smem[c] >= chunk, 0.0, NEGATIVE)
        bias = jnp.where(lane == c, hidden_by, bias)
    bias_ref[...] = bias
    copies[-2].wait()
    copies[-1].wait()


def reduce_kernel(part_ref, out_ref):
    total = jnp.sum(part_ref[...], axis=0) * (1 / part_ref.shape[0])
    out_ref[...] = jnp.broadcast_to(total[None], out_ref.shape)


def packed(mean, level):
    high = level.astype(jnp.bfloat16).astype(jnp.float32)
    middle = (level - high).astype(jnp.bfloat16).astype(jnp.float32)
    row = lax.broadcasted_iota(jnp.int32, mean.shape, 0)
    lane = lax.broadcasted_iota(jnp.int32, mean.shape, 1)
    line = lax.broadcasted_iota(jnp.int32, (ANS_LEN, HD), 0)
    lines = jnp.zeros((ANS_LEN, HD), jnp.float32)
    for place, term in enumerate((high, middle, level - high - middle)):
        spread = jnp.sum(jnp.where(lane == row, term, 0.0), axis=0, keepdims=True)
        lines = jnp.where(line == place, spread, lines)
    return jnp.concatenate([mean, lines], axis=0).astype(jnp.bfloat16)


def unpacked(state):
    state = state.astype(jnp.float32)
    rows = state.shape[-2] - ANS_LEN
    mean = state[..., :rows, :]
    line = jnp.sum(state[..., rows:, :], axis=-2, keepdims=True)
    row = lax.broadcasted_iota(jnp.int32, mean.shape, mean.ndim - 2)
    lane = lax.broadcasted_iota(jnp.int32, mean.shape, mean.ndim - 1)
    return mean, jnp.sum(jnp.where(lane == row, line, 0.0), axis=-1, keepdims=True)


def merged(mean, level):
    best = jnp.max(level, axis=0)
    factor = jnp.exp(level - best[None])
    total = jnp.sum(factor, axis=0)
    return jnp.sum(mean * factor, axis=0) / total, best + jnp.log(total)


def attend_kernel(query_ref, cache_ref, other_ref, bias_ref, out_ref):
    scale = HD ** (-0.5)
    rows = out_ref.shape[1] - ANS_LEN
    far, side, lo = (lax.axis_size(name) for name in ("far", "side", "lo"))
    assert ROW_BLOCK == lo * rows
    cores = lax.axis_size("core")
    cands = rows // ANS_LEN
    row = lax.broadcasted_iota(jnp.int32, (ROW_BLOCK, HD), 0)
    lane = lax.broadcasted_iota(jnp.int32, (ROW_BLOCK, HD), 1)
    caches = (cache_ref, other_ref)
    steps = [(r, cache) for r in range(side) for cache in caches]

    def scored(step):
        r, cache = step
        parts = [
            sum(query_ref[counted(NEAR, side=r, lo=j, far=half), :rows] for half in range(far))
            for j in range(lo)
        ]
        query = (jnp.concatenate(parts, axis=0) * (1 / SMALL_SCALE)).astype(jnp.bfloat16)
        return dot_transposed(query, cache[0])

    ahead = scored(steps[0])
    held = []
    for i, (r, cache) in enumerate(steps):
        scores = ahead
        if i + 1 < len(steps):
            ahead = scored(steps[i + 1])
        top = jnp.max(scores, axis=1, keepdims=True)
        weights = jnp.exp2((scores - top) * (scale * LOG2E))
        total = jnp.sum(weights, axis=1, keepdims=True)
        held.append((top * scale, total, dot(weights.astype(jnp.bfloat16), cache[1])))
        if len(held) < len(caches):
            continue
        top = jnp.maximum(held[0][0], held[1][0])
        factors = [jnp.exp(part[0] - top) for part in held]
        total = held[0][1] * factors[0] + held[1][1] * factors[1]
        mean = (held[0][2] * factors[0] + held[1][2] * factors[1]) / total
        held = []
        place = (row + r * ROW_BLOCK) // ANS_LEN
        cand = place // cands % lo * cores + lax.axis_index("core")
        candidate = cand * cands + place % cands
        bias = jnp.sum(jnp.where(lane == candidate, bias_ref[0:1, :], 0.0), axis=1, keepdims=True)
        level = top + jnp.log(total) + bias
        for j in range(lo):
            part = slice(j * rows, (j + 1) * rows)
            state = packed(mean[part], level[part])
            for f in range(far):
                out_ref[counted(NEAR, side=r, lo=j, far=f)] = state


def merge_kernel(state_ref, own_ref, out_ref):
    mean, level = merged(*unpacked(state_ref[...]))
    halves, pairs = lax.axis_size("far"), lax.axis_size(PAIR)
    rows = pairs * ANS_LEN
    tokens = mean.shape[0]

    def own(s, part, scale):
        lo = lax.axis_index("lo")
        total = sum(own_ref[counted(NEAR, side=s, lo=lo, far=half), part] for half in range(halves))
        return (total * (1 / scale)).astype(jnp.bfloat16)

    query = own(lax.axis_index("side"), slice(0, tokens), SMALL_SCALE)
    key = own(0, slice(tokens, None), KEY_SCALE)
    value = own(1, slice(tokens, None), SMALL_SCALE)
    scores = dot_transposed(query, key) * HD ** (-0.5)
    row = lax.broadcasted_iota(jnp.int32, scores.shape, 0)
    column = lax.broadcasted_iota(jnp.int32, scores.shape, 1)
    shown = (row // rows == column // ANS_LEN) & (column % ANS_LEN <= row % ANS_LEN)
    scores = jnp.where(shown, scores, NEGATIVE)
    top = jnp.max(scores, axis=1, keepdims=True)
    weights = jnp.where(shown, jnp.exp(scores - top), 0.0)
    total = jnp.sum(weights, axis=1, keepdims=True)
    own_mean = dot(weights.astype(jnp.bfloat16), value) / total
    own_level = top + jnp.log(total)
    row = lax.broadcasted_iota(jnp.int32, level.shape, 0)
    mine = row // ANS_LEN % pairs == lax.axis_index(PAIR)
    own_level = jnp.where(mine, own_level, NEGATIVE)
    mean, level = merged(jnp.stack([mean, own_mean]), jnp.stack([level, own_level]))
    out_ref[...] = jnp.broadcast_to(packed(mean, level)[None], out_ref.shape)


def output_kernel(state_ref, weight_ref, out_ref):
    blocks, _, width = out_ref.shape
    pairs, side = lax.axis_size(PAIR), lax.axis_size("side")
    columns = []
    for h in range(side):
        sources = [counted(RING_OUT, side=h, **coordinates(PAIR, p)) for p in range(pairs)]
        columns.append(merged(*unpacked(jnp.stack([state_ref[place] for place in sources])))[0])
    attention = jnp.concatenate(columns, axis=1).astype(jnp.bfloat16)
    out = dot(attention, weight_ref[...])
    for block in range(blocks):
        place = counted(HEAD_RING, **coordinates(HEAD, block))
        out_ref[place] = out[:, block * width : (block + 1) * width].astype(jnp.bfloat16)


def sum_kernel(part_ref, out_ref):
    out_ref[...] = jnp.sum(part_ref[...].astype(jnp.float32), axis=0).astype(out_ref.dtype)


def body(
    hidden, query_weight, key_weight, value_weight, out_weight, key_cache, value_cache, cand_group
):
    tok_dev, feat_dev = hidden.shape
    heads_dev = query_weight.shape[1] // HD
    head, lo = lax.axis_size(HEAD), lax.axis_size("lo")
    far, pairs, side = (lax.axis_size(name) for name in ("far", PAIR, "side"))
    shard_len = key_cache.shape[0]
    bf16, f32 = jnp.bfloat16, jnp.float32
    rows = tok_dev * heads_dev * lo
    columns = out_weight.shape[1] // head

    inputs = (hidden, query_weight, key_weight, value_weight, cand_group, key_cache, value_cache)
    inputs = [pltpu.with_memory_space_constraint(x, pltpu.HBM) for x in inputs]
    partial, bias, cache = pl.pallas_call(
        project_kernel,
        out_shape=(
            jax.ShapeDtypeStruct((pairs * side, tok_dev + far * ANS_LEN, HD), f32),
            jax.ShapeDtypeStruct((ANS_LEN, HD), f32),
            jax.ShapeDtypeStruct((2, *key_cache.shape), bf16),
        ),
        in_specs=[HBM] * 7,
        out_specs=(VMEM, VMEM, HBM),
        scratch_shapes=[
            pltpu.VMEM(hidden.shape, bf16),
            pltpu.VMEM((feat_dev, (heads_dev + 2) * HD), bf16),
            pltpu.SMEM(cand_group.shape, jnp.int32),
            pltpu.SemaphoreType.DMA((11,)),
        ],
        compiler_params=pltpu.CompilerParams(vmem_limit_bytes=40 * 1024 * 1024),
        cost_estimate=pl.CostEstimate(
            flops=2 * tok_dev * feat_dev * (heads_dev + 2) * HD,
            bytes_accessed=2 * feat_dev * (tok_dev + (heads_dev + 2) * HD),
            transcendentals=0,
        ),
    )(*inputs)
    other = lax.ppermute(cache, "core", [(0, 1), (1, 0)])
    partial = lax.all_to_all(partial.astype(jnp.float16), RING, 0, 0, tiled=True)
    near = far * side * lo
    queries = call(
        reduce_kernel,
        jax.ShapeDtypeStruct((near, *partial.shape[1:]), f32),
        [VMEM],
        flops=partial.size,
        bytes_accessed=partial.size * 4,
        transcendentals=0,
    )(partial.astype(f32))
    queries = queries.astype(jnp.float16)
    queries = lax.all_to_all(queries, NEAR, 0, 0, tiled=True).astype(f32)
    state = call(
        attend_kernel,
        jax.ShapeDtypeStruct((near, tok_dev + ANS_LEN, HD), bf16),
        [VMEM] * 4,
        flops=8 * rows * shard_len * HD,
        bytes_accessed=8 * shard_len * HD,
        transcendentals=2 * rows * shard_len,
    )(queries, cache, other, bias)
    state = lax.all_to_all(state, NEAR, 0, 0, tiled=True)
    state = call(
        merge_kernel,
        jax.ShapeDtypeStruct((side * pairs, tok_dev + ANS_LEN, HD), bf16),
        [VMEM] * 2,
        flops=4 * state.size,
        bytes_accessed=2 * state.size,
        transcendentals=0,
    )(state, queries)
    state = lax.all_to_all(state, RING_OUT, 0, 0, tiled=True)
    projected = call(
        output_kernel,
        jax.ShapeDtypeStruct((head, tok_dev, columns), bf16),
        [VMEM] * 2,
        flops=2 * tok_dev * out_weight.size,
        bytes_accessed=2 * out_weight.size,
        transcendentals=0,
    )(state, out_weight)
    projected = lax.all_to_all(projected, HEAD_RING, 0, 0, tiled=True)
    return call(
        sum_kernel,
        jax.ShapeDtypeStruct((tok_dev, columns), bf16),
        [VMEM],
        flops=projected.size,
        bytes_accessed=2 * projected.size,
        transcendentals=0,
    )(projected)


def solution(mesh):
    seq, head, cand = (mesh.shape[name] for name in ("seq", "head", "cand"))
    parts = jax.sharding.Mesh(
        mesh.devices.reshape(2, seq // 8, 2, 2, head // 4, 2, 2, cand // 2, 2),
        (*SEQ, *HEAD, *CAND),
    )
    in_specs = (
        P(CAND, SEQ),
        P(SEQ, HEAD),
        P(SEQ, None),
        P(SEQ, None),
        P(HEAD, SEQ),
        P((*SEQ, *CAND), None),
        P((*SEQ, *CAND), None),
        P(),
    )
    out_specs = P(CAND, (*SEQ, *HEAD))
    return jax.shard_map(body, mesh=parts, in_specs=in_specs, out_specs=out_specs, check_vma=False)
```

```python
import math

import jax
import jax.numpy as jnp
from jax import lax
from jax.experimental import pallas as pl
from jax.experimental.pallas import tpu as pltpu
from jax.sharding import PartitionSpec as P

HD = 128
GROUPS = 8
ANS_LEN = 8
ROW_BLOCK = 128

NEGATIVE = -1e30
LOG2E = math.log2(math.e)
SMALL_SCALE = 16.0
KEY_SCALE = 2.0

VMEM = pl.BlockSpec(memory_space=pltpu.VMEM)
HBM = pl.BlockSpec(memory_space=pltpu.HBM)

PAIR = ("high", "low")
SEQ = ("far", *PAIR, "side")
RING = ("side", *PAIR[::-1])
HEAD = ("head2", "head1", "head0")
CAND = ("lo", "core")


def call(kernel, out_shape, in_specs, **cost):
    return pl.pallas_call(
        kernel,
        out_shape=out_shape,
        in_specs=in_specs,
        out_specs=jax.tree.map(lambda _: VMEM, out_shape),
        compiler_params=pltpu.CompilerParams(vmem_limit_bytes=40 * 1024 * 1024),
        cost_estimate=pl.CostEstimate(**cost),
    )


def reverse(place, count):
    out = 0
    while count > 1:
        out, place, count = 2 * out + place % 2, place // 2, count // 2
    return out


def dot(a, b):
    return jnp.dot(a, b, preferred_element_type=jnp.float32)


def dot_transposed(a, b):
    return lax.dot_general(a, b, (((1,), (1,)), ((), ())), preferred_element_type=jnp.float32)


def project_kernel(
    hidden_hbm, query_hbm, key_hbm, value_hbm, group_hbm, key_cache, value_cache,
    out_ref, bias_ref, cache_hbm, hidden_ref, weight_ref, group_smem, sems,
):
    far, pairs, side = (lax.axis_size(name) for name in ("far", PAIR, "side"))
    features = hidden_ref.shape[1]
    width = query_hbm.shape[1]
    halves = [pl.ds(i * (features // 2), features // 2) for i in range(2)]
    copies = []

    def start(source, target):
        copies.append(pltpu.make_async_copy(source, target, sems.at[len(copies)]))
        copies[-1].start()

    for half in halves:
        start(query_hbm.at[half, :], weight_ref.at[half, pl.ds(0, width)])
        start(hidden_hbm.at[:, half], hidden_ref.at[:, half])
        start(key_hbm.at[half, :], weight_ref.at[half, pl.ds(width, HD)])
        start(value_hbm.at[half, :], weight_ref.at[half, pl.ds(width + HD, HD)])
    start(group_hbm, group_smem)
    start(key_cache, cache_hbm.at[0])
    start(value_cache, cache_hbm.at[1])
    total = None
    for i, half in enumerate(halves):
        for copy in copies[4 * i : 4 * i + 4]:
            copy.wait()
        part = dot(hidden_ref[:, half], weight_ref[half, :])
        total = part if total is None else total + part
    ring = SMALL_SCALE * lax.axis_size(PAIR) * side
    tokens = total.shape[0]
    for h in range(side):
        for p in range(pairs):
            out_ref[h * pairs + p, :tokens] = total[:, h * HD : (h + 1) * HD] * ring
    for s, scale in ((0, ring * KEY_SCALE / SMALL_SCALE), (1, ring)):
        part = total[:, width + s * HD : width + (s + 1) * HD] * scale
        for p in range(pairs):
            for f in range(far):
                place = slice((f * pairs + p) * ANS_LEN, (f * pairs + p + 1) * ANS_LEN)
                target = s * pairs + reverse(p, pairs)
                out_ref[target, tokens + f * ANS_LEN : tokens + (f + 1) * ANS_LEN] = part[place]
    copies[-3].wait()
    chunk = lax.axis_index(SEQ) // (lax.axis_size(SEQ) // GROUPS)
    lane = lax.broadcasted_iota(jnp.int32, bias_ref.shape, 1)
    bias = jnp.zeros(bias_ref.shape, jnp.float32)
    for c in range(group_smem.shape[0]):
        hidden_by = jnp.where(group_smem[c] >= chunk, 0.0, NEGATIVE)
        bias = jnp.where(lane == c, hidden_by, bias)
    bias_ref[...] = bias
    copies[-2].wait()
    copies[-1].wait()


def reduce_kernel(part_ref, _, out_ref, __):
    total = jnp.sum(part_ref[...], axis=0) * (1 / part_ref.shape[0])
    out_ref[...] = jnp.broadcast_to(total[None], out_ref.shape)


def packed(mean, level):
    high = level.astype(jnp.bfloat16).astype(jnp.float32)
    middle = (level - high).astype(jnp.bfloat16).astype(jnp.float32)
    row = lax.broadcasted_iota(jnp.int32, mean.shape, 0)
    lane = lax.broadcasted_iota(jnp.int32, mean.shape, 1)
    line = lax.broadcasted_iota(jnp.int32, (ANS_LEN, HD), 0)
    lines = jnp.zeros((ANS_LEN, HD), jnp.float32)
    for place, term in enumerate((high, middle, level - high - middle)):
        spread = jnp.sum(jnp.where(lane == row, term, 0.0), axis=0, keepdims=True)
        lines = jnp.where(line == place, spread, lines)
    return jnp.concatenate([mean, lines], axis=0).astype(jnp.bfloat16)


def unpacked(state):
    state = state.astype(jnp.float32)
    rows = state.shape[-2] - ANS_LEN
    mean = state[..., :rows, :]
    line = jnp.sum(state[..., rows:, :], axis=-2, keepdims=True)
    row = lax.broadcasted_iota(jnp.int32, mean.shape, mean.ndim - 2)
    lane = lax.broadcasted_iota(jnp.int32, mean.shape, mean.ndim - 1)
    return mean, jnp.sum(jnp.where(lane == row, line, 0.0), axis=-1, keepdims=True)


def merged(mean, level):
    best = jnp.max(level, axis=0)
    factor = jnp.exp(level - best[None])
    total = jnp.sum(factor, axis=0)
    return jnp.sum(mean * factor, axis=0) / total, best + jnp.log(total)


def attend_kernel(query_ref, cache_ref, other_ref, bias_ref, out_ref):
    scale = HD ** (-0.5)
    side, far, lo, rows, _ = out_ref.shape
    rows -= ANS_LEN
    halves = far
    assert ROW_BLOCK == lo * rows
    cores = lax.axis_size("core")
    cands = rows // ANS_LEN
    row = lax.broadcasted_iota(jnp.int32, (ROW_BLOCK, HD), 0)
    lane = lax.broadcasted_iota(jnp.int32, (ROW_BLOCK, HD), 1)
    caches = (cache_ref, other_ref)
    steps = [(r, cache) for r in range(side) for cache in caches]

    def scored(step):
        r, cache = step
        parts = query_ref[r * halves * lo : (r + 1) * halves * lo, :rows]
        query = jnp.sum(parts.reshape(halves, lo, rows, HD), axis=0).reshape(ROW_BLOCK, HD)
        query = (query * (1 / SMALL_SCALE)).astype(jnp.bfloat16)
        return dot_transposed(query, cache[0])

    ahead = scored(steps[0])
    held = []
    for i, (r, cache) in enumerate(steps):
        scores = ahead
        if i + 1 < len(steps):
            ahead = scored(steps[i + 1])
        top = jnp.max(scores, axis=1, keepdims=True)
        weights = jnp.exp2((scores - top) * (scale * LOG2E))
        total = jnp.sum(weights, axis=1, keepdims=True)
        held.append((top * scale, total, dot(weights.astype(jnp.bfloat16), cache[1])))
        if len(held) < len(caches):
            continue
        top = jnp.maximum(held[0][0], held[1][0])
        factors = [jnp.exp(part[0] - top) for part in held]
        total = held[0][1] * factors[0] + held[1][1] * factors[1]
        mean = (held[0][2] * factors[0] + held[1][2] * factors[1]) / total
        held = []
        place = (row + r * ROW_BLOCK) // ANS_LEN
        cand = place // cands % lo * cores + lax.axis_index("core")
        candidate = cand * cands + place % cands
        bias = jnp.sum(jnp.where(lane == candidate, bias_ref[0:1, :], 0.0), axis=1, keepdims=True)
        level = top + jnp.log(total) + bias
        for j in range(lo):
            part = slice(j * rows, (j + 1) * rows)
            state = packed(mean[part], level[part])
            for f in range(far):
                out_ref[r, f, j] = state


def merge_kernel(state_ref, own_ref, out_ref):
    mean, level = merged(*unpacked(state_ref[...]))
    halves, pairs = lax.axis_size("far"), lax.axis_size(PAIR)
    rows = pairs * ANS_LEN
    tokens = mean.shape[0]

    def own(s, part, scale):
        lo = lax.axis_size("lo")
        place = s * halves * lo + lax.axis_index("lo")
        total = own_ref[place, part]
        for half in range(1, halves):
            total = total + own_ref[place + half * lo, part]
        return (total * (1 / scale)).astype(jnp.bfloat16)

    query = own(lax.axis_index("side"), slice(0, tokens), SMALL_SCALE)
    key = own(0, slice(tokens, None), KEY_SCALE)
    value = own(1, slice(tokens, None), SMALL_SCALE)
    scores = dot_transposed(query, key) * HD ** (-0.5)
    row = lax.broadcasted_iota(jnp.int32, scores.shape, 0)
    column = lax.broadcasted_iota(jnp.int32, scores.shape, 1)
    shown = (row // rows == column // ANS_LEN) & (column % ANS_LEN <= row % ANS_LEN)
    scores = jnp.where(shown, scores, NEGATIVE)
    top = jnp.max(scores, axis=1, keepdims=True)
    weights = jnp.where(shown, jnp.exp(scores - top), 0.0)
    total = jnp.sum(weights, axis=1, keepdims=True)
    own_mean = dot(weights.astype(jnp.bfloat16), value) / total
    own_level = top + jnp.log(total)
    row = lax.broadcasted_iota(jnp.int32, level.shape, 0)
    mine = row // ANS_LEN % pairs == lax.axis_index(PAIR)
    own_level = jnp.where(mine, own_level, NEGATIVE)
    mean, level = merged(jnp.stack([mean, own_mean]), jnp.stack([level, own_level]))
    out_ref[...] = jnp.broadcast_to(packed(mean, level)[None], out_ref.shape)


def output_kernel(state_ref, weight_ref, out_ref):
    blocks, _, width = out_ref.shape
    columns = [merged(*unpacked(state_ref[s]))[0] for s in range(state_ref.shape[0])]
    attention = jnp.concatenate(columns, axis=1).astype(jnp.bfloat16)
    out = dot(attention, weight_ref[...])
    for block in range(blocks):
        place = reverse(block, blocks)
        out_ref[block] = out[:, place * width : (place + 1) * width].astype(jnp.bfloat16)


def sum_kernel(part_ref, out_ref):
    out_ref[...] = jnp.sum(part_ref[...].astype(jnp.float32), axis=0).astype(out_ref.dtype)


def body(
    hidden, query_weight, key_weight, value_weight, out_weight, key_cache, value_cache, cand_group
):
    tok_dev, feat_dev = hidden.shape
    heads_dev = query_weight.shape[1] // HD
    head, lo = lax.axis_size(HEAD), lax.axis_size("lo")
    far, pairs, side = (lax.axis_size(name) for name in ("far", PAIR, "side"))
    shard_len = key_cache.shape[0]
    bf16, f32 = jnp.bfloat16, jnp.float32
    rows = tok_dev * heads_dev * lo
    columns = out_weight.shape[1] // head

    inputs = (hidden, query_weight, key_weight, value_weight, cand_group, key_cache, value_cache)
    inputs = [pltpu.with_memory_space_constraint(x, pltpu.HBM) for x in inputs]
    partial, bias, cache = pl.pallas_call(
        project_kernel,
        out_shape=(
            jax.ShapeDtypeStruct((pairs * side, tok_dev + far * ANS_LEN, HD), f32),
            jax.ShapeDtypeStruct((ANS_LEN, HD), f32),
            jax.ShapeDtypeStruct((2, *key_cache.shape), bf16),
        ),
        in_specs=[HBM] * 7,
        out_specs=(VMEM, VMEM, HBM),
        scratch_shapes=[
            pltpu.VMEM(hidden.shape, bf16),
            pltpu.VMEM((feat_dev, (heads_dev + 2) * HD), bf16),
            pltpu.SMEM(cand_group.shape, jnp.int32),
            pltpu.SemaphoreType.DMA((11,)),
        ],
        compiler_params=pltpu.CompilerParams(vmem_limit_bytes=40 * 1024 * 1024),
        cost_estimate=pl.CostEstimate(
            flops=2 * tok_dev * feat_dev * (heads_dev + 2) * HD,
            bytes_accessed=2 * feat_dev * (tok_dev + (heads_dev + 2) * HD),
            transcendentals=0,
        ),
    )(*inputs)
    partial = lax.all_to_all(partial.astype(jnp.float16), RING, 0, 0, tiled=True)
    near = far * side * lo
    queries, cache = pl.pallas_call(
        reduce_kernel,
        out_shape=(
            jax.ShapeDtypeStruct((near, *partial.shape[1:]), f32),
            jax.ShapeDtypeStruct(cache.shape, cache.dtype),
        ),
        in_specs=[VMEM, pl.BlockSpec(memory_space=pl.ANY)],
        out_specs=(VMEM, pl.BlockSpec(memory_space=pl.ANY)),
        input_output_aliases={1: 1},
        compiler_params=pltpu.CompilerParams(vmem_limit_bytes=40 * 1024 * 1024),
        cost_estimate=pl.CostEstimate(
            flops=partial.size, bytes_accessed=partial.size * 4, transcendentals=0
        ),
    )(partial.astype(f32), cache)
    other = lax.ppermute(cache, "core", [(0, 1), (1, 0)])
    queries = queries.astype(jnp.float16)
    queries = lax.all_to_all(queries, ("side", "far", "lo"), 0, 0, tiled=True).astype(f32)
    state = call(
        attend_kernel,
        jax.ShapeDtypeStruct((side, far, lo, tok_dev + ANS_LEN, HD), bf16),
        [VMEM] * 4,
        flops=8 * rows * shard_len * HD,
        bytes_accessed=8 * shard_len * HD,
        transcendentals=2 * rows * shard_len,
    )(queries, cache, other, bias)
    state = state.reshape(near, tok_dev + ANS_LEN, HD)
    state = lax.all_to_all(state, ("side", "far", "lo"), 0, 0, tiled=True)
    state = call(
        merge_kernel,
        jax.ShapeDtypeStruct((side * pairs, tok_dev + ANS_LEN, HD), bf16),
        [VMEM] * 2,
        flops=4 * state.size,
        bytes_accessed=2 * state.size,
        transcendentals=0,
    )(state, queries)
    state = lax.all_to_all(state, RING, 0, 0, tiled=True)
    projected = call(
        output_kernel,
        jax.ShapeDtypeStruct((head, tok_dev, columns), bf16),
        [VMEM] * 2,
        flops=2 * tok_dev * out_weight.size,
        bytes_accessed=2 * out_weight.size,
        transcendentals=0,
    )(state.reshape(side, pairs, tok_dev + ANS_LEN, HD), out_weight)
    projected = lax.all_to_all(projected, HEAD[::-1], 0, 0, tiled=True)
    return call(
        sum_kernel,
        jax.ShapeDtypeStruct((tok_dev, columns), bf16),
        [VMEM],
        flops=projected.size,
        bytes_accessed=2 * projected.size,
        transcendentals=0,
    )(projected)


def solution(mesh):
    seq, head, cand = (mesh.shape[name] for name in ("seq", "head", "cand"))
    parts = jax.sharding.Mesh(
        mesh.devices.reshape(2, seq // 8, 2, 2, head // 4, 2, 2, cand // 2, 2),
        (*SEQ, *HEAD, *CAND),
    )
    in_specs = (
        P(CAND, SEQ),
        P(SEQ, HEAD),
        P(SEQ, None),
        P(SEQ, None),
        P(HEAD, SEQ),
        P((*SEQ, *CAND), None),
        P((*SEQ, *CAND), None),
        P(),
    )
    out_specs = P(CAND, (*SEQ, *HEAD))
    return jax.shard_map(body, mesh=parts, in_specs=in_specs, out_specs=out_specs, check_vma=False)
```

```python
import math

import jax
import jax.numpy as jnp
from jax import lax
from jax.experimental import pallas as pl
from jax.experimental.pallas import tpu as pltpu
from jax.sharding import PartitionSpec as P

HD = 128
GROUPS = 8
ANS_LEN = 8
ROW_BLOCK = 128

NEGATIVE = -1e30
LOG2E = math.log2(math.e)
SMALL_SCALE = 16.0
KEY_SCALE = 2.0

VMEM = pl.BlockSpec(memory_space=pltpu.VMEM)
HBM = pl.BlockSpec(memory_space=pltpu.HBM)

PAIR = ("high", "low")
SEQ = ("far", *PAIR, "side")
RING = ("side", *PAIR[::-1])
HEAD = ("head2", "head1", "head0")
CAND = ("lo", "core")


def call(kernel, out_shape, in_specs, **cost):
    return pl.pallas_call(
        kernel,
        out_shape=out_shape,
        in_specs=in_specs,
        out_specs=jax.tree.map(lambda _: VMEM, out_shape),
        compiler_params=pltpu.CompilerParams(vmem_limit_bytes=40 * 1024 * 1024),
        cost_estimate=pl.CostEstimate(**cost),
    )


def reverse(place, count):
    out = 0
    while count > 1:
        out, place, count = 2 * out + place % 2, place // 2, count // 2
    return out


def dot(a, b):
    return jnp.dot(a, b, preferred_element_type=jnp.float32)


def dot_transposed(a, b):
    return lax.dot_general(a, b, (((1,), (1,)), ((), ())), preferred_element_type=jnp.float32)


def project_kernel(
    hidden_hbm, query_hbm, key_hbm, value_hbm, group_hbm, key_cache, value_cache,
    out_ref, bias_ref, cache_hbm, hidden_ref, weight_ref, group_smem, sems,
):
    far, pairs, side = (lax.axis_size(name) for name in ("far", PAIR, "side"))
    features = hidden_ref.shape[1]
    width = query_hbm.shape[1]
    halves = [pl.ds(i * (features // 2), features // 2) for i in range(2)]
    copies = []

    def start(source, target):
        copies.append(pltpu.make_async_copy(source, target, sems.at[len(copies)]))
        copies[-1].start()

    start(group_hbm, group_smem)
    for half in halves:
        start(query_hbm.at[half, :], weight_ref.at[half, pl.ds(0, width)])
        start(hidden_hbm.at[:, half], hidden_ref.at[:, half])
        start(key_hbm.at[half, :], weight_ref.at[half, pl.ds(width, HD)])
        start(value_hbm.at[half, :], weight_ref.at[half, pl.ds(width + HD, HD)])
    copies[0].wait()
    chunk = lax.axis_index(SEQ) // (lax.axis_size(SEQ) // GROUPS)
    lane = lax.broadcasted_iota(jnp.int32, bias_ref.shape, 1)
    bias = jnp.zeros(bias_ref.shape, jnp.float32)
    for c in range(group_smem.shape[0]):
        hidden_by = jnp.where(group_smem[c] >= chunk, 0.0, NEGATIVE)
        bias = jnp.where(lane == c, hidden_by, bias)
    bias_ref[...] = bias
    total = None
    for i, half in enumerate(halves):
        for copy in copies[4 * i + 1 : 4 * i + 5]:
            copy.wait()
        if i == 0:
            start(key_cache, cache_hbm.at[0])
            start(value_cache, cache_hbm.at[1])
        part = dot(hidden_ref[:, half], weight_ref[half, :])
        total = part if total is None else total + part
    ring = SMALL_SCALE * lax.axis_size(PAIR) * side
    tokens = total.shape[0]
    for h in range(side):
        for p in range(pairs):
            out_ref[h * pairs + p, :tokens] = total[:, h * HD : (h + 1) * HD] * ring
    for s, scale in ((0, ring * KEY_SCALE / SMALL_SCALE), (1, ring)):
        part = total[:, width + s * HD : width + (s + 1) * HD] * scale
        for p in range(pairs):
            for f in range(far):
                place = slice((f * pairs + p) * ANS_LEN, (f * pairs + p + 1) * ANS_LEN)
                target = s * pairs + reverse(p, pairs)
                out_ref[target, tokens + f * ANS_LEN : tokens + (f + 1) * ANS_LEN] = part[place]
    copies[-2].wait()
    copies[-1].wait()


def reduce_kernel(part_ref, _, out_ref, __):
    total = jnp.sum(part_ref[...], axis=0) * (1 / part_ref.shape[0])
    out_ref[...] = jnp.broadcast_to(total[None], out_ref.shape)


def packed(mean, level):
    high = level.astype(jnp.bfloat16).astype(jnp.float32)
    middle = (level - high).astype(jnp.bfloat16).astype(jnp.float32)
    row = lax.broadcasted_iota(jnp.int32, mean.shape, 0)
    lane = lax.broadcasted_iota(jnp.int32, mean.shape, 1)
    line = lax.broadcasted_iota(jnp.int32, (ANS_LEN, HD), 0)
    lines = jnp.zeros((ANS_LEN, HD), jnp.float32)
    for place, term in enumerate((high, middle, level - high - middle)):
        spread = jnp.sum(jnp.where(lane == row, term, 0.0), axis=0, keepdims=True)
        lines = jnp.where(line == place, spread, lines)
    return jnp.concatenate([mean, lines], axis=0).astype(jnp.bfloat16)


def unpacked(state):
    state = state.astype(jnp.float32)
    rows = state.shape[-2] - ANS_LEN
    mean = state[..., :rows, :]
    line = jnp.sum(state[..., rows:, :], axis=-2, keepdims=True)
    row = lax.broadcasted_iota(jnp.int32, mean.shape, mean.ndim - 2)
    lane = lax.broadcasted_iota(jnp.int32, mean.shape, mean.ndim - 1)
    return mean, jnp.sum(jnp.where(lane == row, line, 0.0), axis=-1, keepdims=True)


def merged(mean, level):
    best = jnp.max(level, axis=0)
    factor = jnp.exp(level - best[None])
    total = jnp.sum(factor, axis=0)
    return jnp.sum(mean * factor, axis=0) / total, best + jnp.log(total)


def attend_kernel(query_ref, cache_ref, other_ref, bias_ref, out_ref):
    scale = HD ** (-0.5)
    side, far, lo, rows, _ = out_ref.shape
    rows -= ANS_LEN
    halves = far
    assert ROW_BLOCK == lo * rows
    cores = lax.axis_size("core")
    cands = rows // ANS_LEN
    row = lax.broadcasted_iota(jnp.int32, (ROW_BLOCK, HD), 0)
    lane = lax.broadcasted_iota(jnp.int32, (ROW_BLOCK, HD), 1)
    caches = (cache_ref, other_ref)
    steps = [(r, cache) for r in range(side) for cache in caches]

    def scored(step):
        r, cache = step
        parts = query_ref[r * halves * lo : (r + 1) * halves * lo, :rows]
        query = jnp.sum(parts.reshape(halves, lo, rows, HD), axis=0).reshape(ROW_BLOCK, HD)
        query = (query * (1 / SMALL_SCALE)).astype(jnp.bfloat16)
        return dot_transposed(query, cache[0])

    ahead = scored(steps[0])
    held = []
    for i, (r, cache) in enumerate(steps):
        scores = ahead
        if i + 1 < len(steps):
            ahead = scored(steps[i + 1])
        top = jnp.max(scores, axis=1, keepdims=True)
        weights = jnp.exp2((scores - top) * (scale * LOG2E))
        total = jnp.sum(weights, axis=1, keepdims=True)
        held.append((top * scale, total, dot(weights.astype(jnp.bfloat16), cache[1])))
        if len(held) < len(caches):
            continue
        top = jnp.maximum(held[0][0], held[1][0])
        factors = [jnp.exp(part[0] - top) for part in held]
        total = held[0][1] * factors[0] + held[1][1] * factors[1]
        mean = (held[0][2] * factors[0] + held[1][2] * factors[1]) / total
        held = []
        place = (row + r * ROW_BLOCK) // ANS_LEN
        cand = place // cands % lo * cores + lax.axis_index("core")
        candidate = cand * cands + place % cands
        bias = jnp.sum(jnp.where(lane == candidate, bias_ref[0:1, :], 0.0), axis=1, keepdims=True)
        level = top + jnp.log(total) + bias
        for j in range(lo):
            part = slice(j * rows, (j + 1) * rows)
            state = packed(mean[part], level[part])
            for f in range(far):
                out_ref[r, f, j] = state


def merge_kernel(state_ref, own_ref, out_ref):
    mean, level = merged(*unpacked(state_ref[...]))
    halves, pairs = lax.axis_size("far"), lax.axis_size(PAIR)
    rows = pairs * ANS_LEN
    tokens = mean.shape[0]

    def own(s, part, scale):
        lo = lax.axis_size("lo")
        place = s * halves * lo + lax.axis_index("lo")
        total = own_ref[place, part]
        for half in range(1, halves):
            total = total + own_ref[place + half * lo, part]
        return (total * (1 / scale)).astype(jnp.bfloat16)

    query = own(lax.axis_index("side"), slice(0, tokens), SMALL_SCALE)
    key = own(0, slice(tokens, None), KEY_SCALE)
    value = own(1, slice(tokens, None), SMALL_SCALE)
    scores = dot_transposed(query, key) * HD ** (-0.5)
    row = lax.broadcasted_iota(jnp.int32, scores.shape, 0)
    column = lax.broadcasted_iota(jnp.int32, scores.shape, 1)
    shown = (row // rows == column // ANS_LEN) & (column % ANS_LEN <= row % ANS_LEN)
    scores = jnp.where(shown, scores, NEGATIVE)
    top = jnp.max(scores, axis=1, keepdims=True)
    weights = jnp.where(shown, jnp.exp(scores - top), 0.0)
    total = jnp.sum(weights, axis=1, keepdims=True)
    own_mean = dot(weights.astype(jnp.bfloat16), value) / total
    own_level = top + jnp.log(total)
    row = lax.broadcasted_iota(jnp.int32, level.shape, 0)
    mine = row // ANS_LEN % pairs == lax.axis_index(PAIR)
    own_level = jnp.where(mine, own_level, NEGATIVE)
    mean, level = merged(jnp.stack([mean, own_mean]), jnp.stack([level, own_level]))
    out_ref[...] = jnp.broadcast_to(packed(mean, level)[None], out_ref.shape)


def output_kernel(state_ref, weight_ref, out_ref):
    blocks, _, width = out_ref.shape
    columns = [merged(*unpacked(state_ref[s]))[0] for s in range(state_ref.shape[0])]
    attention = jnp.concatenate(columns, axis=1).astype(jnp.bfloat16)
    out = dot(attention, weight_ref[...])
    for block in range(blocks):
        place = reverse(block, blocks)
        out_ref[block] = out[:, place * width : (place + 1) * width].astype(jnp.bfloat16)


def sum_kernel(part_ref, out_ref):
    out_ref[...] = jnp.sum(part_ref[...].astype(jnp.float32), axis=0).astype(out_ref.dtype)


def body(
    hidden, query_weight, key_weight, value_weight, out_weight, key_cache, value_cache, cand_group
):
    tok_dev, feat_dev = hidden.shape
    heads_dev = query_weight.shape[1] // HD
    head, lo = lax.axis_size(HEAD), lax.axis_size("lo")
    far, pairs, side = (lax.axis_size(name) for name in ("far", PAIR, "side"))
    shard_len = key_cache.shape[0]
    bf16, f32 = jnp.bfloat16, jnp.float32
    rows = tok_dev * heads_dev * lo
    columns = out_weight.shape[1] // head

    inputs = (hidden, query_weight, key_weight, value_weight, cand_group, key_cache, value_cache)
    inputs = [pltpu.with_memory_space_constraint(x, pltpu.HBM) for x in inputs]
    partial, bias, cache = pl.pallas_call(
        project_kernel,
        out_shape=(
            jax.ShapeDtypeStruct((pairs * side, tok_dev + far * ANS_LEN, HD), f32),
            jax.ShapeDtypeStruct((ANS_LEN, HD), f32),
            jax.ShapeDtypeStruct((2, *key_cache.shape), bf16),
        ),
        in_specs=[HBM] * 7,
        out_specs=(VMEM, VMEM, HBM),
        scratch_shapes=[
            pltpu.VMEM(hidden.shape, bf16),
            pltpu.VMEM((feat_dev, (heads_dev + 2) * HD), bf16),
            pltpu.SMEM(cand_group.shape, jnp.int32),
            pltpu.SemaphoreType.DMA((11,)),
        ],
        compiler_params=pltpu.CompilerParams(vmem_limit_bytes=40 * 1024 * 1024),
        cost_estimate=pl.CostEstimate(
            flops=2 * tok_dev * feat_dev * (heads_dev + 2) * HD,
            bytes_accessed=2 * feat_dev * (tok_dev + (heads_dev + 2) * HD),
            transcendentals=0,
        ),
    )(*inputs)
    partial = lax.all_to_all(partial.astype(jnp.float16), RING, 0, 0, tiled=True)
    near = far * side * lo
    queries, cache = pl.pallas_call(
        reduce_kernel,
        out_shape=(
            jax.ShapeDtypeStruct((near, *partial.shape[1:]), f32),
            jax.ShapeDtypeStruct(cache.shape, cache.dtype),
        ),
        in_specs=[VMEM, pl.BlockSpec(memory_space=pl.ANY)],
        out_specs=(VMEM, pl.BlockSpec(memory_space=pl.ANY)),
        input_output_aliases={1: 1},
        compiler_params=pltpu.CompilerParams(vmem_limit_bytes=40 * 1024 * 1024),
        cost_estimate=pl.CostEstimate(
            flops=partial.size, bytes_accessed=partial.size * 4, transcendentals=0
        ),
    )(partial.astype(f32), cache)
    other = lax.ppermute(cache, "core", [(0, 1), (1, 0)])
    queries = queries.astype(jnp.float16)
    queries = lax.all_to_all(queries, ("side", "far", "lo"), 0, 0, tiled=True).astype(f32)
    state = call(
        attend_kernel,
        jax.ShapeDtypeStruct((side, far, lo, tok_dev + ANS_LEN, HD), bf16),
        [VMEM] * 4,
        flops=8 * rows * shard_len * HD,
        bytes_accessed=8 * shard_len * HD,
        transcendentals=2 * rows * shard_len,
    )(queries, cache, other, bias)
    state = state.reshape(near, tok_dev + ANS_LEN, HD)
    state = lax.all_to_all(state, ("side", "far", "lo"), 0, 0, tiled=True)
    state = call(
        merge_kernel,
        jax.ShapeDtypeStruct((side * pairs, tok_dev + ANS_LEN, HD), bf16),
        [VMEM] * 2,
        flops=4 * state.size,
        bytes_accessed=2 * state.size,
        transcendentals=0,
    )(state, queries)
    state = lax.all_to_all(state, RING, 0, 0, tiled=True)
    projected = call(
        output_kernel,
        jax.ShapeDtypeStruct((head, tok_dev, columns), bf16),
        [VMEM] * 2,
        flops=2 * tok_dev * out_weight.size,
        bytes_accessed=2 * out_weight.size,
        transcendentals=0,
    )(state.reshape(side, pairs, tok_dev + ANS_LEN, HD), out_weight)
    projected = lax.all_to_all(projected, HEAD[::-1], 0, 0, tiled=True)
    return call(
        sum_kernel,
        jax.ShapeDtypeStruct((tok_dev, columns), bf16),
        [VMEM],
        flops=projected.size,
        bytes_accessed=2 * projected.size,
        transcendentals=0,
    )(projected)


def solution(mesh):
    seq, head, cand = (mesh.shape[name] for name in ("seq", "head", "cand"))
    parts = jax.sharding.Mesh(
        mesh.devices.reshape(2, seq // 8, 2, 2, head // 4, 2, 2, cand // 2, 2),
        (*SEQ, *HEAD, *CAND),
    )
    in_specs = (
        P(CAND, SEQ),
        P(SEQ, HEAD),
        P(SEQ, None),
        P(SEQ, None),
        P(HEAD, SEQ),
        P((*SEQ, *CAND), None),
        P((*SEQ, *CAND), None),
        P(),
    )
    out_specs = P(CAND, (*SEQ, *HEAD))
    return jax.shard_map(body, mesh=parts, in_specs=in_specs, out_specs=out_specs, check_vma=False)
```

```python
import math

import jax
import jax.numpy as jnp
from jax import lax
from jax.experimental import pallas as pl
from jax.experimental.pallas import tpu as pltpu
from jax.sharding import PartitionSpec as P

HD = 128
GROUPS = 8
ANS_LEN = 8
ROW_BLOCK = 128

NEGATIVE = -1e30
LOG2E = math.log2(math.e)
SMALL_SCALE = 16.0
KEY_SCALE = 2.0

VMEM = pl.BlockSpec(memory_space=pltpu.VMEM)
HBM = pl.BlockSpec(memory_space=pltpu.HBM)

PAIR = ("high", "low")
SEQ = ("far", *PAIR, "side")
RING = ("side", *PAIR[::-1])
HEAD = ("head2", "head1", "head0")
CAND = ("lo", "core")


def call(kernel, out_shape, in_specs, **cost):
    return pl.pallas_call(
        kernel,
        out_shape=out_shape,
        in_specs=in_specs,
        out_specs=jax.tree.map(lambda _: VMEM, out_shape),
        compiler_params=pltpu.CompilerParams(vmem_limit_bytes=40 * 1024 * 1024),
        cost_estimate=pl.CostEstimate(**cost),
    )


def reverse(place, count):
    out = 0
    while count > 1:
        out, place, count = 2 * out + place % 2, place // 2, count // 2
    return out


def dot(a, b):
    return jnp.dot(a, b, preferred_element_type=jnp.float32)


def dot_transposed(a, b):
    return lax.dot_general(a, b, (((1,), (1,)), ((), ())), preferred_element_type=jnp.float32)


def project_kernel(
    hidden_hbm, query_hbm, key_hbm, value_hbm, group_hbm, key_cache, value_cache,
    out_ref, bias_ref, cache_hbm, hidden_ref, weight_ref, group_smem, sems,
):
    far, pairs, side = (lax.axis_size(name) for name in ("far", PAIR, "side"))
    features = hidden_ref.shape[1]
    width = query_hbm.shape[1]
    halves = [pl.ds(i * (features // 2), features // 2) for i in range(2)]
    copies = []

    def start(source, target):
        copies.append(pltpu.make_async_copy(source, target, sems.at[len(copies)]))
        copies[-1].start()

    for half in halves:
        start(query_hbm.at[half, :], weight_ref.at[half, pl.ds(0, width)])
        start(hidden_hbm.at[:, half], hidden_ref.at[:, half])
        start(key_hbm.at[half, :], weight_ref.at[half, pl.ds(width, HD)])
        start(value_hbm.at[half, :], weight_ref.at[half, pl.ds(width + HD, HD)])
    start(group_hbm, group_smem)
    start(key_cache, cache_hbm.at[0])
    start(value_cache, cache_hbm.at[1])
    total = None
    for i, half in enumerate(halves):
        for copy in copies[4 * i : 4 * i + 4]:
            copy.wait()
        part = dot(hidden_ref[:, half], weight_ref[half, :])
        total = part if total is None else total + part
    ring = SMALL_SCALE * lax.axis_size(PAIR) * side
    tokens = total.shape[0]
    for h in range(side):
        for p in range(pairs):
            out_ref[h * pairs + p, :tokens] = total[:, h * HD : (h + 1) * HD] * ring
    for s, scale in ((0, ring * KEY_SCALE / SMALL_SCALE), (1, ring)):
        part = total[:, width + s * HD : width + (s + 1) * HD] * scale
        for p in range(pairs):
            for f in range(far):
                place = slice((f * pairs + p) * ANS_LEN, (f * pairs + p + 1) * ANS_LEN)
                target = s * pairs + reverse(p, pairs)
                out_ref[target, tokens + f * ANS_LEN : tokens + (f + 1) * ANS_LEN] = part[place]
    copies[-3].wait()
    chunk = lax.axis_index(SEQ) // (lax.axis_size(SEQ) // GROUPS)
    lane = lax.broadcasted_iota(jnp.int32, bias_ref.shape, 1)
    bias = jnp.zeros(bias_ref.shape, jnp.float32)
    for c in range(group_smem.shape[0]):
        hidden_by = jnp.where(group_smem[c] >= chunk, 0.0, NEGATIVE)
        bias = jnp.where(lane == c, hidden_by, bias)
    bias_ref[...] = bias
    copies[-2].wait()
    copies[-1].wait()


def reduce_kernel(part_ref, _, out_ref, __):
    total = jnp.sum(part_ref[...], axis=0) * (1 / part_ref.shape[0])
    out_ref[...] = jnp.broadcast_to(total[None], out_ref.shape)


def packed(mean, level):
    high = level.astype(jnp.bfloat16).astype(jnp.float32)
    middle = (level - high).astype(jnp.bfloat16).astype(jnp.float32)
    row = lax.broadcasted_iota(jnp.int32, mean.shape, 0)
    lane = lax.broadcasted_iota(jnp.int32, mean.shape, 1)
    line = lax.broadcasted_iota(jnp.int32, (ANS_LEN, HD), 0)
    lines = jnp.zeros((ANS_LEN, HD), jnp.float32)
    for place, term in enumerate((high, middle, level - high - middle)):
        spread = jnp.sum(jnp.where(lane == row, term, 0.0), axis=0, keepdims=True)
        lines = jnp.where(line == place, spread, lines)
    return jnp.concatenate([mean, lines], axis=0).astype(jnp.bfloat16)


def unpacked(state):
    state = state.astype(jnp.float32)
    rows = state.shape[-2] - ANS_LEN
    mean = state[..., :rows, :]
    line = jnp.sum(state[..., rows:, :], axis=-2, keepdims=True)
    row = lax.broadcasted_iota(jnp.int32, mean.shape, mean.ndim - 2)
    lane = lax.broadcasted_iota(jnp.int32, mean.shape, mean.ndim - 1)
    return mean, jnp.sum(jnp.where(lane == row, line, 0.0), axis=-1, keepdims=True)


def merged(mean, level):
    best = jnp.max(level, axis=0)
    factor = jnp.exp(level - best[None])
    total = jnp.sum(factor, axis=0)
    return jnp.sum(mean * factor, axis=0) / total, best + jnp.log(total)


def attend_kernel(query_ref, cache_ref, other_ref, bias_ref, out_ref):
    scale = HD ** (-0.5)
    side, far, lo, rows, _ = out_ref.shape
    rows -= ANS_LEN
    halves = far
    assert ROW_BLOCK == lo * rows
    cores = lax.axis_size("core")
    cands = rows // ANS_LEN
    row = lax.broadcasted_iota(jnp.int32, (ROW_BLOCK, HD), 0)
    lane = lax.broadcasted_iota(jnp.int32, (ROW_BLOCK, HD), 1)
    caches = (cache_ref, other_ref)
    steps = [(r, cache) for r in range(side) for cache in caches]

    def scored(step):
        r, cache = step
        parts = query_ref[r * halves * lo : (r + 1) * halves * lo, :rows]
        query = jnp.sum(parts.reshape(halves, lo, rows, HD), axis=0).reshape(ROW_BLOCK, HD)
        query = (query * (1 / SMALL_SCALE)).astype(jnp.bfloat16)
        return dot_transposed(query, cache[0])

    ahead = scored(steps[0])
    held = []
    for i, (r, cache) in enumerate(steps):
        scores = ahead
        if i + 1 < len(steps):
            ahead = scored(steps[i + 1])
        top = jnp.max(scores, axis=1, keepdims=True)
        weights = jnp.exp2((scores - top) * (scale * LOG2E))
        total = jnp.sum(weights, axis=1, keepdims=True)
        held.append((top * scale, total, dot(weights.astype(jnp.bfloat16), cache[1])))
        if len(held) < len(caches):
            continue
        top = jnp.maximum(held[0][0], held[1][0])
        factors = [jnp.exp(part[0] - top) for part in held]
        total = held[0][1] * factors[0] + held[1][1] * factors[1]
        mean = (held[0][2] * factors[0] + held[1][2] * factors[1]) / total
        held = []
        place = (row + r * ROW_BLOCK) // ANS_LEN
        cand = place // cands % lo * cores + lax.axis_index("core")
        candidate = cand * cands + place % cands
        bias = jnp.sum(jnp.where(lane == candidate, bias_ref[0:1, :], 0.0), axis=1, keepdims=True)
        level = top + jnp.log(total) + bias
        for j in range(lo):
            part = slice(j * rows, (j + 1) * rows)
            state = packed(mean[part], level[part])
            for f in range(far):
                out_ref[r, f, j] = state


def merge_kernel(state_ref, own_ref, out_ref):
    mean, level = merged(*unpacked(state_ref[...]))
    halves, pairs = lax.axis_size("far"), lax.axis_size(PAIR)
    rows = pairs * ANS_LEN
    tokens = mean.shape[0]

    def own(s, part, scale):
        lo = lax.axis_size("lo")
        place = s * halves * lo + lax.axis_index("lo")
        total = own_ref[place, part]
        for half in range(1, halves):
            total = total + own_ref[place + half * lo, part]
        return (total * (1 / scale)).astype(jnp.bfloat16)

    query = own(lax.axis_index("side"), slice(0, tokens), SMALL_SCALE)
    key = own(0, slice(tokens, None), KEY_SCALE)
    value = own(1, slice(tokens, None), SMALL_SCALE)
    scores = dot_transposed(query, key) * HD ** (-0.5)
    row = lax.broadcasted_iota(jnp.int32, scores.shape, 0)
    column = lax.broadcasted_iota(jnp.int32, scores.shape, 1)
    shown = (row // rows == column // ANS_LEN) & (column % ANS_LEN <= row % ANS_LEN)
    scores = jnp.where(shown, scores, NEGATIVE)
    top = jnp.max(scores, axis=1, keepdims=True)
    weights = jnp.where(shown, jnp.exp(scores - top), 0.0)
    total = jnp.sum(weights, axis=1, keepdims=True)
    own_mean = dot(weights.astype(jnp.bfloat16), value) / total
    own_level = top + jnp.log(total)
    row = lax.broadcasted_iota(jnp.int32, level.shape, 0)
    mine = row // ANS_LEN % pairs == lax.axis_index(PAIR)
    own_level = jnp.where(mine, own_level, NEGATIVE)
    mean, level = merged(jnp.stack([mean, own_mean]), jnp.stack([level, own_level]))
    out_ref[...] = jnp.broadcast_to(packed(mean, level)[None], out_ref.shape)


def output_kernel(state_ref, weight_ref, out_ref):
    blocks, _, width = out_ref.shape
    columns = [merged(*unpacked(state_ref[s]))[0] for s in range(state_ref.shape[0])]
    attention = jnp.concatenate(columns, axis=1).astype(jnp.bfloat16)
    out = dot(attention, weight_ref[...])
    for block in range(blocks):
        place = 2 * (block % (blocks // 2)) + block // (blocks // 2)
        out_ref[block] = out[:, place * width : (place + 1) * width].astype(jnp.bfloat16)


def sum_kernel(part_ref, out_ref):
    out_ref[...] = jnp.sum(part_ref[...].astype(jnp.float32), axis=0).astype(out_ref.dtype)


def body(
    hidden, query_weight, key_weight, value_weight, out_weight, key_cache, value_cache, cand_group
):
    tok_dev, feat_dev = hidden.shape
    heads_dev = query_weight.shape[1] // HD
    head, lo = lax.axis_size(HEAD), lax.axis_size("lo")
    far, pairs, side = (lax.axis_size(name) for name in ("far", PAIR, "side"))
    shard_len = key_cache.shape[0]
    bf16, f32 = jnp.bfloat16, jnp.float32
    rows = tok_dev * heads_dev * lo
    columns = out_weight.shape[1] // head

    inputs = (hidden, query_weight, key_weight, value_weight, cand_group, key_cache, value_cache)
    inputs = [pltpu.with_memory_space_constraint(x, pltpu.HBM) for x in inputs]
    partial, bias, cache = pl.pallas_call(
        project_kernel,
        out_shape=(
            jax.ShapeDtypeStruct((pairs * side, tok_dev + far * ANS_LEN, HD), f32),
            jax.ShapeDtypeStruct((ANS_LEN, HD), f32),
            jax.ShapeDtypeStruct((2, *key_cache.shape), bf16),
        ),
        in_specs=[HBM] * 7,
        out_specs=(VMEM, VMEM, HBM),
        scratch_shapes=[
            pltpu.VMEM(hidden.shape, bf16),
            pltpu.VMEM((feat_dev, (heads_dev + 2) * HD), bf16),
            pltpu.SMEM(cand_group.shape, jnp.int32),
            pltpu.SemaphoreType.DMA((11,)),
        ],
        compiler_params=pltpu.CompilerParams(vmem_limit_bytes=40 * 1024 * 1024),
        cost_estimate=pl.CostEstimate(
            flops=2 * tok_dev * feat_dev * (heads_dev + 2) * HD,
            bytes_accessed=2 * feat_dev * (tok_dev + (heads_dev + 2) * HD),
            transcendentals=0,
        ),
    )(*inputs)
    partial = lax.all_to_all(partial.astype(jnp.float16), RING, 0, 0, tiled=True)
    near = far * side * lo
    queries, cache = pl.pallas_call(
        reduce_kernel,
        out_shape=(
            jax.ShapeDtypeStruct((near, *partial.shape[1:]), f32),
            jax.ShapeDtypeStruct(cache.shape, cache.dtype),
        ),
        in_specs=[VMEM, pl.BlockSpec(memory_space=pl.ANY)],
        out_specs=(VMEM, pl.BlockSpec(memory_space=pl.ANY)),
        input_output_aliases={1: 1},
        compiler_params=pltpu.CompilerParams(vmem_limit_bytes=40 * 1024 * 1024),
        cost_estimate=pl.CostEstimate(
            flops=partial.size, bytes_accessed=partial.size * 4, transcendentals=0
        ),
    )(partial.astype(f32), cache)
    other = lax.ppermute(cache, "core", [(0, 1), (1, 0)])
    queries = queries.astype(jnp.float16)
    queries = lax.all_to_all(queries, ("side", "far", "lo"), 0, 0, tiled=True).astype(f32)
    state = call(
        attend_kernel,
        jax.ShapeDtypeStruct((side, far, lo, tok_dev + ANS_LEN, HD), bf16),
        [VMEM] * 4,
        flops=8 * rows * shard_len * HD,
        bytes_accessed=8 * shard_len * HD,
        transcendentals=2 * rows * shard_len,
    )(queries, cache, other, bias)
    state = state.reshape(near, tok_dev + ANS_LEN, HD)
    state = lax.all_to_all(state, ("side", "far", "lo"), 0, 0, tiled=True)
    state = call(
        merge_kernel,
        jax.ShapeDtypeStruct((side * pairs, tok_dev + ANS_LEN, HD), bf16),
        [VMEM] * 2,
        flops=4 * state.size,
        bytes_accessed=2 * state.size,
        transcendentals=0,
    )(state, queries)
    state = lax.all_to_all(state, ("side", *PAIR), 0, 0, tiled=True)
    projected = call(
        output_kernel,
        jax.ShapeDtypeStruct((head, tok_dev, columns), bf16),
        [VMEM] * 2,
        flops=2 * tok_dev * out_weight.size,
        bytes_accessed=2 * out_weight.size,
        transcendentals=0,
    )(state.reshape(side, pairs, tok_dev + ANS_LEN, HD), out_weight)
    projected = lax.all_to_all(projected, (HEAD[2], *HEAD[:2]), 0, 0, tiled=True)
    return call(
        sum_kernel,
        jax.ShapeDtypeStruct((tok_dev, columns), bf16),
        [VMEM],
        flops=projected.size,
        bytes_accessed=2 * projected.size,
        transcendentals=0,
    )(projected)


def solution(mesh):
    seq, head, cand = (mesh.shape[name] for name in ("seq", "head", "cand"))
    parts = jax.sharding.Mesh(
        mesh.devices.reshape(2, seq // 8, 2, 2, head // 4, 2, 2, cand // 2, 2),
        (*SEQ, *HEAD, *CAND),
    )
    in_specs = (
        P(CAND, SEQ),
        P(SEQ, HEAD),
        P(SEQ, None),
        P(SEQ, None),
        P(HEAD, SEQ),
        P((*SEQ, *CAND), None),
        P((*SEQ, *CAND), None),
        P(),
    )
    out_specs = P(CAND, (*SEQ, *HEAD))
    return jax.shard_map(body, mesh=parts, in_specs=in_specs, out_specs=out_specs, check_vma=False)
```

```python
import math

import jax
import jax.numpy as jnp
from jax import lax
from jax.experimental import pallas as pl
from jax.experimental.pallas import tpu as pltpu
from jax.sharding import PartitionSpec as P

HD = 128
GROUPS = 8
ANS_LEN = 8
ROW_BLOCK = 128

NEGATIVE = -1e30
LOG2E = math.log2(math.e)
SMALL_SCALE = 16.0
KEY_SCALE = 2.0

VMEM = pl.BlockSpec(memory_space=pltpu.VMEM)
HBM = pl.BlockSpec(memory_space=pltpu.HBM)

PAIR = ("high", "low")
SEQ = ("far", *PAIR, "side")
RING = ("side", *PAIR[::-1])
HEAD = ("head2", "head1", "head0")
CAND = ("lo", "core")


def call(kernel, out_shape, in_specs, **cost):
    return pl.pallas_call(
        kernel,
        out_shape=out_shape,
        in_specs=in_specs,
        out_specs=jax.tree.map(lambda _: VMEM, out_shape),
        compiler_params=pltpu.CompilerParams(vmem_limit_bytes=40 * 1024 * 1024),
        cost_estimate=pl.CostEstimate(**cost),
    )


def reverse(place, count):
    out = 0
    while count > 1:
        out, place, count = 2 * out + place % 2, place // 2, count // 2
    return out


def dot(a, b):
    return jnp.dot(a, b, preferred_element_type=jnp.float32)


def dot_transposed(a, b):
    return lax.dot_general(a, b, (((1,), (1,)), ((), ())), preferred_element_type=jnp.float32)


def project_kernel(
    hidden_hbm, query_hbm, key_hbm, value_hbm, group_hbm, key_cache, value_cache,
    out_ref, bias_ref, cache_hbm, hidden_ref, weight_ref, group_smem, sems,
):
    far, pairs, side = (lax.axis_size(name) for name in ("far", PAIR, "side"))
    features = hidden_ref.shape[1]
    width = query_hbm.shape[1]
    halves = [pl.ds(i * (features // 2), features // 2) for i in range(2)]
    copies = []

    def start(source, target):
        copies.append(pltpu.make_async_copy(source, target, sems.at[len(copies)]))
        copies[-1].start()

    for half in halves:
        start(query_hbm.at[half, :], weight_ref.at[half, pl.ds(0, width)])
        start(hidden_hbm.at[:, half], hidden_ref.at[:, half])
        start(key_hbm.at[half, :], weight_ref.at[half, pl.ds(width, HD)])
        start(value_hbm.at[half, :], weight_ref.at[half, pl.ds(width + HD, HD)])
    start(group_hbm, group_smem)
    start(key_cache, cache_hbm.at[0])
    start(value_cache, cache_hbm.at[1])
    total = None
    for i, half in enumerate(halves):
        for copy in copies[4 * i : 4 * i + 4]:
            copy.wait()
        part = dot(hidden_ref[:, half], weight_ref[half, :])
        total = part if total is None else total + part
    ring = SMALL_SCALE * lax.axis_size(PAIR) * side
    tokens = total.shape[0]
    for h in range(side):
        for p in range(pairs):
            out_ref[h * pairs + p, :tokens] = total[:, h * HD : (h + 1) * HD] * ring
    for s, scale in ((0, ring * KEY_SCALE / SMALL_SCALE), (1, ring)):
        part = total[:, width + s * HD : width + (s + 1) * HD] * scale
        for p in range(pairs):
            for f in range(far):
                place = slice((f * pairs + p) * ANS_LEN, (f * pairs + p + 1) * ANS_LEN)
                target = s * pairs + reverse(p, pairs)
                out_ref[target, tokens + f * ANS_LEN : tokens + (f + 1) * ANS_LEN] = part[place]
    copies[-3].wait()
    chunk = lax.axis_index(SEQ) // (lax.axis_size(SEQ) // GROUPS)
    lane = lax.broadcasted_iota(jnp.int32, bias_ref.shape, 1)
    bias = jnp.zeros(bias_ref.shape, jnp.float32)
    for c in range(group_smem.shape[0]):
        hidden_by = jnp.where(group_smem[c] >= chunk, 0.0, NEGATIVE)
        bias = jnp.where(lane == c, hidden_by, bias)
    bias_ref[...] = bias
    copies[-2].wait()
    copies[-1].wait()


def reduce_kernel(part_ref, _, out_ref, __):
    total = jnp.sum(part_ref[...], axis=0) * (1 / part_ref.shape[0])
    out_ref[...] = jnp.broadcast_to(total[None], out_ref.shape)


def packed(mean, level):
    high = level.astype(jnp.bfloat16).astype(jnp.float32)
    middle = (level - high).astype(jnp.bfloat16).astype(jnp.float32)
    row = lax.broadcasted_iota(jnp.int32, mean.shape, 0)
    lane = lax.broadcasted_iota(jnp.int32, mean.shape, 1)
    line = lax.broadcasted_iota(jnp.int32, (ANS_LEN, HD), 0)
    lines = jnp.zeros((ANS_LEN, HD), jnp.float32)
    for place, term in enumerate((high, middle, level - high - middle)):
        spread = jnp.sum(jnp.where(lane == row, term, 0.0), axis=0, keepdims=True)
        lines = jnp.where(line == place, spread, lines)
    return jnp.concatenate([mean, lines], axis=0).astype(jnp.bfloat16)


def unpacked(state):
    state = state.astype(jnp.float32)
    rows = state.shape[-2] - ANS_LEN
    mean = state[..., :rows, :]
    line = jnp.sum(state[..., rows:, :], axis=-2, keepdims=True)
    row = lax.broadcasted_iota(jnp.int32, mean.shape, mean.ndim - 2)
    lane = lax.broadcasted_iota(jnp.int32, mean.shape, mean.ndim - 1)
    return mean, jnp.sum(jnp.where(lane == row, line, 0.0), axis=-1, keepdims=True)


def merged(mean, level):
    best = jnp.max(level, axis=0)
    factor = jnp.exp(level - best[None])
    total = jnp.sum(factor, axis=0)
    return jnp.sum(mean * factor, axis=0) / total, best + jnp.log(total)


def attend_kernel(query_ref, cache_ref, other_ref, bias_ref, out_ref):
    scale = HD ** (-0.5)
    side, far, lo, rows, _ = out_ref.shape
    rows = (rows - ANS_LEN) // side
    halves = far
    assert ROW_BLOCK == lo * rows
    cores = lax.axis_size("core")
    cands = rows // ANS_LEN
    row = lax.broadcasted_iota(jnp.int32, (ROW_BLOCK, HD), 0)
    lane = lax.broadcasted_iota(jnp.int32, (ROW_BLOCK, HD), 1)
    caches = (cache_ref, other_ref)
    steps = [(r, cache) for r in range(side) for cache in caches]

    def scored(step):
        r, cache = step
        parts = query_ref[r * halves * lo : (r + 1) * halves * lo, :rows]
        query = jnp.sum(parts.reshape(halves, lo, rows, HD), axis=0).reshape(ROW_BLOCK, HD)
        query = (query * (1 / SMALL_SCALE)).astype(jnp.bfloat16)
        return dot_transposed(query, cache[0])

    ahead = scored(steps[0])
    held, heads = [], []
    for i, (r, cache) in enumerate(steps):
        scores = ahead
        if i + 1 < len(steps):
            ahead = scored(steps[i + 1])
        top = jnp.max(scores, axis=1, keepdims=True)
        weights = jnp.exp2((scores - top) * (scale * LOG2E))
        total = jnp.sum(weights, axis=1, keepdims=True)
        held.append((top * scale, total, dot(weights.astype(jnp.bfloat16), cache[1])))
        if len(held) < len(caches):
            continue
        top = jnp.maximum(held[0][0], held[1][0])
        factors = [jnp.exp(part[0] - top) for part in held]
        total = held[0][1] * factors[0] + held[1][1] * factors[1]
        mean = (held[0][2] * factors[0] + held[1][2] * factors[1]) / total
        held = []
        place = (row + r * ROW_BLOCK) // ANS_LEN
        cand = place // cands % lo * cores + lax.axis_index("core")
        candidate = cand * cands + place % cands
        bias = jnp.sum(jnp.where(lane == candidate, bias_ref[0:1, :], 0.0), axis=1, keepdims=True)
        level = top + jnp.log(total) + bias
        heads.append((mean, level))
    for j in range(lo):
        part = slice(j * rows, (j + 1) * rows)
        mean, level = (jnp.concatenate([head[k][part] for head in heads], axis=0) for k in (0, 1))
        state = packed(mean, level)
        for r in range(side):
            for f in range(far):
                out_ref[r, f, j] = state


def merge_kernel(state_ref, own_ref, out_ref):
    mean, level = merged(*unpacked(state_ref[...]))
    halves, pairs = lax.axis_size("far"), lax.axis_size(PAIR)
    rows = pairs * ANS_LEN
    tokens = mean.shape[0]

    def own(s, part, scale):
        lo = lax.axis_size("lo")
        place = s * halves * lo + lax.axis_index("lo")
        total = own_ref[place, part]
        for half in range(1, halves):
            total = total + own_ref[place + half * lo, part]
        return (total * (1 / scale)).astype(jnp.bfloat16)

    heads = lax.axis_size("side")
    tokens //= heads
    query = [own(s, slice(0, tokens), SMALL_SCALE) for s in range(heads)]
    query = jnp.concatenate(query, axis=0)
    key = own(0, slice(tokens, None), KEY_SCALE)
    value = own(1, slice(tokens, None), SMALL_SCALE)
    scores = dot_transposed(query, key) * HD ** (-0.5)
    row = lax.broadcasted_iota(jnp.int32, scores.shape, 0)
    column = lax.broadcasted_iota(jnp.int32, scores.shape, 1)
    shown = (row % tokens // rows == column // ANS_LEN) & (column % ANS_LEN <= row % ANS_LEN)
    scores = jnp.where(shown, scores, NEGATIVE)
    top = jnp.max(scores, axis=1, keepdims=True)
    weights = jnp.where(shown, jnp.exp(scores - top), 0.0)
    total = jnp.sum(weights, axis=1, keepdims=True)
    own_mean = dot(weights.astype(jnp.bfloat16), value) / total
    own_level = top + jnp.log(total)
    row = lax.broadcasted_iota(jnp.int32, level.shape, 0)
    mine = row // ANS_LEN % pairs == lax.axis_index(PAIR)
    own_level = jnp.where(mine, own_level, NEGATIVE)
    mean, level = merged(jnp.stack([mean, own_mean]), jnp.stack([level, own_level]))
    out_ref[...] = jnp.broadcast_to(packed(mean, level)[None], out_ref.shape)


def output_kernel(state_ref, weight_ref, out_ref):
    blocks, tokens, width = out_ref.shape
    attention = merged(*unpacked(state_ref[...]))[0]
    columns = [attention[at : at + tokens] for at in range(0, attention.shape[0], tokens)]
    attention = jnp.concatenate(columns, axis=1).astype(jnp.bfloat16)
    out = dot(attention, weight_ref[...])
    for block in range(blocks):
        place = reverse(block, blocks)
        out_ref[block] = out[:, place * width : (place + 1) * width].astype(jnp.bfloat16)


def sum_kernel(part_ref, out_ref):
    out_ref[...] = jnp.sum(part_ref[...].astype(jnp.float32), axis=0).astype(out_ref.dtype)


def body(
    hidden, query_weight, key_weight, value_weight, out_weight, key_cache, value_cache, cand_group
):
    tok_dev, feat_dev = hidden.shape
    heads_dev = query_weight.shape[1] // HD
    head, lo = lax.axis_size(HEAD), lax.axis_size("lo")
    far, pairs, side = (lax.axis_size(name) for name in ("far", PAIR, "side"))
    shard_len = key_cache.shape[0]
    bf16, f32 = jnp.bfloat16, jnp.float32
    rows = tok_dev * heads_dev * lo
    columns = out_weight.shape[1] // head

    inputs = (hidden, query_weight, key_weight, value_weight, cand_group, key_cache, value_cache)
    inputs = [pltpu.with_memory_space_constraint(x, pltpu.HBM) for x in inputs]
    partial, bias, cache = pl.pallas_call(
        project_kernel,
        out_shape=(
            jax.ShapeDtypeStruct((pairs * side, tok_dev + far * ANS_LEN, HD), f32),
            jax.ShapeDtypeStruct((ANS_LEN, HD), f32),
            jax.ShapeDtypeStruct((2, *key_cache.shape), bf16),
        ),
        in_specs=[HBM] * 7,
        out_specs=(VMEM, VMEM, HBM),
        scratch_shapes=[
            pltpu.VMEM(hidden.shape, bf16),
            pltpu.VMEM((feat_dev, (heads_dev + 2) * HD), bf16),
            pltpu.SMEM(cand_group.shape, jnp.int32),
            pltpu.SemaphoreType.DMA((11,)),
        ],
        compiler_params=pltpu.CompilerParams(vmem_limit_bytes=40 * 1024 * 1024),
        cost_estimate=pl.CostEstimate(
            flops=2 * tok_dev * feat_dev * (heads_dev + 2) * HD,
            bytes_accessed=2 * feat_dev * (tok_dev + (heads_dev + 2) * HD),
            transcendentals=0,
        ),
    )(*inputs)
    partial = lax.all_to_all(partial.astype(jnp.float16), RING, 0, 0, tiled=True)
    near = far * side * lo
    queries, cache = pl.pallas_call(
        reduce_kernel,
        out_shape=(
            jax.ShapeDtypeStruct((near, *partial.shape[1:]), f32),
            jax.ShapeDtypeStruct(cache.shape, cache.dtype),
        ),
        in_specs=[VMEM, pl.BlockSpec(memory_space=pl.ANY)],
        out_specs=(VMEM, pl.BlockSpec(memory_space=pl.ANY)),
        input_output_aliases={1: 1},
        compiler_params=pltpu.CompilerParams(vmem_limit_bytes=40 * 1024 * 1024),
        cost_estimate=pl.CostEstimate(
            flops=partial.size, bytes_accessed=partial.size * 4, transcendentals=0
        ),
    )(partial.astype(f32), cache)
    other = lax.ppermute(cache, "core", [(0, 1), (1, 0)])
    queries = queries.astype(jnp.float16)
    queries = lax.all_to_all(queries, ("side", "far", "lo"), 0, 0, tiled=True).astype(f32)
    state = call(
        attend_kernel,
        jax.ShapeDtypeStruct((side, far, lo, side * tok_dev + ANS_LEN, HD), bf16),
        [VMEM] * 4,
        flops=8 * rows * shard_len * HD,
        bytes_accessed=8 * shard_len * HD,
        transcendentals=2 * rows * shard_len,
    )(queries, cache, other, bias)
    state = state.reshape(near, side * tok_dev + ANS_LEN, HD)
    state = lax.all_to_all(state, ("side", "far", "lo"), 0, 0, tiled=True)
    state = call(
        merge_kernel,
        jax.ShapeDtypeStruct((pairs, side * tok_dev + ANS_LEN, HD), bf16),
        [VMEM] * 2,
        flops=4 * state.size,
        bytes_accessed=2 * state.size,
        transcendentals=0,
    )(state, queries)
    state = lax.all_to_all(state, PAIR[::-1], 0, 0, tiled=True)
    projected = call(
        output_kernel,
        jax.ShapeDtypeStruct((head, tok_dev, columns), bf16),
        [VMEM] * 2,
        flops=2 * tok_dev * out_weight.size,
        bytes_accessed=2 * out_weight.size,
        transcendentals=0,
    )(state, out_weight)
    projected = lax.all_to_all(projected, HEAD[::-1], 0, 0, tiled=True)
    return call(
        sum_kernel,
        jax.ShapeDtypeStruct((tok_dev, columns), bf16),
        [VMEM],
        flops=projected.size,
        bytes_accessed=2 * projected.size,
        transcendentals=0,
    )(projected)


def solution(mesh):
    seq, head, cand = (mesh.shape[name] for name in ("seq", "head", "cand"))
    parts = jax.sharding.Mesh(
        mesh.devices.reshape(2, seq // 8, 2, 2, head // 4, 2, 2, cand // 2, 2),
        (*SEQ, *HEAD, *CAND),
    )
    in_specs = (
        P(CAND, SEQ),
        P(SEQ, HEAD),
        P(SEQ, None),
        P(SEQ, None),
        P(HEAD, SEQ),
        P((*SEQ, *CAND), None),
        P((*SEQ, *CAND), None),
        P(),
    )
    out_specs = P(CAND, (*SEQ, *HEAD))
    return jax.shard_map(body, mesh=parts, in_specs=in_specs, out_specs=out_specs, check_vma=False)
```

```python
import math

import jax
import jax.numpy as jnp
from jax import lax
from jax.experimental import pallas as pl
from jax.experimental.pallas import tpu as pltpu
from jax.sharding import PartitionSpec as P

HD = 128
GROUPS = 8
ANS_LEN = 8
KEY_BLOCK = 1024

NEGATIVE = -1e30
LOG2E = math.log2(math.e)
SMALL_SCALE = 16.0
KEY_SCALE = 2.0

VMEM = pl.BlockSpec(memory_space=pltpu.VMEM)
HBM = pl.BlockSpec(memory_space=pltpu.HBM)

PAIR = ("high", "low")
SEQ = ("far", *PAIR, "side")
RING = ("side", *PAIR[::-1])
HEAD = ("head2", "head1", "head0")
CAND = ("lo", "core")


def call(kernel, out_shape, in_specs, **cost):
    return pl.pallas_call(
        kernel,
        out_shape=out_shape,
        in_specs=in_specs,
        out_specs=jax.tree.map(lambda _: VMEM, out_shape),
        compiler_params=pltpu.CompilerParams(vmem_limit_bytes=40 * 1024 * 1024),
        cost_estimate=pl.CostEstimate(**cost),
    )


def reverse(place, count):
    out = 0
    while count > 1:
        out, place, count = 2 * out + place % 2, place // 2, count // 2
    return out


def dot(a, b):
    return jnp.dot(a, b, preferred_element_type=jnp.float32)


def dot_transposed(a, b):
    return lax.dot_general(a, b, (((1,), (1,)), ((), ())), preferred_element_type=jnp.float32)


def project_kernel(
    hidden_hbm, query_hbm, key_hbm, value_hbm, group_hbm, key_cache, value_cache,
    out_ref, bias_ref, cache_hbm, hidden_ref, weight_ref, group_smem, sems,
):
    far, pairs, side = (lax.axis_size(name) for name in ("far", PAIR, "side"))
    features = hidden_ref.shape[1]
    width = query_hbm.shape[1]
    halves = [pl.ds(i * (features // 2), features // 2) for i in range(2)]
    copies = []

    def start(source, target):
        copies.append(pltpu.make_async_copy(source, target, sems.at[len(copies)]))
        copies[-1].start()

    start(group_hbm, group_smem)
    for half in halves:
        start(query_hbm.at[half, :], weight_ref.at[half, pl.ds(0, width)])
        start(hidden_hbm.at[:, half], hidden_ref.at[:, half])
        start(key_hbm.at[half, :], weight_ref.at[half, pl.ds(width, HD)])
        start(value_hbm.at[half, :], weight_ref.at[half, pl.ds(width + HD, HD)])
    start(key_cache, cache_hbm.at[0])
    start(value_cache, cache_hbm.at[1])
    copies[0].wait()
    chunk = lax.axis_index(SEQ) // (lax.axis_size(SEQ) // GROUPS)
    lane = lax.broadcasted_iota(jnp.int32, bias_ref.shape, 1)
    bias = jnp.zeros(bias_ref.shape, jnp.float32)
    for c in range(group_smem.shape[0]):
        hidden_by = jnp.where(group_smem[c] >= chunk, 0.0, NEGATIVE)
        bias = jnp.where(lane == c, hidden_by, bias)
    bias_ref[...] = bias
    total = None
    for i, half in enumerate(halves):
        for copy in copies[4 * i + 1 : 4 * i + 5]:
            copy.wait()
        part = dot(hidden_ref[:, half], weight_ref[half, :])
        total = part if total is None else total + part
    ring = SMALL_SCALE * lax.axis_size(PAIR) * side
    tokens = total.shape[0]
    for h in range(side):
        for p in range(pairs):
            out_ref[h * pairs + p, :tokens] = total[:, h * HD : (h + 1) * HD] * ring
    for s, scale in ((0, ring * KEY_SCALE / SMALL_SCALE), (1, ring)):
        part = total[:, width + s * HD : width + (s + 1) * HD] * scale
        for p in range(pairs):
            for f in range(far):
                place = slice((f * pairs + p) * ANS_LEN, (f * pairs + p + 1) * ANS_LEN)
                target = s * pairs + reverse(p, pairs)
                out_ref[target, tokens + f * ANS_LEN : tokens + (f + 1) * ANS_LEN] = part[place]
    copies[-2].wait()
    copies[-1].wait()


def reduce_kernel(part_ref, _, out_ref, __):
    total = jnp.sum(part_ref[...], axis=0) * (1 / part_ref.shape[0])
    out_ref[...] = jnp.broadcast_to(total[None], out_ref.shape)


def packed(mean, level):
    high = level.astype(jnp.bfloat16).astype(jnp.float32)
    middle = (level - high).astype(jnp.bfloat16).astype(jnp.float32)
    row = lax.broadcasted_iota(jnp.int32, mean.shape, 0)
    lane = lax.broadcasted_iota(jnp.int32, mean.shape, 1)
    line = lax.broadcasted_iota(jnp.int32, (ANS_LEN, HD), 0)
    lines = jnp.zeros((ANS_LEN, HD), jnp.float32)
    for place, term in enumerate((high, middle, level - high - middle)):
        spread = jnp.sum(jnp.where(lane == row, term, 0.0), axis=0, keepdims=True)
        lines = jnp.where(line == place, spread, lines)
    return jnp.concatenate([mean, lines], axis=0).astype(jnp.bfloat16)


def unpacked(state):
    state = state.astype(jnp.float32)
    rows = state.shape[-2] - ANS_LEN
    mean = state[..., :rows, :]
    line = jnp.sum(state[..., rows:, :], axis=-2, keepdims=True)
    row = lax.broadcasted_iota(jnp.int32, mean.shape, mean.ndim - 2)
    lane = lax.broadcasted_iota(jnp.int32, mean.shape, mean.ndim - 1)
    return mean, jnp.sum(jnp.where(lane == row, line, 0.0), axis=-1, keepdims=True)


def merged(mean, level):
    best = jnp.max(level, axis=0)
    factor = jnp.exp(level - best[None])
    total = jnp.sum(factor, axis=0)
    return jnp.sum(mean * factor, axis=0) / total, best + jnp.log(total)


def attend_kernel(query_ref, cache_ref, other_ref, bias_ref, out_ref):
    scale = HD ** (-0.5)
    side, far, lo, rows, _ = out_ref.shape
    rows -= ANS_LEN
    halves = far
    cores = lax.axis_size("core")
    cands = rows // ANS_LEN
    query = query_ref[:, :rows].reshape(side, halves, lo * rows, HD)
    query = jnp.sum(query, axis=1).reshape(side * lo * rows, HD)
    query = (query * (1 / SMALL_SCALE)).astype(jnp.bfloat16)
    steps = [
        (cache, slice(start, start + KEY_BLOCK))
        for cache in (cache_ref, other_ref)
        for start in range(0, cache_ref.shape[1], KEY_BLOCK)
    ]

    def scored(step):
        cache, part = step
        return dot_transposed(query, cache[0, part])

    ahead = scored(steps[0])
    held = []
    for i, (cache, part) in enumerate(steps):
        scores = ahead
        if i + 1 < len(steps):
            ahead = scored(steps[i + 1])
        top = jnp.max(scores, axis=1, keepdims=True)
        weights = jnp.exp2((scores - top) * (scale * LOG2E))
        total = jnp.sum(weights, axis=1, keepdims=True)
        held.append((top * scale, total, dot(weights.astype(jnp.bfloat16), cache[1, part])))
    top = held[0][0]
    for part in held[1:]:
        top = jnp.maximum(top, part[0])
    factors = [jnp.exp(part[0] - top) for part in held]
    total = sum(part[1] * factor for part, factor in zip(held, factors))
    mean = sum(part[2] * factor for part, factor in zip(held, factors)) / total
    place = lax.broadcasted_iota(jnp.int32, mean.shape, 0) // ANS_LEN
    lane = lax.broadcasted_iota(jnp.int32, mean.shape, 1)
    cand = place // cands % lo * cores + lax.axis_index("core")
    candidate = cand * cands + place % cands
    bias = jnp.sum(jnp.where(lane == candidate, bias_ref[0:1, :], 0.0), axis=1, keepdims=True)
    level = top + jnp.log(total) + bias
    for r in range(side):
        for j in range(lo):
            start = (r * lo + j) * rows
            state = packed(mean[start : start + rows], level[start : start + rows])
            for f in range(far):
                out_ref[r, f, j] = state


def merge_kernel(state_ref, own_ref, out_ref):
    mean, level = merged(*unpacked(state_ref[...]))
    halves, pairs = lax.axis_size("far"), lax.axis_size(PAIR)
    rows = pairs * ANS_LEN
    tokens = mean.shape[0]

    def own(s, part, scale):
        lo = lax.axis_size("lo")
        place = s * halves * lo + lax.axis_index("lo")
        total = own_ref[place, part]
        for half in range(1, halves):
            total = total + own_ref[place + half * lo, part]
        return (total * (1 / scale)).astype(jnp.bfloat16)

    query = own(lax.axis_index("side"), slice(0, tokens), SMALL_SCALE)
    key = own(0, slice(tokens, None), KEY_SCALE)
    value = own(1, slice(tokens, None), SMALL_SCALE)
    scores = dot_transposed(query, key) * HD ** (-0.5)
    row = lax.broadcasted_iota(jnp.int32, scores.shape, 0)
    column = lax.broadcasted_iota(jnp.int32, scores.shape, 1)
    shown = (row // rows == column // ANS_LEN) & (column % ANS_LEN <= row % ANS_LEN)
    scores = jnp.where(shown, scores, NEGATIVE)
    top = jnp.max(scores, axis=1, keepdims=True)
    weights = jnp.where(shown, jnp.exp(scores - top), 0.0)
    total = jnp.sum(weights, axis=1, keepdims=True)
    own_mean = dot(weights.astype(jnp.bfloat16), value) / total
    own_level = top + jnp.log(total)
    row = lax.broadcasted_iota(jnp.int32, level.shape, 0)
    mine = row // ANS_LEN % pairs == lax.axis_index(PAIR)
    own_level = jnp.where(mine, own_level, NEGATIVE)
    mean, level = merged(jnp.stack([mean, own_mean]), jnp.stack([level, own_level]))
    out_ref[...] = jnp.broadcast_to(packed(mean, level)[None], out_ref.shape)


def output_kernel(state_ref, weight_ref, out_ref):
    blocks, _, width = out_ref.shape
    columns = [merged(*unpacked(state_ref[s]))[0] for s in range(state_ref.shape[0])]
    attention = jnp.concatenate(columns, axis=1).astype(jnp.bfloat16)
    out = dot(attention, weight_ref[...])
    for block in range(blocks):
        place = reverse(block, blocks)
        out_ref[block] = out[:, place * width : (place + 1) * width].astype(jnp.bfloat16)


def sum_kernel(part_ref, out_ref):
    out_ref[...] = jnp.sum(part_ref[...].astype(jnp.float32), axis=0).astype(out_ref.dtype)


def body(
    hidden, query_weight, key_weight, value_weight, out_weight, key_cache, value_cache, cand_group
):
    tok_dev, feat_dev = hidden.shape
    heads_dev = query_weight.shape[1] // HD
    head, lo = lax.axis_size(HEAD), lax.axis_size("lo")
    far, pairs, side = (lax.axis_size(name) for name in ("far", PAIR, "side"))
    shard_len = key_cache.shape[0]
    bf16, f32 = jnp.bfloat16, jnp.float32
    rows = tok_dev * heads_dev * lo
    columns = out_weight.shape[1] // head

    inputs = (hidden, query_weight, key_weight, value_weight, cand_group, key_cache, value_cache)
    inputs = [pltpu.with_memory_space_constraint(x, pltpu.HBM) for x in inputs]
    partial, bias, cache = pl.pallas_call(
        project_kernel,
        out_shape=(
            jax.ShapeDtypeStruct((pairs * side, tok_dev + far * ANS_LEN, HD), f32),
            jax.ShapeDtypeStruct((ANS_LEN, HD), f32),
            jax.ShapeDtypeStruct((2, *key_cache.shape), bf16),
        ),
        in_specs=[HBM] * 7,
        out_specs=(VMEM, VMEM, HBM),
        scratch_shapes=[
            pltpu.VMEM(hidden.shape, bf16),
            pltpu.VMEM((feat_dev, (heads_dev + 2) * HD), bf16),
            pltpu.SMEM(cand_group.shape, jnp.int32),
            pltpu.SemaphoreType.DMA((11,)),
        ],
        compiler_params=pltpu.CompilerParams(vmem_limit_bytes=40 * 1024 * 1024),
        cost_estimate=pl.CostEstimate(
            flops=2 * tok_dev * feat_dev * (heads_dev + 2) * HD,
            bytes_accessed=2 * feat_dev * (tok_dev + (heads_dev + 2) * HD),
            transcendentals=0,
        ),
    )(*inputs)
    partial = lax.all_to_all(partial.astype(jnp.float16), RING, 0, 0, tiled=True)
    near = far * side * lo
    queries, cache = pl.pallas_call(
        reduce_kernel,
        out_shape=(
            jax.ShapeDtypeStruct((near, *partial.shape[1:]), f32),
            jax.ShapeDtypeStruct(cache.shape, cache.dtype),
        ),
        in_specs=[VMEM, pl.BlockSpec(memory_space=pl.ANY)],
        out_specs=(VMEM, pl.BlockSpec(memory_space=pl.ANY)),
        input_output_aliases={1: 1},
        compiler_params=pltpu.CompilerParams(vmem_limit_bytes=40 * 1024 * 1024),
        cost_estimate=pl.CostEstimate(
            flops=partial.size, bytes_accessed=partial.size * 4, transcendentals=0
        ),
    )(partial.astype(f32), cache)
    other = lax.ppermute(cache, "core", [(0, 1), (1, 0)])
    queries = queries.astype(jnp.float16)
    queries = lax.all_to_all(queries, ("side", "far", "lo"), 0, 0, tiled=True).astype(f32)
    state = call(
        attend_kernel,
        jax.ShapeDtypeStruct((side, far, lo, tok_dev + ANS_LEN, HD), bf16),
        [VMEM] * 4,
        flops=8 * rows * shard_len * HD,
        bytes_accessed=8 * shard_len * HD,
        transcendentals=2 * rows * shard_len,
    )(queries, cache, other, bias)
    state = state.reshape(near, tok_dev + ANS_LEN, HD)
    state = lax.all_to_all(state, ("side", "far", "lo"), 0, 0, tiled=True)
    state = call(
        merge_kernel,
        jax.ShapeDtypeStruct((side * pairs, tok_dev + ANS_LEN, HD), bf16),
        [VMEM] * 2,
        flops=4 * state.size,
        bytes_accessed=2 * state.size,
        transcendentals=0,
    )(state, queries)
    state = lax.all_to_all(state, RING, 0, 0, tiled=True)
    projected = call(
        output_kernel,
        jax.ShapeDtypeStruct((head, tok_dev, columns), bf16),
        [VMEM] * 2,
        flops=2 * tok_dev * out_weight.size,
        bytes_accessed=2 * out_weight.size,
        transcendentals=0,
    )(state.reshape(side, pairs, tok_dev + ANS_LEN, HD), out_weight)
    projected = lax.all_to_all(projected, HEAD[::-1], 0, 0, tiled=True)
    return call(
        sum_kernel,
        jax.ShapeDtypeStruct((tok_dev, columns), bf16),
        [VMEM],
        flops=projected.size,
        bytes_accessed=2 * projected.size,
        transcendentals=0,
    )(projected)


def solution(mesh):
    seq, head, cand = (mesh.shape[name] for name in ("seq", "head", "cand"))
    parts = jax.sharding.Mesh(
        mesh.devices.reshape(2, seq // 8, 2, 2, head // 4, 2, 2, cand // 2, 2),
        (*SEQ, *HEAD, *CAND),
    )
    in_specs = (
        P(CAND, SEQ),
        P(SEQ, HEAD),
        P(SEQ, None),
        P(SEQ, None),
        P(HEAD, SEQ),
        P((*SEQ, *CAND), None),
        P((*SEQ, *CAND), None),
        P(),
    )
    out_specs = P(CAND, (*SEQ, *HEAD))
    return jax.shard_map(body, mesh=parts, in_specs=in_specs, out_specs=out_specs, check_vma=False)
```

```python
import math

import jax
import jax.numpy as jnp
from jax import lax
from jax.experimental import pallas as pl
from jax.experimental.pallas import tpu as pltpu
from jax.sharding import PartitionSpec as P

HD = 128
GROUPS = 8
ANS_LEN = 8
KEY_BLOCK = 1024

NEGATIVE = -1e30
LOG2E = math.log2(math.e)
SMALL_SCALE = 16.0
KEY_SCALE = 2.0

VMEM = pl.BlockSpec(memory_space=pltpu.VMEM)
HBM = pl.BlockSpec(memory_space=pltpu.HBM)

PAIR = ("high", "low")
SEQ = ("far", *PAIR, "side")
RING = ("side", *PAIR[::-1])
HEAD = ("head2", "head1", "head0")
CAND = ("lo", "core")


def call(kernel, out_shape, in_specs, **cost):
    return pl.pallas_call(
        kernel,
        out_shape=out_shape,
        in_specs=in_specs,
        out_specs=jax.tree.map(lambda _: VMEM, out_shape),
        compiler_params=pltpu.CompilerParams(vmem_limit_bytes=40 * 1024 * 1024),
        cost_estimate=pl.CostEstimate(**cost),
    )


def reverse(place, count):
    out = 0
    while count > 1:
        out, place, count = 2 * out + place % 2, place // 2, count // 2
    return out


def dot(a, b):
    return jnp.dot(a, b, preferred_element_type=jnp.float32)


def dot_transposed(a, b):
    return lax.dot_general(a, b, (((1,), (1,)), ((), ())), preferred_element_type=jnp.float32)


def project_kernel(
    hidden_hbm, query_hbm, key_hbm, value_hbm, group_hbm, key_cache, value_cache,
    out_ref, bias_ref, cache_hbm, hidden_ref, weight_ref, group_smem, sems,
):
    far, pairs, side = (lax.axis_size(name) for name in ("far", PAIR, "side"))
    features = hidden_ref.shape[1]
    width = query_hbm.shape[1]
    halves = [pl.ds(i * (features // 2), features // 2) for i in range(2)]
    copies = []

    def start(source, target):
        copies.append(pltpu.make_async_copy(source, target, sems.at[len(copies)]))
        copies[-1].start()

    start(group_hbm, group_smem)
    for half in halves:
        start(query_hbm.at[half, :], weight_ref.at[half, pl.ds(0, width)])
        start(hidden_hbm.at[:, half], hidden_ref.at[:, half])
        start(key_hbm.at[half, :], weight_ref.at[half, pl.ds(width, HD)])
        start(value_hbm.at[half, :], weight_ref.at[half, pl.ds(width + HD, HD)])
    start(key_cache, cache_hbm.at[0])
    start(value_cache, cache_hbm.at[1])
    copies[0].wait()
    chunk = lax.axis_index(SEQ) // (lax.axis_size(SEQ) // GROUPS)
    lane = lax.broadcasted_iota(jnp.int32, bias_ref.shape, 1)
    bias = jnp.zeros(bias_ref.shape, jnp.float32)
    for c in range(group_smem.shape[0]):
        hidden_by = jnp.where(group_smem[c] >= chunk, 0.0, NEGATIVE)
        bias = jnp.where(lane == c, hidden_by, bias)
    bias_ref[...] = bias
    total = None
    for i, half in enumerate(halves):
        for copy in copies[4 * i + 1 : 4 * i + 5]:
            copy.wait()
        part = dot(hidden_ref[:, half], weight_ref[half, :])
        total = part if total is None else total + part
    ring = SMALL_SCALE * lax.axis_size(PAIR) * side
    tokens = total.shape[0]
    for h in range(side):
        for p in range(pairs):
            out_ref[h * pairs + p, :tokens] = total[:, h * HD : (h + 1) * HD] * ring
    for s, scale in ((0, ring * KEY_SCALE / SMALL_SCALE), (1, ring)):
        part = total[:, width + s * HD : width + (s + 1) * HD] * scale
        for p in range(pairs):
            for f in range(far):
                place = slice((f * pairs + p) * ANS_LEN, (f * pairs + p + 1) * ANS_LEN)
                target = s * pairs + reverse(p, pairs)
                out_ref[target, tokens + f * ANS_LEN : tokens + (f + 1) * ANS_LEN] = part[place]
    copies[-2].wait()
    copies[-1].wait()


def reduce_kernel(part_ref, _, out_ref, __):
    total = jnp.sum(part_ref[...], axis=0) * (1 / part_ref.shape[0])
    out_ref[...] = jnp.broadcast_to(total[None], out_ref.shape)


def packed(mean, level):
    high = level.astype(jnp.bfloat16).astype(jnp.float32)
    middle = (level - high).astype(jnp.bfloat16).astype(jnp.float32)
    row = lax.broadcasted_iota(jnp.int32, mean.shape, 0)
    lane = lax.broadcasted_iota(jnp.int32, mean.shape, 1)
    line = lax.broadcasted_iota(jnp.int32, (ANS_LEN, HD), 0)
    lines = jnp.zeros((ANS_LEN, HD), jnp.float32)
    for place, term in enumerate((high, middle, level - high - middle)):
        spread = jnp.sum(jnp.where(lane == row, term, 0.0), axis=0, keepdims=True)
        lines = jnp.where(line == place, spread, lines)
    return jnp.concatenate([mean, lines], axis=0).astype(jnp.bfloat16)


def unpacked(state):
    state = state.astype(jnp.float32)
    rows = state.shape[-2] - ANS_LEN
    mean = state[..., :rows, :]
    line = jnp.sum(state[..., rows:, :], axis=-2, keepdims=True)
    row = lax.broadcasted_iota(jnp.int32, mean.shape, mean.ndim - 2)
    lane = lax.broadcasted_iota(jnp.int32, mean.shape, mean.ndim - 1)
    return mean, jnp.sum(jnp.where(lane == row, line, 0.0), axis=-1, keepdims=True)


def merged(mean, level):
    best = jnp.max(level, axis=0)
    factor = jnp.exp(level - best[None])
    total = jnp.sum(factor, axis=0)
    return jnp.sum(mean * factor, axis=0) / total, best + jnp.log(total)


def attend_kernel(query_ref, cache_ref, other_ref, bias_ref, out_ref):
    scale = HD ** (-0.5)
    side, far, lo, rows, _ = out_ref.shape
    rows -= ANS_LEN
    halves = far
    cores = lax.axis_size("core")
    cands = rows // ANS_LEN
    query = jnp.sum(query_ref[:, :rows].reshape(halves, lo, side, rows, HD), axis=0)
    query = jnp.concatenate([query[j, r] for r in range(side) for j in range(lo)], axis=0)
    query = (query * (1 / SMALL_SCALE)).astype(jnp.bfloat16)
    steps = [
        (cache, slice(start, start + KEY_BLOCK))
        for cache in (cache_ref, other_ref)
        for start in range(0, cache_ref.shape[1], KEY_BLOCK)
    ]

    def scored(step):
        cache, part = step
        return dot_transposed(query, cache[0, part])

    ahead = scored(steps[0])
    held = []
    for i, (cache, part) in enumerate(steps):
        scores = ahead
        if i + 1 < len(steps):
            ahead = scored(steps[i + 1])
        top = jnp.max(scores, axis=1, keepdims=True)
        weights = jnp.exp2((scores - top) * (scale * LOG2E))
        total = jnp.sum(weights, axis=1, keepdims=True)
        held.append((top * scale, total, dot(weights.astype(jnp.bfloat16), cache[1, part])))
    top = held[0][0]
    for part in held[1:]:
        top = jnp.maximum(top, part[0])
    factors = [jnp.exp(part[0] - top) for part in held]
    total = sum(part[1] * factor for part, factor in zip(held, factors))
    mean = sum(part[2] * factor for part, factor in zip(held, factors)) / total
    place = lax.broadcasted_iota(jnp.int32, mean.shape, 0) // ANS_LEN
    lane = lax.broadcasted_iota(jnp.int32, mean.shape, 1)
    cand = place // cands % lo * cores + lax.axis_index("core")
    candidate = cand * cands + place % cands
    bias = jnp.sum(jnp.where(lane == candidate, bias_ref[0:1, :], 0.0), axis=1, keepdims=True)
    level = top + jnp.log(total) + bias
    for r in range(side):
        for j in range(lo):
            start = (r * lo + j) * rows
            state = packed(mean[start : start + rows], level[start : start + rows])
            for f in range(far):
                out_ref[r, f, j] = state


def merge_kernel(state_ref, own_ref, out_ref):
    mean, level = merged(*unpacked(state_ref[...]))
    halves, pairs = lax.axis_size("far"), lax.axis_size(PAIR)
    rows = pairs * ANS_LEN
    tokens = mean.shape[0]

    def own(s, part, scale):
        lo = lax.axis_size("lo")
        heads = lax.axis_size("side")
        place = lax.axis_index("lo") * heads + s
        total = own_ref[place, part]
        for half in range(1, halves):
            total = total + own_ref[place + half * lo * heads, part]
        return (total * (1 / scale)).astype(jnp.bfloat16)

    query = own(lax.axis_index("side"), slice(0, tokens), SMALL_SCALE)
    key = own(0, slice(tokens, None), KEY_SCALE)
    value = own(1, slice(tokens, None), SMALL_SCALE)
    scores = dot_transposed(query, key) * HD ** (-0.5)
    row = lax.broadcasted_iota(jnp.int32, scores.shape, 0)
    column = lax.broadcasted_iota(jnp.int32, scores.shape, 1)
    shown = (row // rows == column // ANS_LEN) & (column % ANS_LEN <= row % ANS_LEN)
    scores = jnp.where(shown, scores, NEGATIVE)
    top = jnp.max(scores, axis=1, keepdims=True)
    weights = jnp.where(shown, jnp.exp(scores - top), 0.0)
    total = jnp.sum(weights, axis=1, keepdims=True)
    own_mean = dot(weights.astype(jnp.bfloat16), value) / total
    own_level = top + jnp.log(total)
    row = lax.broadcasted_iota(jnp.int32, level.shape, 0)
    mine = row // ANS_LEN % pairs == lax.axis_index(PAIR)
    own_level = jnp.where(mine, own_level, NEGATIVE)
    mean, level = merged(jnp.stack([mean, own_mean]), jnp.stack([level, own_level]))
    out_ref[...] = jnp.broadcast_to(packed(mean, level)[None], out_ref.shape)


def output_kernel(state_ref, weight_ref, out_ref):
    blocks, _, width = out_ref.shape
    columns = [merged(*unpacked(state_ref[s]))[0] for s in range(state_ref.shape[0])]
    attention = jnp.concatenate(columns, axis=1).astype(jnp.bfloat16)
    out = dot(attention, weight_ref[...])
    for block in range(blocks):
        place = reverse(block, blocks)
        out_ref[block] = out[:, place * width : (place + 1) * width].astype(jnp.bfloat16)


def sum_kernel(part_ref, out_ref):
    out_ref[...] = jnp.sum(part_ref[...].astype(jnp.float32), axis=0).astype(out_ref.dtype)


def body(
    hidden, query_weight, key_weight, value_weight, out_weight, key_cache, value_cache, cand_group
):
    tok_dev, feat_dev = hidden.shape
    heads_dev = query_weight.shape[1] // HD
    head, lo = lax.axis_size(HEAD), lax.axis_size("lo")
    far, pairs, side = (lax.axis_size(name) for name in ("far", PAIR, "side"))
    shard_len = key_cache.shape[0]
    bf16, f32 = jnp.bfloat16, jnp.float32
    rows = tok_dev * heads_dev * lo
    columns = out_weight.shape[1] // head

    inputs = (hidden, query_weight, key_weight, value_weight, cand_group, key_cache, value_cache)
    inputs = [pltpu.with_memory_space_constraint(x, pltpu.HBM) for x in inputs]
    partial, bias, cache = pl.pallas_call(
        project_kernel,
        out_shape=(
            jax.ShapeDtypeStruct((pairs * side, tok_dev + far * ANS_LEN, HD), f32),
            jax.ShapeDtypeStruct((ANS_LEN, HD), f32),
            jax.ShapeDtypeStruct((2, *key_cache.shape), bf16),
        ),
        in_specs=[HBM] * 7,
        out_specs=(VMEM, VMEM, HBM),
        scratch_shapes=[
            pltpu.VMEM(hidden.shape, bf16),
            pltpu.VMEM((feat_dev, (heads_dev + 2) * HD), bf16),
            pltpu.SMEM(cand_group.shape, jnp.int32),
            pltpu.SemaphoreType.DMA((11,)),
        ],
        compiler_params=pltpu.CompilerParams(vmem_limit_bytes=40 * 1024 * 1024),
        cost_estimate=pl.CostEstimate(
            flops=2 * tok_dev * feat_dev * (heads_dev + 2) * HD,
            bytes_accessed=2 * feat_dev * (tok_dev + (heads_dev + 2) * HD),
            transcendentals=0,
        ),
    )(*inputs)
    partial = lax.all_to_all(partial.astype(jnp.float16), RING, 0, 0, tiled=True)
    near = far * side * lo
    queries, cache = pl.pallas_call(
        reduce_kernel,
        out_shape=(
            jax.ShapeDtypeStruct((near, *partial.shape[1:]), f32),
            jax.ShapeDtypeStruct(cache.shape, cache.dtype),
        ),
        in_specs=[VMEM, pl.BlockSpec(memory_space=pl.ANY)],
        out_specs=(VMEM, pl.BlockSpec(memory_space=pl.ANY)),
        input_output_aliases={1: 1},
        compiler_params=pltpu.CompilerParams(vmem_limit_bytes=40 * 1024 * 1024),
        cost_estimate=pl.CostEstimate(
            flops=partial.size, bytes_accessed=partial.size * 4, transcendentals=0
        ),
    )(partial.astype(f32), cache)
    other = lax.ppermute(cache, "core", [(0, 1), (1, 0)])
    queries = queries.astype(jnp.float16)
    queries = lax.all_to_all(queries, ("far", "lo", "side"), 0, 0, tiled=True).astype(f32)
    state = call(
        attend_kernel,
        jax.ShapeDtypeStruct((side, far, lo, tok_dev + ANS_LEN, HD), bf16),
        [VMEM] * 4,
        flops=8 * rows * shard_len * HD,
        bytes_accessed=8 * shard_len * HD,
        transcendentals=2 * rows * shard_len,
    )(queries, cache, other, bias)
    state = state.reshape(near, tok_dev + ANS_LEN, HD)
    state = lax.all_to_all(state, ("side", "far", "lo"), 0, 0, tiled=True)
    state = call(
        merge_kernel,
        jax.ShapeDtypeStruct((side * pairs, tok_dev + ANS_LEN, HD), bf16),
        [VMEM] * 2,
        flops=4 * state.size,
        bytes_accessed=2 * state.size,
        transcendentals=0,
    )(state, queries)
    state = lax.all_to_all(state, RING, 0, 0, tiled=True)
    projected = call(
        output_kernel,
        jax.ShapeDtypeStruct((head, tok_dev, columns), bf16),
        [VMEM] * 2,
        flops=2 * tok_dev * out_weight.size,
        bytes_accessed=2 * out_weight.size,
        transcendentals=0,
    )(state.reshape(side, pairs, tok_dev + ANS_LEN, HD), out_weight)
    projected = lax.all_to_all(projected, HEAD[::-1], 0, 0, tiled=True)
    return call(
        sum_kernel,
        jax.ShapeDtypeStruct((tok_dev, columns), bf16),
        [VMEM],
        flops=projected.size,
        bytes_accessed=2 * projected.size,
        transcendentals=0,
    )(projected)


def solution(mesh):
    seq, head, cand = (mesh.shape[name] for name in ("seq", "head", "cand"))
    parts = jax.sharding.Mesh(
        mesh.devices.reshape(2, seq // 8, 2, 2, head // 4, 2, 2, cand // 2, 2),
        (*SEQ, *HEAD, *CAND),
    )
    in_specs = (
        P(CAND, SEQ),
        P(SEQ, HEAD),
        P(SEQ, None),
        P(SEQ, None),
        P(HEAD, SEQ),
        P((*SEQ, *CAND), None),
        P((*SEQ, *CAND), None),
        P(),
    )
    out_specs = P(CAND, (*SEQ, *HEAD))
    return jax.shard_map(body, mesh=parts, in_specs=in_specs, out_specs=out_specs, check_vma=False)
```

```python
import math

import jax
import jax.numpy as jnp
from jax import lax
from jax.experimental import pallas as pl
from jax.experimental.pallas import tpu as pltpu
from jax.sharding import PartitionSpec as P

HD = 128
GROUPS = 8
ANS_LEN = 8
KEY_BLOCK = 1024

NEGATIVE = -1e30
LOG2E = math.log2(math.e)
SMALL_SCALE = 16.0
KEY_SCALE = 2.0

VMEM = pl.BlockSpec(memory_space=pltpu.VMEM)
HBM = pl.BlockSpec(memory_space=pltpu.HBM)

PAIR = ("high", "low")
SEQ = ("far", *PAIR, "side")
RING = ("side", *PAIR[::-1])
HEAD = ("head2", "head1", "head0")
CAND = ("lo", "core")


def call(kernel, out_shape, in_specs, **cost):
    return pl.pallas_call(
        kernel,
        out_shape=out_shape,
        in_specs=in_specs,
        out_specs=jax.tree.map(lambda _: VMEM, out_shape),
        compiler_params=pltpu.CompilerParams(vmem_limit_bytes=40 * 1024 * 1024),
        cost_estimate=pl.CostEstimate(**cost),
    )


def reverse(place, count):
    out = 0
    while count > 1:
        out, place, count = 2 * out + place % 2, place // 2, count // 2
    return out


def dot(a, b):
    return jnp.dot(a, b, preferred_element_type=jnp.float32)


def dot_transposed(a, b):
    return lax.dot_general(a, b, (((1,), (1,)), ((), ())), preferred_element_type=jnp.float32)


def project_kernel(
    hidden_hbm, query_hbm, key_hbm, value_hbm, group_hbm, key_cache, value_cache,
    out_ref, bias_ref, cache_hbm, hidden_ref, weight_ref, group_smem, sems,
):
    far, pairs, side = (lax.axis_size(name) for name in ("far", PAIR, "side"))
    features = hidden_ref.shape[1]
    width = query_hbm.shape[1]
    first = features // 4 * 3
    halves = [pl.ds(0, first), pl.ds(first, features - first)]
    copies = []

    def start(source, target):
        copies.append(pltpu.make_async_copy(source, target, sems.at[len(copies)]))
        copies[-1].start()

    start(group_hbm, group_smem)
    for half in halves:
        start(query_hbm.at[half, :], weight_ref.at[half, pl.ds(0, width)])
        start(hidden_hbm.at[:, half], hidden_ref.at[:, half])
        start(key_hbm.at[half, :], weight_ref.at[half, pl.ds(width, HD)])
        start(value_hbm.at[half, :], weight_ref.at[half, pl.ds(width + HD, HD)])
    start(key_cache, cache_hbm.at[0])
    start(value_cache, cache_hbm.at[1])
    copies[0].wait()
    chunk = lax.axis_index(SEQ) // (lax.axis_size(SEQ) // GROUPS)
    lane = lax.broadcasted_iota(jnp.int32, bias_ref.shape, 1)
    bias = jnp.zeros(bias_ref.shape, jnp.float32)
    for c in range(group_smem.shape[0]):
        hidden_by = jnp.where(group_smem[c] >= chunk, 0.0, NEGATIVE)
        bias = jnp.where(lane == c, hidden_by, bias)
    bias_ref[...] = bias
    total = None
    for i, half in enumerate(halves):
        for copy in copies[4 * i + 1 : 4 * i + 5]:
            copy.wait()
        part = dot(hidden_ref[:, half], weight_ref[half, :])
        total = part if total is None else total + part
    ring = SMALL_SCALE * lax.axis_size(PAIR) * side
    tokens = total.shape[0]
    for h in range(side):
        for p in range(pairs):
            out_ref[h * pairs + p, :tokens] = total[:, h * HD : (h + 1) * HD] * ring
    for s, scale in ((0, ring * KEY_SCALE / SMALL_SCALE), (1, ring)):
        part = total[:, width + s * HD : width + (s + 1) * HD] * scale
        for p in range(pairs):
            for f in range(far):
                place = slice((f * pairs + p) * ANS_LEN, (f * pairs + p + 1) * ANS_LEN)
                target = s * pairs + reverse(p, pairs)
                out_ref[target, tokens + f * ANS_LEN : tokens + (f + 1) * ANS_LEN] = part[place]
    copies[-2].wait()
    copies[-1].wait()


def reduce_kernel(part_ref, _, out_ref, __):
    total = jnp.sum(part_ref[...], axis=0) * (1 / part_ref.shape[0])
    out_ref[...] = jnp.broadcast_to(total[None], out_ref.shape)


def packed(mean, level):
    high = level.astype(jnp.bfloat16).astype(jnp.float32)
    middle = (level - high).astype(jnp.bfloat16).astype(jnp.float32)
    row = lax.broadcasted_iota(jnp.int32, mean.shape, 0)
    lane = lax.broadcasted_iota(jnp.int32, mean.shape, 1)
    line = lax.broadcasted_iota(jnp.int32, (ANS_LEN, HD), 0)
    lines = jnp.zeros((ANS_LEN, HD), jnp.float32)
    for place, term in enumerate((high, middle, level - high - middle)):
        spread = jnp.sum(jnp.where(lane == row, term, 0.0), axis=0, keepdims=True)
        lines = jnp.where(line == place, spread, lines)
    return jnp.concatenate([mean, lines], axis=0).astype(jnp.bfloat16)


def unpacked(state):
    state = state.astype(jnp.float32)
    rows = state.shape[-2] - ANS_LEN
    mean = state[..., :rows, :]
    line = jnp.sum(state[..., rows:, :], axis=-2, keepdims=True)
    row = lax.broadcasted_iota(jnp.int32, mean.shape, mean.ndim - 2)
    lane = lax.broadcasted_iota(jnp.int32, mean.shape, mean.ndim - 1)
    return mean, jnp.sum(jnp.where(lane == row, line, 0.0), axis=-1, keepdims=True)


def merged(mean, level):
    best = jnp.max(level, axis=0)
    factor = jnp.exp(level - best[None])
    total = jnp.sum(factor, axis=0)
    return jnp.sum(mean * factor, axis=0) / total, best + jnp.log(total)


def attend_kernel(query_ref, cache_ref, other_ref, bias_ref, out_ref):
    scale = HD ** (-0.5)
    side, far, lo, rows, _ = out_ref.shape
    rows -= ANS_LEN
    halves = far
    cores = lax.axis_size("core")
    cands = rows // ANS_LEN
    query = jnp.sum(query_ref[:, :rows].reshape(halves, lo, side, rows, HD), axis=0)
    query = jnp.concatenate([query[j, r] for r in range(side) for j in range(lo)], axis=0)
    query = (query * (1 / SMALL_SCALE)).astype(jnp.bfloat16)
    steps = [
        (cache, slice(start, start + KEY_BLOCK))
        for cache in (cache_ref, other_ref)
        for start in range(0, cache_ref.shape[1], KEY_BLOCK)
    ]

    def scored(step):
        cache, part = step
        return dot_transposed(query, cache[0, part])

    ahead = scored(steps[0])
    held = []
    for i, (cache, part) in enumerate(steps):
        scores = ahead
        if i + 1 < len(steps):
            ahead = scored(steps[i + 1])
        top = jnp.max(scores, axis=1, keepdims=True)
        weights = jnp.exp2((scores - top) * (scale * LOG2E))
        total = jnp.sum(weights, axis=1, keepdims=True)
        held.append((top * scale, total, dot(weights.astype(jnp.bfloat16), cache[1, part])))
    top = held[0][0]
    for part in held[1:]:
        top = jnp.maximum(top, part[0])
    factors = [jnp.exp(part[0] - top) for part in held]
    total = sum(part[1] * factor for part, factor in zip(held, factors))
    mean = sum(part[2] * factor for part, factor in zip(held, factors)) / total
    place = lax.broadcasted_iota(jnp.int32, mean.shape, 0) // ANS_LEN
    lane = lax.broadcasted_iota(jnp.int32, mean.shape, 1)
    cand = place // cands % lo * cores + lax.axis_index("core")
    candidate = cand * cands + place % cands
    bias = jnp.sum(jnp.where(lane == candidate, bias_ref[0:1, :], 0.0), axis=1, keepdims=True)
    level = top + jnp.log(total) + bias
    for r in range(side):
        for j in range(lo):
            start = (r * lo + j) * rows
            state = packed(mean[start : start + rows], level[start : start + rows])
            for f in range(far):
                out_ref[r, f, j] = state


def merge_kernel(state_ref, own_ref, out_ref):
    mean, level = merged(*unpacked(state_ref[...]))
    halves, pairs = lax.axis_size("far"), lax.axis_size(PAIR)
    rows = pairs * ANS_LEN
    tokens = mean.shape[0]

    def own(s, part, scale):
        lo = lax.axis_size("lo")
        heads = lax.axis_size("side")
        place = lax.axis_index("lo") * heads + s
        total = own_ref[place, part]
        for half in range(1, halves):
            total = total + own_ref[place + half * lo * heads, part]
        return (total * (1 / scale)).astype(jnp.bfloat16)

    query = own(lax.axis_index("side"), slice(0, tokens), SMALL_SCALE)
    key = own(0, slice(tokens, None), KEY_SCALE)
    value = own(1, slice(tokens, None), SMALL_SCALE)
    scores = dot_transposed(query, key) * HD ** (-0.5)
    row = lax.broadcasted_iota(jnp.int32, scores.shape, 0)
    column = lax.broadcasted_iota(jnp.int32, scores.shape, 1)
    shown = (row // rows == column // ANS_LEN) & (column % ANS_LEN <= row % ANS_LEN)
    scores = jnp.where(shown, scores, NEGATIVE)
    top = jnp.max(scores, axis=1, keepdims=True)
    weights = jnp.where(shown, jnp.exp(scores - top), 0.0)
    total = jnp.sum(weights, axis=1, keepdims=True)
    own_mean = dot(weights.astype(jnp.bfloat16), value) / total
    own_level = top + jnp.log(total)
    row = lax.broadcasted_iota(jnp.int32, level.shape, 0)
    mine = row // ANS_LEN % pairs == lax.axis_index(PAIR)
    own_level = jnp.where(mine, own_level, NEGATIVE)
    mean, level = merged(jnp.stack([mean, own_mean]), jnp.stack([level, own_level]))
    out_ref[...] = jnp.broadcast_to(packed(mean, level)[None], out_ref.shape)


def output_kernel(state_ref, weight_ref, out_ref):
    blocks, _, width = out_ref.shape
    columns = [merged(*unpacked(state_ref[s]))[0] for s in range(state_ref.shape[0])]
    attention = jnp.concatenate(columns, axis=1).astype(jnp.bfloat16)
    out = dot(attention, weight_ref[...])
    for block in range(blocks):
        place = reverse(block, blocks)
        out_ref[block] = out[:, place * width : (place + 1) * width].astype(jnp.bfloat16)


def sum_kernel(part_ref, out_ref):
    out_ref[...] = jnp.sum(part_ref[...].astype(jnp.float32), axis=0).astype(out_ref.dtype)


def body(
    hidden, query_weight, key_weight, value_weight, out_weight, key_cache, value_cache, cand_group
):
    tok_dev, feat_dev = hidden.shape
    heads_dev = query_weight.shape[1] // HD
    head, lo = lax.axis_size(HEAD), lax.axis_size("lo")
    far, pairs, side = (lax.axis_size(name) for name in ("far", PAIR, "side"))
    shard_len = key_cache.shape[0]
    bf16, f32 = jnp.bfloat16, jnp.float32
    rows = tok_dev * heads_dev * lo
    columns = out_weight.shape[1] // head

    inputs = (hidden, query_weight, key_weight, value_weight, cand_group, key_cache, value_cache)
    inputs = [pltpu.with_memory_space_constraint(x, pltpu.HBM) for x in inputs]
    partial, bias, cache = pl.pallas_call(
        project_kernel,
        out_shape=(
            jax.ShapeDtypeStruct((pairs * side, tok_dev + far * ANS_LEN, HD), f32),
            jax.ShapeDtypeStruct((ANS_LEN, HD), f32),
            jax.ShapeDtypeStruct((2, *key_cache.shape), bf16),
        ),
        in_specs=[HBM] * 7,
        out_specs=(VMEM, VMEM, HBM),
        scratch_shapes=[
            pltpu.VMEM(hidden.shape, bf16),
            pltpu.VMEM((feat_dev, (heads_dev + 2) * HD), bf16),
            pltpu.SMEM(cand_group.shape, jnp.int32),
            pltpu.SemaphoreType.DMA((11,)),
        ],
        compiler_params=pltpu.CompilerParams(vmem_limit_bytes=40 * 1024 * 1024),
        cost_estimate=pl.CostEstimate(
            flops=2 * tok_dev * feat_dev * (heads_dev + 2) * HD,
            bytes_accessed=2 * feat_dev * (tok_dev + (heads_dev + 2) * HD),
            transcendentals=0,
        ),
    )(*inputs)
    partial = lax.all_to_all(partial.astype(jnp.float16), RING, 0, 0, tiled=True)
    near = far * side * lo
    queries, cache = pl.pallas_call(
        reduce_kernel,
        out_shape=(
            jax.ShapeDtypeStruct((near, *partial.shape[1:]), f32),
            jax.ShapeDtypeStruct(cache.shape, cache.dtype),
        ),
        in_specs=[VMEM, pl.BlockSpec(memory_space=pl.ANY)],
        out_specs=(VMEM, pl.BlockSpec(memory_space=pl.ANY)),
        input_output_aliases={1: 1},
        compiler_params=pltpu.CompilerParams(vmem_limit_bytes=40 * 1024 * 1024),
        cost_estimate=pl.CostEstimate(
            flops=partial.size, bytes_accessed=partial.size * 4, transcendentals=0
        ),
    )(partial.astype(f32), cache)
    other = lax.ppermute(cache, "core", [(0, 1), (1, 0)])
    queries = queries.astype(jnp.float16)
    queries = lax.all_to_all(queries, ("far", "lo", "side"), 0, 0, tiled=True).astype(f32)
    state = call(
        attend_kernel,
        jax.ShapeDtypeStruct((side, far, lo, tok_dev + ANS_LEN, HD), bf16),
        [VMEM] * 4,
        flops=8 * rows * shard_len * HD,
        bytes_accessed=8 * shard_len * HD,
        transcendentals=2 * rows * shard_len,
    )(queries, cache, other, bias)
    state = state.reshape(near, tok_dev + ANS_LEN, HD)
    state = lax.all_to_all(state, ("side", "far", "lo"), 0, 0, tiled=True)
    state = call(
        merge_kernel,
        jax.ShapeDtypeStruct((side * pairs, tok_dev + ANS_LEN, HD), bf16),
        [VMEM] * 2,
        flops=4 * state.size,
        bytes_accessed=2 * state.size,
        transcendentals=0,
    )(state, queries)
    state = lax.all_to_all(state, RING, 0, 0, tiled=True)
    projected = call(
        output_kernel,
        jax.ShapeDtypeStruct((head, tok_dev, columns), bf16),
        [VMEM] * 2,
        flops=2 * tok_dev * out_weight.size,
        bytes_accessed=2 * out_weight.size,
        transcendentals=0,
    )(state.reshape(side, pairs, tok_dev + ANS_LEN, HD), out_weight)
    projected = lax.all_to_all(projected, HEAD[::-1], 0, 0, tiled=True)
    return call(
        sum_kernel,
        jax.ShapeDtypeStruct((tok_dev, columns), bf16),
        [VMEM],
        flops=projected.size,
        bytes_accessed=2 * projected.size,
        transcendentals=0,
    )(projected)


def solution(mesh):
    seq, head, cand = (mesh.shape[name] for name in ("seq", "head", "cand"))
    parts = jax.sharding.Mesh(
        mesh.devices.reshape(2, seq // 8, 2, 2, head // 4, 2, 2, cand // 2, 2),
        (*SEQ, *HEAD, *CAND),
    )
    in_specs = (
        P(CAND, SEQ),
        P(SEQ, HEAD),
        P(SEQ, None),
        P(SEQ, None),
        P(HEAD, SEQ),
        P((*SEQ, *CAND), None),
        P((*SEQ, *CAND), None),
        P(),
    )
    out_specs = P(CAND, (*SEQ, *HEAD))
    return jax.shard_map(body, mesh=parts, in_specs=in_specs, out_specs=out_specs, check_vma=False)
```
